768 devices in a mesh: depth: 12 (over z_hi, x), freq: 64 (over y, z_lo, core).
Axes of the slice: x: 4, y: 8, z: 12 (z_hi: 3, z_lo: 4; z = z_hi * 4 + z_lo), core: 2. Of those that a mesh axis runs over, the one named last changes fastest.
Arguments:
- surface: bfloat16 [256, 2, 64, 256], P('freq'), may hold values from -6 to 6
- regions: int32 [12, 64, 256], P('depth'), may hold values from 0 to 3
- table: bfloat16 [256, 4, 2, 2, 25], P('freq'), may hold values from -1 to 1
- source: bfloat16 [12, 256, 2, 64, 256], P('depth', 'freq'), may hold values from -6 to 6
Outputs:
- image: float32 [12, 32, 64, 256], P('depth', None, 'freq')
The draws below stay inside these ranges and needn't reach their ends.
All inputs are finite; a program needn't handle non-finite values.
Results may differ from the reference program's by a relative error of at most 0.011.
Values may be sent and summed in bfloat16 or wider, within the bound.
No kernel may reach another device: no remote copies, remote signals or barrier semaphores. Data moves between devices by JAX's collectives and lax.ppermute only.
A program may use at most 32 MiB of HBM per device.

```python
import math
import jax
import jax.numpy as jnp
from jax import lax

NX = 64
NY = 256
R = 4
TAPS = 25
H = 32
F = 256
NZ = 12


def draw_table(key, part):
    key_centre = jax.random.fold_in(key, 11)
    key_angle = jax.random.fold_in(key, 23)
    key_size = jax.random.fold_in(key, 37)
    centre_angle = jax.random.uniform(key_centre, (F, R, 2, 1), jnp.float32, -math.pi, math.pi)
    side_angle = jax.random.uniform(key_angle, (F, R, 2, TAPS), jnp.float32, -math.pi, math.pi)
    side_size = 0.3 / (TAPS - 1) * jax.random.uniform(key_size, (F, R, 2, TAPS), jnp.float32, 0.5, 1.5)
    centre_mask = (jnp.arange(TAPS) == TAPS // 2)[None, None, None, :]
    magnitude = jnp.where(centre_mask, 1.0, side_size)
    phase = jnp.where(centre_mask, centre_angle, side_angle)
    real_part = magnitude * jnp.cos(phase)
    imag_part = magnitude * jnp.sin(phase)
    return jnp.stack([real_part, imag_part], axis=3).astype(jnp.bfloat16)


def with_ends(values, stream_key, least, high):
    spot = [jax.random.randint(jax.random.fold_in(stream_key, axis), (), 0, length) for axis, length in enumerate(values.shape)]
    widest = values.shape.index(max(values.shape))
    next_to = spot[:widest] + [(spot[widest] + 1) % values.shape[widest]] + spot[widest + 1:]
    return values.at[tuple(spot)].set(least).at[tuple(next_to)].set(high)


def shard_levels(key, dims, cuts, low, top_value):
    def one(axis_at, shards_of):
        heights = jax.random.uniform(jax.random.fold_in(jax.random.fold_in(key, 6), axis_at), (shards_of,), jnp.float32, low / len(cuts), top_value / len(cuts))
        return jnp.repeat(jnp.exp(heights), dims[axis_at] // shards_of).reshape((-1,) + (1,) * (len(dims) - axis_at - 1))

    level = one(*cuts[0])
    for cut in cuts[1:]:
        level = level * one(*cut)
    return level


def gaussian(stream_key, shape, scale, limit, cuts=(), kind=jnp.bfloat16):
    values = scale * jax.random.normal(stream_key, shape, jnp.float32)
    if cuts:
        values = values * shard_levels(stream_key, shape, cuts, -0.22, 0.18)
    return jnp.clip(values, -limit, limit).astype(kind)


def setup_inputs(seed: int = 0) -> dict:
    arg_keys = jax.random.split(jax.random.key(seed), 5)
    return {
        "surface": gaussian(arg_keys[0], (F, 2, NX, NY), 1.0, 6.0, ((0, 64),)),
        "regions": with_ends(jax.random.randint(arg_keys[1], (NZ, NX, NY), 0, R), jax.random.fold_in(arg_keys[1], 1), 0, R - 1).astype(jnp.int32),
        "table": draw_table(jax.random.fold_in(arg_keys[4], 71), 0),
        "source": gaussian(arg_keys[3], (NZ, F, 2, NX, NY), 1.0, 6.0, ((0, 12), (1, 64))),
    }


def band_matrices(taps, extent):
    count = taps.shape[-1]
    positions = jnp.arange(extent)
    offset_table = positions[None, :] - positions[:, None] + count // 2
    onehot = (offset_table[:, :, None] == jnp.arange(count)[None, None, :]).astype(jnp.float32)
    return jnp.einsum('...t,ijt->...ij', taps.astype(jnp.float32), onehot).astype(jnp.bfloat16)

def complex_pass(wavefield, bands, region_masks, along_first):
    accumulated = jnp.zeros(wavefield.shape, jnp.float32)
    wave_real = wavefield[:, 0].astype(jnp.float32)
    wave_imag = wavefield[:, 1].astype(jnp.float32)
    for region in range(bands.shape[1]):
        band_real = bands[:, region, 0].astype(jnp.float32)
        band_imag = bands[:, region, 1].astype(jnp.float32)

        def product(band, signal):
            if along_first:
                return jnp.einsum('bxk,bky->bxy', band, signal)
            return jnp.einsum('bxk,byk->bxy', signal, band)
        real_part = product(band_real, wave_real) - product(band_imag, wave_imag)
        imag_part = product(band_real, wave_imag) + product(band_imag, wave_real)
        accumulated = accumulated + region_masks[region] * jnp.stack([real_part, imag_part], axis=1)
    return accumulated.astype(jnp.bfloat16)

def offset_image(wavefield, source_field):
    reach = H // 2
    lateral = wavefield.shape[2]
    padded_wave = jnp.pad(wavefield, ((0, 0), (0, 0), (reach, reach), (0, 0)))
    padded_source = jnp.pad(source_field, ((0, 0), (0, 0), (reach, reach), (0, 0)))
    images = []
    for shift_value in range(-reach, reach):
        first = padded_wave[:, :, reach + shift_value:reach + shift_value + lateral].astype(jnp.float32)
        second = padded_source[:, :, reach - shift_value:reach - shift_value + lateral].astype(jnp.float32)
        images.append(lax.optimization_barrier(jnp.sum(first * second, axis=(0, 1))))
    return jnp.stack(images)

def reference(surface, regions, table, source):
    band_first = band_matrices(table[:, :, 0], NX)
    band_second = band_matrices(table[:, :, 1], NY)
    wavefield = surface
    images = []
    for depth_step in range(NZ):
        region_masks = (regions[depth_step][None] == jnp.arange(R)[:, None, None]).astype(jnp.float32)
        between = complex_pass(wavefield, band_first, region_masks, True)
        wavefield = complex_pass(between, band_second, region_masks, False)
        images.append(offset_image(wavefield, source[depth_step]) / jnp.sqrt(jnp.float32(F)))
    return jnp.stack(images)
```

```python
import math

import jax
import jax.numpy as jnp
import numpy as np
from jax import lax
from jax.experimental import pallas as pl
from jax.experimental.pallas import tpu as pltpu
from jax.sharding import Mesh
from jax.sharding import PartitionSpec as P

H = 32
REACH = H // 2
NX = 64
NY = 256
HALF = 128
R = 4
TAPS = 25
MID = TAPS // 2
GROUP = 4

DEPTH = ("zh", "x")
FREQ = ("y", "zl", "core")


def tap_rows(table):
    first, second = table[:, 0], table[:, 1]

    def gap(n):
        return jnp.zeros((R, 1, n), jnp.float32)

    rows = []
    for a, b in ((first[:, 0:1], -first[:, 1:2]), (first[:, 1:2], first[:, 0:1])):
        rows.append(
            jnp.concatenate([a[..., MID:], gap(39), b, gap(39), a[..., :MID]], axis=-1)
        )
    rows_first = jnp.concatenate(rows, axis=1).reshape(R * 2, HALF)
    back = second[..., ::-1]
    rows_second = jnp.concatenate(
        [back[..., MID:], jnp.zeros((R, 2, NY - TAPS), jnp.float32), back[..., :MID]], axis=-1
    ).reshape(R * 2, NY)
    return rows_first, rows_second


def pick(masks, values):
    out = values[R - 1]
    for region in range(R - 2, -1, -1):
        out = jnp.where(masks[region], values[region], out)
    return out


def chain_kernel(count_ref, rows_first_ref, rows_second_ref, surface_ref, regions_ref, out_ref, band_first, band_second, state):
    def fan(row, height):
        wide = jnp.broadcast_to(row, (height, row.shape[-1]))
        return pltpu.roll(wide, 0, 1, stride=1, stride_axis=0)

    row_at = lax.broadcasted_iota(jnp.int32, (NX, HALF), 0)
    lane_at = lax.broadcasted_iota(jnp.int32, (NX, HALF), 1)
    near = jnp.abs((lane_at & (NX - 1)) - row_at) <= MID
    for block in range(R * 2):
        band = fan(rows_first_ref[block : block + 1, :], NX)
        band_first[block * NX : (block + 1) * NX, :] = jnp.where(near, band, 0.0).astype(jnp.bfloat16)

    row_at = lax.broadcasted_iota(jnp.int32, (NY, NY), 0)
    lane_at = lax.broadcasted_iota(jnp.int32, (NY, NY), 1)
    near = jnp.abs(lane_at - row_at) <= MID
    for region in range(R):
        for part in range(2):
            block = region * 2 + part
            band = fan(rows_second_ref[block : block + 1, :], NY)
            band = jnp.where(near, band, 0.0)
            plain = band.astype(jnp.bfloat16)
            for half in range(2):
                cut = plain[:, half * HALF : (half + 1) * HALF]

                def lanes(part_out):
                    start = ((part_out * 2 + half) * R + region) * HALF
                    return slice(start, start + HALF)

                if part == 0:
                    band_second[:NY, lanes(0)] = cut
                    band_second[NY:, lanes(1)] = cut
                else:
                    band_second[NY:, lanes(0)] = -cut
                    band_second[:NY, lanes(1)] = cut

    state[:NX, :] = surface_ref[0]
    state[NX:, :] = surface_ref[1]
    count = count_ref[0]

    def step(t, carry):
        region = regions_ref[t].astype(jnp.float32)
        masks = [region == float(r) for r in range(R - 1)]
        field = jnp.dot(band_first[...], state[...], preferred_element_type=jnp.float32)
        between = []
        for part in range(2):
            values = [field[(r * 2 + part) * NX : (r * 2 + part + 1) * NX] for r in range(R)]
            between.append(pick(masks, values).astype(jnp.bfloat16))
        between = jnp.concatenate(between, axis=1)
        slot = jnp.maximum(t - (count - GROUP), 0)
        for half in range(2):
            cut = [m[:, half * HALF : (half + 1) * HALF] for m in masks]
            for part in range(2):
                start = (part * 2 + half) * R * HALF
                wide = jnp.dot(
                    between,
                    band_second[:, start : start + R * HALF],
                    preferred_element_type=jnp.float32,
                )
                values = [wide[:, r * HALF : (r + 1) * HALF] for r in range(R)]
                leaving = pick(cut, values).astype(jnp.bfloat16)
                state[part * NX : (part + 1) * NX, half * HALF : (half + 1) * HALF] = leaving
                out_ref[slot * 2 + half, part] = leaving
        return carry

    lax.fori_loop(0, count, step, 0)


def image_kernel(scale, wave_ref, mine_ref, other_ref, core_ref, out_ref, wave, src):
    edge = jnp.zeros((4, 2, REACH, HALF), jnp.float32)
    mine = core_ref[0]
    for core in range(2):
        for ref in (wave, src):
            ref[core, :, :, :REACH, :] = edge
            ref[core, :, :, REACH + NX :, :] = edge
        for f in range(GROUP):
            wave[core, f, :, REACH : REACH + NX, :] = wave_ref[f * 2 + core].astype(jnp.float32)
    src[mine, :, :, REACH : REACH + NX, :] = mine_ref[...].astype(jnp.float32)
    src[1 - mine, :, :, REACH : REACH + NX, :] = other_ref[...].astype(jnp.float32)

    def row(x, carry):
        total = jnp.zeros((H, HALF), jnp.float32)
        for core in range(2):
            for f in range(GROUP):
                for part in range(2):
                    total = total + wave[core, f, part, pl.ds(x, H), :] * src[core, f, part, pl.ds(NX - 1 - x, H), :]
        out_ref[x] = (total * scale).astype(jnp.bfloat16)
        return carry

    lax.fori_loop(0, NX, row, 0)


def sum_kernel(part_ref, out_ref):
    groups = part_ref.shape[0] // 2
    for core in range(2):
        def add(i, total):
            return total + part_ref[2 * i + core].astype(jnp.float32)

        total = lax.fori_loop(0, groups, add, jnp.zeros((H, HALF), jnp.float32), unroll=True)
        out_ref[:, core * HALF : (core + 1) * HALF] = total


VMEM = pl.BlockSpec(memory_space=pltpu.VMEM)
SMEM = pl.BlockSpec(memory_space=pltpu.SMEM)


def body(surface, regions, table, source):
    zh = lax.axis_index("zh")
    mine_x = lax.axis_index("x")
    core = lax.axis_index("core")
    depths = lax.axis_size("zh") * lax.axis_size("x")

    local = regions[0].astype(jnp.bfloat16)
    all_regions = lax.all_to_all(
        jnp.broadcast_to(local[None], (depths, NX, NY)), DEPTH, 0, 0, tiled=True
    )

    flipped = source[0][:, :, ::-1, :]
    low, high = flipped[..., :HALF], flipped[..., HALF:]
    kept = jnp.where(core == 0, low, high)
    given = jnp.where(core == 0, high, low)
    other = lax.ppermute(given, "core", [(0, 1), (1, 0)])

    rows_first, rows_second = tap_rows(
        lax.dynamic_index_in_dim(table, mine_x, 0, keepdims=False).astype(jnp.float32)
    )
    entering = lax.dynamic_index_in_dim(surface, mine_x, 0, keepdims=False)
    count = ((zh + 1) * GROUP).astype(jnp.int32).reshape(1)

    waves = pl.pallas_call(
        chain_kernel,
        out_shape=jax.ShapeDtypeStruct((GROUP * 2, 2, NX, HALF), jnp.bfloat16),
        in_specs=[SMEM, VMEM, VMEM, VMEM, VMEM],
        out_specs=VMEM,
        scratch_shapes=[
            pltpu.VMEM((R * 2 * NX, 2 * NX), jnp.bfloat16),
            pltpu.VMEM((2 * NY, R * 2 * NY), jnp.bfloat16),
            pltpu.VMEM((2 * NX, NY), jnp.bfloat16),
        ],
        compiler_params=pltpu.CompilerParams(vmem_limit_bytes=24 << 20),
        cost_estimate=pl.CostEstimate(flops=4_000_000_000, bytes_accessed=4_000_000, transcendentals=0),
        name="chain",
    )(count, rows_first, rows_second, entering, all_regions)

    waves = lax.all_to_all(waves, ("x", "core"), 0, 0, tiled=True)

    scale = 1.0 / math.sqrt(surface.shape[0] * lax.axis_size(FREQ))
    partial_image = pl.pallas_call(
        lambda *refs: image_kernel(scale, *refs),
        out_shape=jax.ShapeDtypeStruct((NX, H, HALF), jnp.bfloat16),
        in_specs=[VMEM, VMEM, VMEM, SMEM],
        out_specs=VMEM,
        scratch_shapes=[
            pltpu.VMEM((2, GROUP, 2, NX + H, HALF), jnp.float32),
            pltpu.VMEM((2, GROUP, 2, NX + H, HALF), jnp.float32),
        ],
        compiler_params=pltpu.CompilerParams(vmem_limit_bytes=24 << 20),
        cost_estimate=pl.CostEstimate(flops=10_000_000, bytes_accessed=2_000_000, transcendentals=0),
        name="image",
    )(waves, kept, other, core.astype(jnp.int32).reshape(1))

    parts = lax.all_to_all(partial_image, FREQ, 0, 0, tiled=True)

    mine = pl.pallas_call(
        sum_kernel,
        out_shape=jax.ShapeDtypeStruct((H, NY), jnp.float32),
        in_specs=[VMEM],
        out_specs=VMEM,
        compiler_params=pltpu.CompilerParams(vmem_limit_bytes=24 << 20),
        name="total",
    )(parts)
    return mine[None, :, None, :]


def solution(mesh):
    wide = Mesh(np.asarray(mesh.devices).reshape(3, 4, 8, 4, 2), ("zh", "x", "y", "zl", "core"))
    in_specs = (
        P(FREQ, None, None, None),
        P(DEPTH, None, None),
        P(FREQ, None, None, None, None),
        P(DEPTH, FREQ, None, None, None),
    )
    out_specs = P(DEPTH, None, FREQ, None)
    return jax.shard_map(body, mesh=wide, in_specs=in_specs, out_specs=out_specs, check_vma=False)
```

```python
import math

import jax
import jax.numpy as jnp
import numpy as np
from jax import lax
from jax.experimental import pallas as pl
from jax.experimental.pallas import tpu as pltpu
from jax.sharding import Mesh
from jax.sharding import PartitionSpec as P

H = 32
REACH = H // 2
NX = 64
NY = 256
LANES = 128
QUARTER = 64
R = 4
TAPS = 25
MID = TAPS // 2
GROUP = 4

AXES = ("zh", "x", "y", "zq", "zp", "core")
DEPTH = ("zh", "x")
FREQ = ("y", "zq", "zp", "core")
QUAD = ("zp", "core")


def tap_rows(table):
    first, second = table[:, 0], table[:, 1]

    def gap(n):
        return jnp.zeros((R, 1, n), jnp.float32)

    rows = []
    for a, b in ((first[:, 0:1], -first[:, 1:2]), (first[:, 1:2], first[:, 0:1])):
        rows.append(
            jnp.concatenate([a[..., MID:], gap(39), b, gap(39), a[..., :MID]], axis=-1)
        )
    rows_first = jnp.concatenate(rows, axis=1).reshape(R * 2, LANES)
    back = second[..., ::-1]
    rows_second = jnp.concatenate(
        [back[..., MID:], jnp.zeros((R, 2, LANES - TAPS), jnp.float32), back[..., :MID]], axis=-1
    ).reshape(R * 2, LANES)
    return rows_first, rows_second


def fan(row, height, shift):
    wide = jnp.broadcast_to(row, (height, row.shape[-1]))
    return pltpu.roll(wide, shift, 1, stride=1, stride_axis=0)


def bands_kernel(rows_first_ref, rows_second_ref, band_first, band_even, band_odd):
    row_at = lax.broadcasted_iota(jnp.int32, (NX, LANES), 0)
    lane_at = lax.broadcasted_iota(jnp.int32, (NX, LANES), 1)
    near = jnp.abs((lane_at & (NX - 1)) - row_at) <= MID
    for block in range(R * 2):
        band = fan(rows_first_ref[block : block + 1, :], NX, 0)
        band_first[block * NX : (block + 1) * NX, :] = jnp.where(near, band, 0.0).astype(jnp.bfloat16)

    left = lax.broadcasted_iota(jnp.int32, (LANES, LANES), 1) < QUARTER
    for region in range(R):
        tap_real = rows_second_ref[2 * region : 2 * region + 1, :]
        tap_imag = rows_second_ref[2 * region + 1 : 2 * region + 2, :]
        cols = slice(region * LANES, (region + 1) * LANES)
        for part, (to_real, to_imag) in enumerate(((tap_real, tap_imag), (-tap_imag, tap_real))):
            rows = slice(part * LANES, (part + 1) * LANES)
            real_band = fan(to_real, LANES, 0)
            imag_band = fan(to_imag, LANES, QUARTER)
            band_even[rows, cols] = jnp.where(left, real_band, imag_band).astype(jnp.bfloat16)
            band_odd[rows, cols] = jnp.where(left, imag_band, real_band).astype(jnp.bfloat16)


def pick(masks, values):
    out = values[R - 1]
    for region in range(R - 2, -1, -1):
        out = jnp.where(masks[region], values[region], out)
    return out


def chain_kernel(scalar_ref, band_first, band_even, band_odd, surface_ref, own_ref, swapped_ref, out_ref, state):
    state[:NX, :] = surface_ref[0]
    state[NX:, :] = surface_ref[1]
    core = scalar_ref[1]
    lane = lax.broadcasted_iota(jnp.int32, (NX, LANES), 1)
    left = lane < QUARTER
    low = lane < 96
    high = lane >= 32

    def split(values):
        return [values == float(r) for r in range(R - 1)]

    def step(t, slot):
        own = own_ref[t].astype(jnp.float32)
        swapped = swapped_ref[t].astype(jnp.float32)
        halves = [jnp.where(core == half, own, swapped) for half in range(2)]
        turned = [pltpu.roll(half, QUARTER, 1) for half in halves]
        full = split(jnp.concatenate(halves, axis=1))
        even_mask = split(jnp.concatenate([jnp.where(left, a, b) for a, b in zip(halves, turned)], axis=0))
        odd_mask = split(jnp.concatenate([jnp.where(left, b, a) for a, b in zip(halves, turned)], axis=0))

        field = jnp.dot(band_first[...], state[...], preferred_element_type=jnp.float32)
        even_in, odd_in = [], []
        for part in range(2):
            values = [field[(r * 2 + part) * NX : (r * 2 + part + 1) * NX] for r in range(R)]
            between = pick(full, values)
            a, b = between[:, :LANES], between[:, LANES:]
            even_in.append(jnp.concatenate([jnp.where(low, a, 0.0), jnp.where(low, b, a)], axis=0).astype(jnp.bfloat16))
            odd_in.append(jnp.concatenate([jnp.where(high, a, b), jnp.where(high, b, 0.0)], axis=0).astype(jnp.bfloat16))
        wide = jnp.dot(jnp.concatenate(even_in, axis=1), band_even[...], preferred_element_type=jnp.float32)
        even = pick(even_mask, [wide[:, r * LANES : (r + 1) * LANES] for r in range(R)])
        wide = jnp.dot(jnp.concatenate(odd_in, axis=1), band_odd[...], preferred_element_type=jnp.float32)
        odd = pick(odd_mask, [wide[:, r * LANES : (r + 1) * LANES] for r in range(R)])
        for half in range(2):
            rows = slice(half * NX, (half + 1) * NX)
            cols = slice(half * LANES, (half + 1) * LANES)
            e, o = even[rows], odd[rows]
            out_ref[slot * 4 + half * 2] = e.astype(jnp.bfloat16)
            out_ref[slot * 4 + half * 2 + 1] = o.astype(jnp.bfloat16)
            state[:NX, cols] = jnp.where(left, e, o).astype(jnp.bfloat16)
            state[NX:, cols] = pltpu.roll(jnp.where(left, o, e), QUARTER, 1).astype(jnp.bfloat16)

    def block(b, carry):
        for slot in range(GROUP):
            step(b * GROUP + slot, slot)
        return carry

    lax.fori_loop(0, scalar_ref[0], block, 0)


def pack_kernel(source_ref, out_ref):
    row_at = lax.broadcasted_iota(jnp.int32, (NX, NX), 0)
    col_at = lax.broadcasted_iota(jnp.int32, (NX, NX), 1)
    flip = (row_at + col_at == NX - 1).astype(jnp.bfloat16)
    left = lax.broadcasted_iota(jnp.int32, (NX, LANES), 1) < QUARTER
    for f in range(GROUP):
        real = jnp.dot(flip, source_ref[f, 0], preferred_element_type=jnp.float32)
        imag = jnp.dot(flip, source_ref[f, 1], preferred_element_type=jnp.float32)
        for half in range(2):
            cols = slice(half * LANES, (half + 1) * LANES)
            a = real[:, cols]
            b = pltpu.roll(imag[:, cols], QUARTER, 1)
            out_ref[half * 2, f] = jnp.where(left, a, b).astype(jnp.bfloat16)
            out_ref[half * 2 + 1, f] = jnp.where(left, b, a).astype(jnp.bfloat16)


def image_kernel(scale, wave_ref, source_ref, out_ref, wave, src):
    edge = jnp.zeros((4 * GROUP, REACH, LANES), jnp.float32)
    for ref in (wave, src):
        ref[:, :REACH, :] = edge
        ref[:, REACH + NX :, :] = edge
    for f in range(GROUP):
        for g in range(4):
            wave[f * 4 + g, REACH : REACH + NX, :] = wave_ref[f * 4 + g].astype(jnp.float32)
            src[f * 4 + g, REACH : REACH + NX, :] = source_ref[g, f].astype(jnp.float32)
    left = lax.broadcasted_iota(jnp.int32, (REACH, LANES), 1) < QUARTER

    def row(x, carry):
        total = jnp.zeros((H, LANES), jnp.float32)
        for i in range(4 * GROUP):
            total = total + wave[i, pl.ds(x, H), :] * src[i, pl.ds(NX - 1 - x, H), :]
        total = (total + pltpu.roll(total, QUARTER, 1)) * scale
        out_ref[x] = jnp.where(left, total[:REACH], total[REACH:]).astype(jnp.bfloat16)
        return carry

    lax.fori_loop(0, NX, row, 0, unroll=2)


def sum_kernel(part_ref, out_ref):
    groups = part_ref.shape[0] // 4
    left = lax.broadcasted_iota(jnp.int32, (REACH, LANES), 1) < QUARTER
    for half in range(2):
        totals = []
        for q in (2 * half, 2 * half + 1):
            total = part_ref[q].astype(jnp.float32)
            for i in range(1, groups):
                total = total + part_ref[4 * i + q].astype(jnp.float32)
            totals.append(total)
        a, b = totals
        cols = slice(half * LANES, (half + 1) * LANES)
        out_ref[:REACH, cols] = jnp.where(left, a, pltpu.roll(b, QUARTER, 1))
        out_ref[REACH:, cols] = jnp.where(left, pltpu.roll(a, QUARTER, 1), b)


VMEM = pl.BlockSpec(memory_space=pltpu.VMEM)
SMEM = pl.BlockSpec(memory_space=pltpu.SMEM)
PARAMS = pltpu.CompilerParams(vmem_limit_bytes=24 << 20)


def cost(flops, moved):
    return pl.CostEstimate(flops=flops, bytes_accessed=moved, transcendentals=0)


def body(surface, regions, table, source):
    zh = lax.axis_index("zh")
    mine_x = lax.axis_index("x")
    core = lax.axis_index("core")
    depths = lax.axis_size("zh") * lax.axis_size("x")
    swap = [(0, 1), (1, 0)]

    local = jnp.where(core == 0, regions[0, :, :LANES], regions[0, :, LANES:]).astype(jnp.bfloat16)
    own = lax.all_to_all(
        jnp.broadcast_to(local[None], (depths, NX, LANES)), DEPTH, 0, 0, tiled=True
    )
    swapped = lax.ppermute(own, "core", swap)

    packed = pl.pallas_call(
        pack_kernel,
        out_shape=jax.ShapeDtypeStruct((4, GROUP, NX, LANES), jnp.bfloat16),
        in_specs=[VMEM],
        out_specs=VMEM,
        compiler_params=PARAMS,
        cost_estimate=cost(20_000_000, 1_000_000),
        name="pack",
    )(source[0])
    sources = lax.all_to_all(packed, QUAD, 0, 0, tiled=True)

    rows_first, rows_second = tap_rows(
        lax.dynamic_index_in_dim(table, mine_x, 0, keepdims=False).astype(jnp.float32)
    )
    bands = pl.pallas_call(
        bands_kernel,
        out_shape=(
            jax.ShapeDtypeStruct((R * 2 * NX, LANES), jnp.bfloat16),
            jax.ShapeDtypeStruct((2 * LANES, R * LANES), jnp.bfloat16),
            jax.ShapeDtypeStruct((2 * LANES, R * LANES), jnp.bfloat16),
        ),
        in_specs=[VMEM] * 2,
        out_specs=(VMEM,) * 3,
        compiler_params=PARAMS,
        cost_estimate=cost(10_000_000, 1_000_000),
        name="bands",
    )(rows_first, rows_second)

    entering = lax.dynamic_index_in_dim(surface, mine_x, 0, keepdims=False)
    scalars = jnp.stack([zh + 1, core]).astype(jnp.int32)
    waves = pl.pallas_call(
        chain_kernel,
        out_shape=jax.ShapeDtypeStruct((GROUP * 4, NX, LANES), jnp.bfloat16),
        in_specs=[SMEM] + [VMEM] * 6,
        out_specs=VMEM,
        scratch_shapes=[pltpu.VMEM((2 * NX, NY), jnp.bfloat16)],
        compiler_params=PARAMS,
        cost_estimate=cost(4_000_000_000, 4_000_000),
        name="chain",
    )(scalars, *bands, entering, own, swapped)

    waves = lax.all_to_all(waves, ("x",) + QUAD, 0, 0, tiled=True)

    scale = 1.0 / math.sqrt(surface.shape[0] * lax.axis_size(FREQ))
    partial_image = pl.pallas_call(
        lambda *refs: image_kernel(scale, *refs),
        out_shape=jax.ShapeDtypeStruct((NX, REACH, LANES), jnp.bfloat16),
        in_specs=[VMEM, VMEM],
        out_specs=VMEM,
        scratch_shapes=[pltpu.VMEM((4 * GROUP, NX + H, LANES), jnp.float32)] * 2,
        compiler_params=PARAMS,
        cost_estimate=cost(10_000_000, 2_000_000),
        name="image",
    )(waves, sources)

    parts = lax.all_to_all(partial_image, FREQ, 0, 0, tiled=True)

    mine = pl.pallas_call(
        sum_kernel,
        out_shape=jax.ShapeDtypeStruct((H, NY), jnp.float32),
        in_specs=[VMEM],
        out_specs=VMEM,
        compiler_params=PARAMS,
        name="total",
    )(parts)
    return mine[None, :, None, :]


def solution(mesh):
    wide = Mesh(np.asarray(mesh.devices).reshape(3, 4, 8, 2, 2, 2), AXES)
    in_specs = (
        P(FREQ, None, None, None),
        P(DEPTH, None, None),
        P(FREQ, None, None, None, None),
        P(DEPTH, FREQ, None, None, None),
    )
    out_specs = P(DEPTH, None, FREQ, None)
    return jax.shard_map(body, mesh=wide, in_specs=in_specs, out_specs=out_specs, check_vma=False)
```

```python
import math

import jax
import jax.numpy as jnp
import numpy as np
from jax import lax
from jax.experimental import pallas as pl
from jax.experimental.pallas import tpu as pltpu
from jax.sharding import Mesh
from jax.sharding import PartitionSpec as P

H = 32
REACH = H // 2
NX = 64
NY = 256
LANES = 128
QUARTER = 64
R = 4
TAPS = 25
MID = TAPS // 2
GROUP = 4

AXES = ("zh", "x", "y", "zq", "zp", "core")
DEPTH = ("zh", "x")
FREQ = ("y", "zq", "zp", "core")
QUAD = ("zp", "core")


def tap_rows(table):
    first, second = table[:, 0], table[:, 1]

    def gap(n):
        return jnp.zeros((R, 1, n), jnp.float32)

    rows = []
    for a, b in ((first[:, 0:1], -first[:, 1:2]), (first[:, 1:2], first[:, 0:1])):
        rows.append(
            jnp.concatenate([a[..., MID:], gap(39), b, gap(39), a[..., :MID]], axis=-1)
        )
    rows_first = jnp.concatenate(rows, axis=1).reshape(R * 2, LANES)
    back = second[..., ::-1]
    rows_second = jnp.concatenate(
        [back[..., MID:], jnp.zeros((R, 2, LANES - TAPS), jnp.float32), back[..., :MID]], axis=-1
    ).reshape(R * 2, LANES)
    return rows_first, rows_second


def fan(row, height, shift):
    wide = jnp.broadcast_to(row, (height, row.shape[-1]))
    return pltpu.roll(wide, shift, 1, stride=1, stride_axis=0)


def bands_kernel(rows_first_ref, rows_second_ref, band_first, band_even, band_odd):
    row_at = lax.broadcasted_iota(jnp.int32, (NX, LANES), 0)
    lane_at = lax.broadcasted_iota(jnp.int32, (NX, LANES), 1)
    near = jnp.abs((lane_at & (NX - 1)) - row_at) <= MID
    for block in range(R * 2):
        band = fan(rows_first_ref[block : block + 1, :], NX, 0)
        band_first[block * NX : (block + 1) * NX, :] = jnp.where(near, band, 0.0).astype(jnp.bfloat16)

    left = lax.broadcasted_iota(jnp.int32, (LANES, LANES), 1) < QUARTER
    for region in range(R):
        tap_real = rows_second_ref[2 * region : 2 * region + 1, :]
        tap_imag = rows_second_ref[2 * region + 1 : 2 * region + 2, :]
        cols = slice(region * LANES, (region + 1) * LANES)
        for part, (to_real, to_imag) in enumerate(((tap_real, tap_imag), (-tap_imag, tap_real))):
            rows = slice(part * LANES, (part + 1) * LANES)
            real_band = fan(to_real, LANES, 0)
            imag_band = fan(to_imag, LANES, QUARTER)
            band_even[rows, cols] = jnp.where(left, real_band, imag_band).astype(jnp.bfloat16)
            band_odd[rows, cols] = jnp.where(left, imag_band, real_band).astype(jnp.bfloat16)


def pick(masks, values):
    out = values[R - 1]
    for region in range(R - 2, -1, -1):
        out = jnp.where(masks[region], values[region], out)
    return out


def chain_kernel(scalar_ref, band_first, band_even, band_odd, surface_ref, own_ref, swapped_ref, out_ref, state):
    state[:NX, :] = surface_ref[0]
    state[NX:, :] = surface_ref[1]
    core = scalar_ref[1]
    lane = lax.broadcasted_iota(jnp.int32, (NX, LANES), 1)
    left = lane < QUARTER
    low = lane < 96
    high = lane >= 32

    def split(values):
        return [values == float(r) for r in range(R - 1)]

    def step(t, slot):
        own = own_ref[t].astype(jnp.float32)
        swapped = swapped_ref[t].astype(jnp.float32)
        halves = [jnp.where(core == half, own, swapped) for half in range(2)]
        turned = [pltpu.roll(half, QUARTER, 1) for half in halves]
        full = split(jnp.concatenate(halves, axis=1))
        even_mask = split(jnp.concatenate([jnp.where(left, a, b) for a, b in zip(halves, turned)], axis=0))
        odd_mask = split(jnp.concatenate([jnp.where(left, b, a) for a, b in zip(halves, turned)], axis=0))

        field = [
            jnp.dot(band_first[rows], state[...], preferred_element_type=jnp.float32)
            for rows in (slice(0, 4 * NX), slice(4 * NX, 8 * NX))
        ]
        field = jnp.concatenate(field, axis=0)
        even_in, odd_in = [], []
        for part in range(2):
            values = [field[(r * 2 + part) * NX : (r * 2 + part + 1) * NX] for r in range(R)]
            between = pick(full, values)
            a, b = between[:, :LANES], between[:, LANES:]
            even_in.append(jnp.concatenate([jnp.where(low, a, 0.0), jnp.where(low, b, a)], axis=0).astype(jnp.bfloat16))
            odd_in.append(jnp.concatenate([jnp.where(high, a, b), jnp.where(high, b, 0.0)], axis=0).astype(jnp.bfloat16))
        wide = jnp.dot(jnp.concatenate(even_in, axis=1), band_even[...], preferred_element_type=jnp.float32)
        even = pick(even_mask, [wide[:, r * LANES : (r + 1) * LANES] for r in range(R)])
        wide = jnp.dot(jnp.concatenate(odd_in, axis=1), band_odd[...], preferred_element_type=jnp.float32)
        odd = pick(odd_mask, [wide[:, r * LANES : (r + 1) * LANES] for r in range(R)])
        for half in range(2):
            rows = slice(half * NX, (half + 1) * NX)
            cols = slice(half * LANES, (half + 1) * LANES)
            e, o = even[rows], odd[rows]
            out_ref[slot * 4 + half * 2] = e.astype(jnp.bfloat16)
            out_ref[slot * 4 + half * 2 + 1] = o.astype(jnp.bfloat16)
            state[:NX, cols] = jnp.where(left, e, o).astype(jnp.bfloat16)
            state[NX:, cols] = pltpu.roll(jnp.where(left, o, e), QUARTER, 1).astype(jnp.bfloat16)

    def block(b, carry):
        for slot in range(GROUP):
            step(b * GROUP + slot, slot)
        return carry

    lax.fori_loop(0, scalar_ref[0], block, 0)


def spread_kernel(core_ref, regions_ref, out_ref):
    low = regions_ref[:, :LANES].astype(jnp.float32)
    high = regions_ref[:, LANES:].astype(jnp.float32)
    half = jnp.where(core_ref[0] == 0, low, high).astype(jnp.bfloat16)
    for i in range(out_ref.shape[0]):
        out_ref[i] = half


def pack_kernel(quarter_ref, source_ref, *refs):
    outs, packed = refs[:4], refs[4]
    row_at = lax.broadcasted_iota(jnp.int32, (NX, NX), 0)
    col_at = lax.broadcasted_iota(jnp.int32, (NX, NX), 1)
    flip = (row_at + col_at == NX - 1).astype(jnp.bfloat16)
    left = lax.broadcasted_iota(jnp.int32, (NX, LANES), 1) < QUARTER
    for f in range(GROUP):
        real = jnp.dot(flip, source_ref[f, 0], preferred_element_type=jnp.float32)
        imag = jnp.dot(flip, source_ref[f, 1], preferred_element_type=jnp.float32)
        for half in range(2):
            cols = slice(half * LANES, (half + 1) * LANES)
            a = real[:, cols]
            b = pltpu.roll(imag[:, cols], QUARTER, 1)
            packed[half * 2, f] = jnp.where(left, a, b).astype(jnp.bfloat16)
            packed[half * 2 + 1, f] = jnp.where(left, b, a).astype(jnp.bfloat16)
    for k in range(4):
        outs[k][...] = packed[quarter_ref[0] ^ k]


def image_kernel(scale, quarter_ref, wave_ref, *refs):
    sources, out_ref, wave, src, totals = refs[:4], refs[4], refs[5], refs[6], refs[7]
    edge = jnp.zeros((4 * GROUP, REACH, LANES), jnp.float32)
    for ref in (wave, src):
        ref[:, :REACH, :] = edge
        ref[:, REACH + NX :, :] = edge
    for k in range(4):
        group = (quarter_ref[0] ^ k) * GROUP
        for f in range(GROUP):
            wave[k * GROUP + f, REACH : REACH + NX, :] = wave_ref[f * 4 + k].astype(jnp.float32)
            src[group + f, REACH : REACH + NX, :] = sources[k][f].astype(jnp.float32)

    def row(x, carry):
        total = jnp.zeros((H, LANES), jnp.float32)
        for i in range(4 * GROUP):
            total = total + wave[i, pl.ds(x, H), :] * src[i, pl.ds(NX - 1 - x, H), :]
        totals[x] = total
        return carry

    lax.fori_loop(0, NX, row, 0, unroll=4)
    left = lax.broadcasted_iota(jnp.int32, (REACH, LANES), 1) < QUARTER

    def fold(x, carry):
        total = totals[x]
        total = (total + pltpu.roll(total, QUARTER, 1)) * scale
        out_ref[x] = jnp.where(left, total[:REACH], total[REACH:]).astype(jnp.bfloat16)
        return carry

    lax.fori_loop(0, NX, fold, 0, unroll=8)


def sum_kernel(part_ref, out_ref):
    groups = part_ref.shape[0] // 4
    left = lax.broadcasted_iota(jnp.int32, (REACH, LANES), 1) < QUARTER
    for half in range(2):
        totals = []
        for q in (2 * half, 2 * half + 1):
            total = part_ref[q].astype(jnp.float32)
            for i in range(1, groups):
                total = total + part_ref[4 * i + q].astype(jnp.float32)
            totals.append(total)
        a, b = totals
        cols = slice(half * LANES, (half + 1) * LANES)
        out_ref[0, :REACH, 0, cols] = jnp.where(left, a, pltpu.roll(b, QUARTER, 1))
        out_ref[0, REACH:, 0, cols] = jnp.where(left, pltpu.roll(a, QUARTER, 1), b)


VMEM = pl.BlockSpec(memory_space=pltpu.VMEM)
SMEM = pl.BlockSpec(memory_space=pltpu.SMEM)
PARAMS = pltpu.CompilerParams(vmem_limit_bytes=24 << 20)


def cost(flops, moved):
    return pl.CostEstimate(flops=flops, bytes_accessed=moved, transcendentals=0)


def body(surface, regions, table, source):
    zh = lax.axis_index("zh")
    mine_x = lax.axis_index("x")
    core = lax.axis_index("core")
    depths = lax.axis_size("zh") * lax.axis_size("x")
    swap = [(0, 1), (1, 0)]

    copies = pl.pallas_call(
        spread_kernel,
        out_shape=jax.ShapeDtypeStruct((depths, NX, LANES), jnp.bfloat16),
        in_specs=[SMEM, VMEM],
        out_specs=VMEM,
        compiler_params=PARAMS,
        cost_estimate=cost(1_000_000, 300_000),
        name="spread",
    )(core.astype(jnp.int32).reshape(1), regions[0])
    own = lax.all_to_all(copies, DEPTH, 0, 0, tiled=True)
    swapped = lax.ppermute(own, "core", swap)

    quarter = (lax.axis_index("zp") * 2 + core).astype(jnp.int32).reshape(1)
    packed = pl.pallas_call(
        pack_kernel,
        out_shape=(jax.ShapeDtypeStruct((GROUP, NX, LANES), jnp.bfloat16),) * 4,
        in_specs=[SMEM, VMEM],
        out_specs=(VMEM,) * 4,
        scratch_shapes=[pltpu.VMEM((4, GROUP, NX, LANES), jnp.bfloat16)],
        compiler_params=PARAMS,
        cost_estimate=cost(20_000_000, 1_000_000),
        name="pack",
    )(quarter, source[0])
    sources = [packed[0]] + [
        lax.ppermute(packed[k], QUAD, [(i, i ^ k) for i in range(4)]) for k in (1, 2, 3)
    ]
    own, swapped, *sources = lax.optimization_barrier((own, swapped, *sources))

    rows_first, rows_second = tap_rows(
        lax.dynamic_index_in_dim(table, mine_x, 0, keepdims=False).astype(jnp.float32)
    )
    bands = pl.pallas_call(
        bands_kernel,
        out_shape=(
            jax.ShapeDtypeStruct((R * 2 * NX, LANES), jnp.bfloat16),
            jax.ShapeDtypeStruct((2 * LANES, R * LANES), jnp.bfloat16),
            jax.ShapeDtypeStruct((2 * LANES, R * LANES), jnp.bfloat16),
        ),
        in_specs=[VMEM] * 2,
        out_specs=(VMEM,) * 3,
        compiler_params=PARAMS,
        cost_estimate=cost(10_000_000, 1_000_000),
        name="bands",
    )(rows_first, rows_second)

    entering = lax.dynamic_index_in_dim(surface, mine_x, 0, keepdims=False)
    scalars = jnp.stack([zh + 1, core]).astype(jnp.int32)
    waves = pl.pallas_call(
        chain_kernel,
        out_shape=jax.ShapeDtypeStruct((GROUP * 4, NX, LANES), jnp.bfloat16),
        in_specs=[SMEM] + [VMEM] * 6,
        out_specs=VMEM,
        scratch_shapes=[pltpu.VMEM((2 * NX, NY), jnp.bfloat16)],
        compiler_params=PARAMS,
        cost_estimate=cost(4_000_000_000, 4_000_000),
        name="chain",
    )(scalars, *bands, entering, own, swapped)

    waves = lax.all_to_all(waves, ("x",) + QUAD, 0, 0, tiled=True)

    scale = 1.0 / math.sqrt(surface.shape[0] * lax.axis_size(FREQ))
    partial_image = pl.pallas_call(
        lambda *refs: image_kernel(scale, *refs),
        out_shape=jax.ShapeDtypeStruct((NX, REACH, LANES), jnp.bfloat16),
        in_specs=[SMEM] + [VMEM] * 5,
        out_specs=VMEM,
        scratch_shapes=[pltpu.VMEM((4 * GROUP, NX + H, LANES), jnp.float32)] * 2
        + [pltpu.VMEM((NX, H, LANES), jnp.float32)],
        compiler_params=PARAMS,
        cost_estimate=cost(10_000_000, 2_000_000),
        name="image",
    )(quarter, waves, *sources)

    parts = lax.all_to_all(partial_image, FREQ, 0, 0, tiled=True)

    return pl.pallas_call(
        sum_kernel,
        out_shape=jax.ShapeDtypeStruct((1, H, 1, NY), jnp.float32),
        in_specs=[VMEM],
        out_specs=VMEM,
        compiler_params=PARAMS,
        name="total",
    )(parts)


def solution(mesh):
    wide = Mesh(np.asarray(mesh.devices).reshape(3, 4, 8, 2, 2, 2), AXES)
    in_specs = (
        P(FREQ, None, None, None),
        P(DEPTH, None, None),
        P(FREQ, None, None, None, None),
        P(DEPTH, FREQ, None, None, None),
    )
    out_specs = P(DEPTH, None, FREQ, None)
    return jax.shard_map(body, mesh=wide, in_specs=in_specs, out_specs=out_specs, check_vma=False)
```

```python
import math

import jax
import jax.numpy as jnp
import numpy as np
from jax import lax
from jax.experimental import pallas as pl
from jax.experimental.pallas import tpu as pltpu
from jax.sharding import Mesh
from jax.sharding import PartitionSpec as P

H = 32
REACH = H // 2
NX = 64
NY = 256
LANES = 128
QUARTER = 64
R = 4
TAPS = 25
MID = TAPS // 2
GROUP = 4

AXES = ("zh", "x", "y", "zq", "zp", "core")
DEPTH = ("zh", "x")
FREQ = ("y", "zq", "zp", "core")
QUAD = ("zp", "core")


def tap_rows(table):
    first, second = table[:, 0], table[:, 1]

    def gap(n):
        return jnp.zeros((R, 1, n), jnp.float32)

    rows = []
    for a, b in ((first[:, 0:1], -first[:, 1:2]), (first[:, 1:2], first[:, 0:1])):
        rows.append(
            jnp.concatenate([a[..., MID:], gap(39), b, gap(39), a[..., :MID]], axis=-1)
        )
    rows_first = jnp.concatenate(rows, axis=1).reshape(R * 2, LANES)
    back = second[..., ::-1]
    rows_second = jnp.concatenate(
        [back[..., MID:], jnp.zeros((R, 2, LANES - TAPS), jnp.float32), back[..., :MID]], axis=-1
    ).reshape(R * 2, LANES)
    return rows_first, rows_second


def fan(row, height, shift):
    wide = jnp.broadcast_to(row, (height, row.shape[-1]))
    return pltpu.roll(wide, shift, 1, stride=1, stride_axis=0)


def bands_kernel(rows_first_ref, rows_second_ref, band_first, band_even, band_odd):
    row_at = lax.broadcasted_iota(jnp.int32, (NX, LANES), 0)
    lane_at = lax.broadcasted_iota(jnp.int32, (NX, LANES), 1)
    near = jnp.abs((lane_at & (NX - 1)) - row_at) <= MID
    for block in range(R * 2):
        band = fan(rows_first_ref[block : block + 1, :], NX, 0)
        band_first[block * NX : (block + 1) * NX, :] = jnp.where(near, band, 0.0).astype(jnp.bfloat16)

    left = lax.broadcasted_iota(jnp.int32, (LANES, LANES), 1) < QUARTER
    for region in range(R):
        tap_real = rows_second_ref[2 * region : 2 * region + 1, :]
        tap_imag = rows_second_ref[2 * region + 1 : 2 * region + 2, :]
        cols = slice(region * LANES, (region + 1) * LANES)
        for part, (to_real, to_imag) in enumerate(((tap_real, tap_imag), (-tap_imag, tap_real))):
            rows = slice(part * LANES, (part + 1) * LANES)
            real_band = fan(to_real, LANES, 0)
            imag_band = fan(to_imag, LANES, QUARTER)
            band_even[rows, cols] = jnp.where(left, real_band, imag_band).astype(jnp.bfloat16)
            band_odd[rows, cols] = jnp.where(left, imag_band, real_band).astype(jnp.bfloat16)


def pick(masks, values):
    out = values[R - 1]
    for region in range(R - 2, -1, -1):
        out = jnp.where(masks[region], values[region], out)
    return out


def chain_kernel(scalar_ref, band_first, band_even, band_odd, surface_ref, regions_ref, out_ref, state):
    state[:NX, :] = surface_ref[0]
    state[NX:, :] = surface_ref[1]
    blocks = scalar_ref[0]
    lane = lax.broadcasted_iota(jnp.int32, (NX, LANES), 1)
    left = lane < QUARTER
    low = lane < 96
    high = lane >= 32

    def split(values):
        return [values == float(r) for r in range(R - 1)]

    def step(b, slot):
        region = regions_ref[slot, blocks - 1 - b].astype(jnp.float32)
        halves = [region[:, :LANES], region[:, LANES:]]
        turned = [pltpu.roll(half, QUARTER, 1) for half in halves]
        full = split(region)
        even_mask = split(jnp.concatenate([jnp.where(left, a, b) for a, b in zip(halves, turned)], axis=0))
        odd_mask = split(jnp.concatenate([jnp.where(left, b, a) for a, b in zip(halves, turned)], axis=0))

        field = [
            jnp.dot(band_first[rows], state[...], preferred_element_type=jnp.float32)
            for rows in (slice(0, 4 * NX), slice(4 * NX, 8 * NX))
        ]
        field = jnp.concatenate(field, axis=0)
        even_in, odd_in = [], []
        for part in range(2):
            values = [field[(r * 2 + part) * NX : (r * 2 + part + 1) * NX] for r in range(R)]
            between = pick(full, values)
            a, b = between[:, :LANES], between[:, LANES:]
            even_in.append(jnp.concatenate([jnp.where(low, a, 0.0), jnp.where(low, b, a)], axis=0).astype(jnp.bfloat16))
            odd_in.append(jnp.concatenate([jnp.where(high, a, b), jnp.where(high, b, 0.0)], axis=0).astype(jnp.bfloat16))
        wide = jnp.dot(jnp.concatenate(even_in, axis=1), band_even[...], preferred_element_type=jnp.float32)
        even = pick(even_mask, [wide[:, r * LANES : (r + 1) * LANES] for r in range(R)])
        wide = jnp.dot(jnp.concatenate(odd_in, axis=1), band_odd[...], preferred_element_type=jnp.float32)
        odd = pick(odd_mask, [wide[:, r * LANES : (r + 1) * LANES] for r in range(R)])
        for half in range(2):
            rows = slice(half * NX, (half + 1) * NX)
            cols = slice(half * LANES, (half + 1) * LANES)
            e, o = even[rows], odd[rows]
            out_ref[slot * 4 + half * 2] = e.astype(jnp.bfloat16)
            out_ref[slot * 4 + half * 2 + 1] = o.astype(jnp.bfloat16)
            state[:NX, cols] = jnp.where(left, e, o).astype(jnp.bfloat16)
            state[NX:, cols] = pltpu.roll(jnp.where(left, o, e), QUARTER, 1).astype(jnp.bfloat16)

    def block(b, carry):
        for slot in range(GROUP):
            step(b, slot)
        return carry

    lax.fori_loop(0, blocks, block, 0)


def spread_kernel(*refs):
    out_ref = refs[-1]
    for i in range(out_ref.shape[0]):
        for slot, ref in enumerate(refs[:-1]):
            out_ref[i, slot] = ref[...]


def pack_kernel(quarter_ref, source_ref, *refs):
    outs, packed = refs[:4], refs[4]
    row_at = lax.broadcasted_iota(jnp.int32, (NX, NX), 0)
    col_at = lax.broadcasted_iota(jnp.int32, (NX, NX), 1)
    flip = (row_at + col_at == NX - 1).astype(jnp.bfloat16)
    left = lax.broadcasted_iota(jnp.int32, (NX, LANES), 1) < QUARTER
    for f in range(GROUP):
        real = jnp.dot(flip, source_ref[f, 0], preferred_element_type=jnp.float32)
        imag = jnp.dot(flip, source_ref[f, 1], preferred_element_type=jnp.float32)
        for half in range(2):
            cols = slice(half * LANES, (half + 1) * LANES)
            a = real[:, cols]
            b = pltpu.roll(imag[:, cols], QUARTER, 1)
            packed[half * 2, f] = jnp.where(left, a, b).astype(jnp.bfloat16)
            packed[half * 2 + 1, f] = jnp.where(left, b, a).astype(jnp.bfloat16)
    for k in range(4):
        outs[k][...] = packed[quarter_ref[0] ^ k]


def image_kernel(scale, quarter_ref, wave_ref, *refs):
    sources, out_ref, wave, src, totals = refs[:4], refs[4], refs[5], refs[6], refs[7]
    edge = jnp.zeros((4 * GROUP, REACH, LANES), jnp.float32)
    for ref in (wave, src):
        ref[:, :REACH, :] = edge
        ref[:, REACH + NX :, :] = edge
    for k in range(4):
        group = (quarter_ref[0] ^ k) * GROUP
        for f in range(GROUP):
            wave[k * GROUP + f, REACH : REACH + NX, :] = wave_ref[f * 4 + k].astype(jnp.float32)
            src[group + f, REACH : REACH + NX, :] = sources[k][f].astype(jnp.float32)

    def row(x, carry):
        total = jnp.zeros((H, LANES), jnp.float32)
        for i in range(4 * GROUP):
            total = total + wave[i, pl.ds(x, H), :] * src[i, pl.ds(NX - 1 - x, H), :]
        totals[x] = total
        return carry

    lax.fori_loop(0, NX, row, 0, unroll=4)
    left = lax.broadcasted_iota(jnp.int32, (REACH, LANES), 1) < QUARTER

    def fold(x, carry):
        total = totals[x]
        total = (total + pltpu.roll(total, QUARTER, 1)) * scale
        out_ref[x] = jnp.where(left, total[:REACH], total[REACH:]).astype(jnp.bfloat16)
        return carry

    lax.fori_loop(0, NX, fold, 0, unroll=8)


def sum_kernel(part_ref, out_ref):
    groups = part_ref.shape[0] // 4
    left = lax.broadcasted_iota(jnp.int32, (REACH, LANES), 1) < QUARTER
    for half in range(2):
        totals = []
        for q in (2 * half, 2 * half + 1):
            total = part_ref[q].astype(jnp.float32)
            for i in range(1, groups):
                total = total + part_ref[4 * i + q].astype(jnp.float32)
            totals.append(total)
        a, b = totals
        cols = slice(half * LANES, (half + 1) * LANES)
        out_ref[0, :REACH, 0, cols] = jnp.where(left, a, pltpu.roll(b, QUARTER, 1))
        out_ref[0, REACH:, 0, cols] = jnp.where(left, pltpu.roll(a, QUARTER, 1), b)


VMEM = pl.BlockSpec(memory_space=pltpu.VMEM)
SMEM = pl.BlockSpec(memory_space=pltpu.SMEM)
PARAMS = pltpu.CompilerParams(vmem_limit_bytes=24 << 20)


def cost(flops, moved):
    return pl.CostEstimate(flops=flops, bytes_accessed=moved, transcendentals=0)


def body(surface, regions, table, source):
    zh = lax.axis_index("zh")
    mine_x = lax.axis_index("x")
    core = lax.axis_index("core")
    blocks = lax.axis_size("zh")
    local = regions[0].astype(jnp.bfloat16)
    earlier = [
        lax.ppermute(local, "zh", [(i, i + k) for i in range(blocks - k)]) for k in range(1, blocks)
    ]
    copies = pl.pallas_call(
        spread_kernel,
        out_shape=jax.ShapeDtypeStruct((GROUP, blocks, NX, NY), jnp.bfloat16),
        in_specs=[VMEM] * blocks,
        out_specs=VMEM,
        compiler_params=PARAMS,
        cost_estimate=cost(1_000_000, 500_000),
        name="spread",
    )(local, *earlier)
    copies, local_source = lax.optimization_barrier((copies, source[0]))
    all_regions = lax.all_to_all(copies, "x", 0, 0, tiled=True)

    quarter = (lax.axis_index("zp") * 2 + core).astype(jnp.int32).reshape(1)
    packed = pl.pallas_call(
        pack_kernel,
        out_shape=(jax.ShapeDtypeStruct((GROUP, NX, LANES), jnp.bfloat16),) * 4,
        in_specs=[SMEM, VMEM],
        out_specs=(VMEM,) * 4,
        scratch_shapes=[pltpu.VMEM((4, GROUP, NX, LANES), jnp.bfloat16)],
        compiler_params=PARAMS,
        cost_estimate=cost(20_000_000, 1_000_000),
        name="pack",
    )(quarter, local_source)
    sources = [packed[0]] + [
        lax.ppermute(packed[k], QUAD, [(i, i ^ k) for i in range(4)]) for k in (1, 2, 3)
    ]
    all_regions, *early = lax.optimization_barrier((all_regions, *sources[:3]))
    sources[:3] = early

    rows_first, rows_second = tap_rows(
        lax.dynamic_index_in_dim(table, mine_x, 0, keepdims=False).astype(jnp.float32)
    )
    bands = pl.pallas_call(
        bands_kernel,
        out_shape=(
            jax.ShapeDtypeStruct((R * 2 * NX, LANES), jnp.bfloat16),
            jax.ShapeDtypeStruct((2 * LANES, R * LANES), jnp.bfloat16),
            jax.ShapeDtypeStruct((2 * LANES, R * LANES), jnp.bfloat16),
        ),
        in_specs=[VMEM] * 2,
        out_specs=(VMEM,) * 3,
        compiler_params=PARAMS,
        cost_estimate=cost(10_000_000, 1_000_000),
        name="bands",
    )(rows_first, rows_second)

    entering = lax.dynamic_index_in_dim(surface, mine_x, 0, keepdims=False)
    count = (zh + 1).astype(jnp.int32).reshape(1)
    waves = pl.pallas_call(
        chain_kernel,
        out_shape=jax.ShapeDtypeStruct((GROUP * 4, NX, LANES), jnp.bfloat16),
        in_specs=[SMEM] + [VMEM] * 5,
        out_specs=VMEM,
        scratch_shapes=[pltpu.VMEM((2 * NX, NY), jnp.bfloat16)],
        compiler_params=PARAMS,
        cost_estimate=cost(4_000_000_000, 4_000_000),
        name="chain",
    )(count, *bands, entering, all_regions)

    waves = lax.all_to_all(waves, ("x",) + QUAD, 0, 0, tiled=True)

    scale = 1.0 / math.sqrt(surface.shape[0] * lax.axis_size(FREQ))
    partial_image = pl.pallas_call(
        lambda *refs: image_kernel(scale, *refs),
        out_shape=jax.ShapeDtypeStruct((NX, REACH, LANES), jnp.bfloat16),
        in_specs=[SMEM] + [VMEM] * 5,
        out_specs=VMEM,
        scratch_shapes=[pltpu.VMEM((4 * GROUP, NX + H, LANES), jnp.float32)] * 2
        + [pltpu.VMEM((NX, H, LANES), jnp.float32)],
        compiler_params=PARAMS,
        cost_estimate=cost(10_000_000, 2_000_000),
        name="image",
    )(quarter, waves, *sources)

    parts = lax.all_to_all(partial_image, FREQ, 0, 0, tiled=True)

    return pl.pallas_call(
        sum_kernel,
        out_shape=jax.ShapeDtypeStruct((1, H, 1, NY), jnp.float32),
        in_specs=[VMEM],
        out_specs=VMEM,
        compiler_params=PARAMS,
        name="total",
    )(parts)


def solution(mesh):
    wide = Mesh(np.asarray(mesh.devices).reshape(3, 4, 8, 2, 2, 2), AXES)
    in_specs = (
        P(FREQ, None, None, None),
        P(DEPTH, None, None),
        P(FREQ, None, None, None, None),
        P(DEPTH, FREQ, None, None, None),
    )
    out_specs = P(DEPTH, None, FREQ, None)
    return jax.shard_map(body, mesh=wide, in_specs=in_specs, out_specs=out_specs, check_vma=False)
```

```python
import math

import jax
import jax.numpy as jnp
import numpy as np
from jax import lax
from jax.experimental import pallas as pl
from jax.experimental.pallas import tpu as pltpu
from jax.sharding import Mesh
from jax.sharding import PartitionSpec as P

H = 32
REACH = H // 2
NX = 64
NY = 256
LANES = 128
QUARTER = 64
R = 4
TAPS = 25
MID = TAPS // 2
GROUP = 4

AXES = ("zh", "x", "y", "zq", "zp", "core")
DEPTH = ("zh", "x")
FREQ = ("y", "zq", "zp", "core")
QUAD = ("zp", "core")


def tap_rows(table):
    first, second = table[:, 0], table[:, 1]

    def gap(n):
        return jnp.zeros((R, 1, n), jnp.float32)

    rows = []
    for a, b in ((first[:, 0:1], -first[:, 1:2]), (first[:, 1:2], first[:, 0:1])):
        rows.append(
            jnp.concatenate([a[..., MID:], gap(39), b, gap(39), a[..., :MID]], axis=-1)
        )
    rows_first = jnp.concatenate(rows, axis=1).reshape(R * 2, LANES)
    back = second[..., ::-1]
    rows_second = jnp.concatenate(
        [back[..., MID:], jnp.zeros((R, 2, LANES - TAPS), jnp.float32), back[..., :MID]], axis=-1
    ).reshape(R * 2, LANES)
    return rows_first, rows_second


def fan(row, height, shift):
    wide = jnp.broadcast_to(row, (height, row.shape[-1]))
    return pltpu.roll(wide, shift, 1, stride=1, stride_axis=0)


def bands_kernel(rows_first_ref, rows_second_ref, band_first, band_even, band_odd):
    row_at = lax.broadcasted_iota(jnp.int32, (NX, LANES), 0)
    lane_at = lax.broadcasted_iota(jnp.int32, (NX, LANES), 1)
    near = jnp.abs((lane_at & (NX - 1)) - row_at) <= MID
    for block in range(R * 2):
        band = fan(rows_first_ref[block : block + 1, :], NX, 0)
        band_first[block * NX : (block + 1) * NX, :] = jnp.where(near, band, 0.0).astype(jnp.bfloat16)

    left = lax.broadcasted_iota(jnp.int32, (LANES, LANES), 1) < QUARTER
    for region in range(R):
        tap_real = rows_second_ref[2 * region : 2 * region + 1, :]
        tap_imag = rows_second_ref[2 * region + 1 : 2 * region + 2, :]
        cols = slice(region * LANES, (region + 1) * LANES)
        for part, (to_real, to_imag) in enumerate(((tap_real, tap_imag), (-tap_imag, tap_real))):
            rows = slice(part * LANES, (part + 1) * LANES)
            real_band = fan(to_real, LANES, 0)
            imag_band = fan(to_imag, LANES, QUARTER)
            band_even[rows, cols] = jnp.where(left, real_band, imag_band).astype(jnp.bfloat16)
            band_odd[rows, cols] = jnp.where(left, imag_band, real_band).astype(jnp.bfloat16)


def pick(masks, values):
    out = values[R - 1]
    for region in range(R - 2, -1, -1):
        out = jnp.where(masks[region], values[region], out)
    return out


def chain_kernel(scalar_ref, band_first, band_even, band_odd, surface_ref, regions_ref, out_ref, state):
    state[:NX, :] = surface_ref[0]
    state[NX:, :] = surface_ref[1]
    blocks = scalar_ref[0]
    lane = lax.broadcasted_iota(jnp.int32, (NX, LANES), 1)
    left = lane < QUARTER
    low = lane < 96
    high = lane >= 32

    def split(values):
        return [values == float(r) for r in range(R - 1)]

    def step(b, slot):
        region = regions_ref[slot, blocks - 1 - b].astype(jnp.float32)
        halves = [region[:, :LANES], region[:, LANES:]]
        turned = [pltpu.roll(half, QUARTER, 1) for half in halves]
        full = split(region)
        even_mask = split(jnp.concatenate([jnp.where(left, a, b) for a, b in zip(halves, turned)], axis=0))
        odd_mask = split(jnp.concatenate([jnp.where(left, b, a) for a, b in zip(halves, turned)], axis=0))

        field = [
            jnp.dot(band_first[rows], state[...], preferred_element_type=jnp.float32)
            for rows in (slice(0, 4 * NX), slice(4 * NX, 8 * NX))
        ]
        field = jnp.concatenate(field, axis=0)
        even_in, odd_in = [], []
        for part in range(2):
            values = [field[(r * 2 + part) * NX : (r * 2 + part + 1) * NX] for r in range(R)]
            between = pick(full, values)
            a, b = between[:, :LANES], between[:, LANES:]
            even_in.append(jnp.concatenate([jnp.where(low, a, 0.0), jnp.where(low, b, a)], axis=0).astype(jnp.bfloat16))
            odd_in.append(jnp.concatenate([jnp.where(high, a, b), jnp.where(high, b, 0.0)], axis=0).astype(jnp.bfloat16))
        wide = jnp.dot(jnp.concatenate(even_in, axis=1), band_even[...], preferred_element_type=jnp.float32)
        even = pick(even_mask, [wide[:, r * LANES : (r + 1) * LANES] for r in range(R)])
        wide = jnp.dot(jnp.concatenate(odd_in, axis=1), band_odd[...], preferred_element_type=jnp.float32)
        odd = pick(odd_mask, [wide[:, r * LANES : (r + 1) * LANES] for r in range(R)])
        for half in range(2):
            rows = slice(half * NX, (half + 1) * NX)
            cols = slice(half * LANES, (half + 1) * LANES)
            e, o = even[rows], odd[rows]
            out_ref[slot * 4 + half * 2] = e.astype(jnp.bfloat16)
            out_ref[slot * 4 + half * 2 + 1] = o.astype(jnp.bfloat16)
            state[:NX, cols] = jnp.where(left, e, o).astype(jnp.bfloat16)
            state[NX:, cols] = pltpu.roll(jnp.where(left, o, e), QUARTER, 1).astype(jnp.bfloat16)

    def block(b, carry):
        for slot in range(GROUP):
            step(b, slot)
        return carry

    lax.fori_loop(0, blocks, block, 0)


def spread_kernel(*refs):
    out_ref = refs[-1]
    for i in range(out_ref.shape[0]):
        for slot, ref in enumerate(refs[:-1]):
            out_ref[i, slot] = ref[...]


def pack_kernel(quarter_ref, source_ref, *refs):
    own_ref, core_ref, chip_ref, packed = refs
    row_at = lax.broadcasted_iota(jnp.int32, (NX, NX), 0)
    col_at = lax.broadcasted_iota(jnp.int32, (NX, NX), 1)
    flip = (row_at + col_at == NX - 1).astype(jnp.bfloat16)
    left = lax.broadcasted_iota(jnp.int32, (NX, LANES), 1) < QUARTER
    for f in range(GROUP):
        real = jnp.dot(flip, source_ref[f, 0], preferred_element_type=jnp.float32)
        imag = jnp.dot(flip, source_ref[f, 1], preferred_element_type=jnp.float32)
        for half in range(2):
            cols = slice(half * LANES, (half + 1) * LANES)
            a = real[:, cols]
            b = pltpu.roll(imag[:, cols], QUARTER, 1)
            packed[half * 2, f] = jnp.where(left, a, b).astype(jnp.bfloat16)
            packed[half * 2 + 1, f] = jnp.where(left, b, a).astype(jnp.bfloat16)
    mine = quarter_ref[0]
    own_ref[...] = packed[mine]
    core_ref[0] = packed[mine ^ 1]
    core_ref[1] = packed[mine ^ 3]
    chip_ref[0] = packed[mine ^ 2]


def image_kernel(scale, quarter_ref, wave_ref, own_ref, core_ref, chip_ref, out_ref, wave, src, totals):
    sources = [own_ref, core_ref.at[0], chip_ref.at[0], chip_ref.at[1]]
    edge = jnp.zeros((4 * GROUP, REACH, LANES), jnp.float32)
    for ref in (wave, src):
        ref[:, :REACH, :] = edge
        ref[:, REACH + NX :, :] = edge
    for k in range(4):
        group = (quarter_ref[0] ^ k) * GROUP
        for f in range(GROUP):
            wave[k * GROUP + f, REACH : REACH + NX, :] = wave_ref[f * 4 + k].astype(jnp.float32)
            src[group + f, REACH : REACH + NX, :] = sources[k][f].astype(jnp.float32)

    def row(x, carry):
        total = jnp.zeros((H, LANES), jnp.float32)
        for i in range(4 * GROUP):
            total = total + wave[i, pl.ds(x, H), :] * src[i, pl.ds(NX - 1 - x, H), :]
        totals[x] = total
        return carry

    lax.fori_loop(0, NX, row, 0, unroll=4)
    left = lax.broadcasted_iota(jnp.int32, (REACH, LANES), 1) < QUARTER

    def fold(x, carry):
        total = totals[x]
        total = (total + pltpu.roll(total, QUARTER, 1)) * scale
        out_ref[x] = jnp.where(left, total[:REACH], total[REACH:]).astype(jnp.bfloat16)
        return carry

    lax.fori_loop(0, NX, fold, 0, unroll=8)


def sum_kernel(part_ref, out_ref):
    groups = part_ref.shape[0] // 4
    left = lax.broadcasted_iota(jnp.int32, (REACH, LANES), 1) < QUARTER
    for half in range(2):
        totals = []
        for q in (2 * half, 2 * half + 1):
            total = part_ref[q].astype(jnp.float32)
            for i in range(1, groups):
                total = total + part_ref[4 * i + q].astype(jnp.float32)
            totals.append(total)
        a, b = totals
        cols = slice(half * LANES, (half + 1) * LANES)
        out_ref[0, :REACH, 0, cols] = jnp.where(left, a, pltpu.roll(b, QUARTER, 1))
        out_ref[0, REACH:, 0, cols] = jnp.where(left, pltpu.roll(a, QUARTER, 1), b)


VMEM = pl.BlockSpec(memory_space=pltpu.VMEM)
SMEM = pl.BlockSpec(memory_space=pltpu.SMEM)
PARAMS = pltpu.CompilerParams(vmem_limit_bytes=24 << 20)


def cost(flops, moved):
    return pl.CostEstimate(flops=flops, bytes_accessed=moved, transcendentals=0)


def body(surface, regions, table, source):
    zh = lax.axis_index("zh")
    mine_x = lax.axis_index("x")
    core = lax.axis_index("core")
    blocks = lax.axis_size("zh")
    local = regions[0].astype(jnp.bfloat16)
    earlier = [
        lax.ppermute(local, "zh", [(i, i + k) for i in range(blocks - k)]) for k in range(1, blocks)
    ]
    quarter = (lax.axis_index("zp") * 2 + core).astype(jnp.int32).reshape(1)
    four = jax.ShapeDtypeStruct((GROUP, NX, LANES), jnp.bfloat16)
    pair = jax.ShapeDtypeStruct((2, GROUP, NX, LANES), jnp.bfloat16)
    one = jax.ShapeDtypeStruct((1, GROUP, NX, LANES), jnp.bfloat16)
    packed, to_core, to_chip = pl.pallas_call(
        pack_kernel,
        out_shape=(four, pair, one),
        in_specs=[SMEM, VMEM],
        out_specs=(VMEM,) * 3,
        scratch_shapes=[pltpu.VMEM((4, GROUP, NX, LANES), jnp.bfloat16)],
        compiler_params=PARAMS,
        cost_estimate=cost(20_000_000, 1_000_000),
        name="pack",
    )(quarter, source[0])
    from_core = lax.ppermute(to_core, "core", [(0, 1), (1, 0)])
    copies = pl.pallas_call(
        spread_kernel,
        out_shape=jax.ShapeDtypeStruct((GROUP, blocks, NX, NY), jnp.bfloat16),
        in_specs=[VMEM] * blocks,
        out_specs=VMEM,
        compiler_params=PARAMS,
        cost_estimate=cost(1_000_000, 500_000),
        name="spread",
    )(local, *earlier)
    copies, from_core = lax.optimization_barrier((copies, from_core))
    from_chip = lax.ppermute(
        jnp.concatenate([to_chip, from_core[1:]], axis=0), "zp", [(0, 1), (1, 0)]
    )
    all_regions = lax.all_to_all(copies, "x", 0, 0, tiled=True)

    rows_first, rows_second = tap_rows(
        lax.dynamic_index_in_dim(table, mine_x, 0, keepdims=False).astype(jnp.float32)
    )
    bands = pl.pallas_call(
        bands_kernel,
        out_shape=(
            jax.ShapeDtypeStruct((R * 2 * NX, LANES), jnp.bfloat16),
            jax.ShapeDtypeStruct((2 * LANES, R * LANES), jnp.bfloat16),
            jax.ShapeDtypeStruct((2 * LANES, R * LANES), jnp.bfloat16),
        ),
        in_specs=[VMEM] * 2,
        out_specs=(VMEM,) * 3,
        compiler_params=PARAMS,
        cost_estimate=cost(10_000_000, 1_000_000),
        name="bands",
    )(rows_first, rows_second)

    entering = lax.dynamic_index_in_dim(surface, mine_x, 0, keepdims=False)
    count = (zh + 1).astype(jnp.int32).reshape(1)
    waves = pl.pallas_call(
        chain_kernel,
        out_shape=jax.ShapeDtypeStruct((GROUP * 4, NX, LANES), jnp.bfloat16),
        in_specs=[SMEM] + [VMEM] * 5,
        out_specs=VMEM,
        scratch_shapes=[pltpu.VMEM((2 * NX, NY), jnp.bfloat16)],
        compiler_params=PARAMS,
        cost_estimate=cost(1_000_000, 100_000),
        name="chain",
    )(count, *bands, entering, all_regions)

    waves, from_chip = lax.optimization_barrier((waves, from_chip))
    waves = lax.all_to_all(waves, ("x",) + QUAD, 0, 0, tiled=True)

    scale = 1.0 / math.sqrt(surface.shape[0] * lax.axis_size(FREQ))
    partial_image = pl.pallas_call(
        lambda *refs: image_kernel(scale, *refs),
        out_shape=jax.ShapeDtypeStruct((NX, REACH, LANES), jnp.bfloat16),
        in_specs=[SMEM] + [VMEM] * 4,
        out_specs=VMEM,
        scratch_shapes=[pltpu.VMEM((4 * GROUP, NX + H, LANES), jnp.float32)] * 2
        + [pltpu.VMEM((NX, H, LANES), jnp.float32)],
        compiler_params=PARAMS,
        cost_estimate=cost(10_000_000, 2_000_000),
        name="image",
    )(quarter, waves, packed, from_core, from_chip)

    parts = lax.all_to_all(partial_image, FREQ, 0, 0, tiled=True)

    return pl.pallas_call(
        sum_kernel,
        out_shape=jax.ShapeDtypeStruct((1, H, 1, NY), jnp.float32),
        in_specs=[VMEM],
        out_specs=VMEM,
        compiler_params=PARAMS,
        name="total",
    )(parts)


def solution(mesh):
    wide = Mesh(np.asarray(mesh.devices).reshape(3, 4, 8, 2, 2, 2), AXES)
    in_specs = (
        P(FREQ, None, None, None),
        P(DEPTH, None, None),
        P(FREQ, None, None, None, None),
        P(DEPTH, FREQ, None, None, None),
    )
    out_specs = P(DEPTH, None, FREQ, None)
    return jax.shard_map(body, mesh=wide, in_specs=in_specs, out_specs=out_specs, check_vma=False)
```

```python
import math

import jax
import jax.numpy as jnp
import numpy as np
from jax import lax
from jax.experimental import pallas as pl
from jax.experimental.pallas import tpu as pltpu
from jax.sharding import Mesh
from jax.sharding import PartitionSpec as P

H = 32
REACH = H // 2
NX = 64
NY = 256
LANES = 128
QUARTER = 64
R = 4
TAPS = 25
MID = TAPS // 2
GROUP = 4

AXES = ("zh", "x", "y", "zq", "zp", "core")
DEPTH = ("zh", "x")
FREQ = ("y", "zq", "zp", "core")
QUAD = ("zp", "core")


def onehot(shape, fit, value=1.0):
    row_at = lax.broadcasted_iota(jnp.int32, shape, 0)
    col_at = lax.broadcasted_iota(jnp.int32, shape, 1)
    return jnp.where(fit(row_at, col_at), value, 0.0).astype(jnp.bfloat16)


def exact(a, b):
    return jnp.dot(a, b, preferred_element_type=jnp.float32)


def tap_rows(taps):
    many = R * 2

    def row(pass_at, part):
        return lambda i, j: j == (i >> 1) * 4 + pass_at * 2 + part(i & 1)

    def lanes(shift, sign=1):
        return onehot((LANES, LANES), lambda k, n: k == ((sign * n + shift) & (LANES - 1)))

    def chosen(fit):
        return exact(fit, taps).astype(jnp.bfloat16)

    shape = (many, 2 * many)
    straight = chosen(onehot(shape, row(0, lambda p: p)))
    row_at = lax.broadcasted_iota(jnp.int32, (many, LANES), 0)
    crossed = exact(chosen(onehot(shape, row(0, lambda p: 1 - p))), lanes(-(QUARTER - MID)))
    crossed = jnp.where((row_at & 1) == 0, -crossed, crossed)
    rows_first = exact(straight, lanes(MID)) + crossed
    rows_second = exact(chosen(onehot(shape, row(1, lambda p: p))), lanes(MID, -1))
    return rows_first, rows_second


def fan(row, height, shift):
    wide = jnp.broadcast_to(row, (height, row.shape[-1]))
    return pltpu.roll(wide, shift, 1, stride=1, stride_axis=0)


def bands_kernel(index_ref, table_ref, band_first, band_even, band_odd):
    taps = table_ref[pl.ds(pl.multiple_of(index_ref[0] * 16, 16), 16), :]
    rows_first, rows_second = tap_rows(taps)
    row_at = lax.broadcasted_iota(jnp.int32, (NX, LANES), 0)
    lane_at = lax.broadcasted_iota(jnp.int32, (NX, LANES), 1)
    near = jnp.abs((lane_at & (NX - 1)) - row_at) <= MID
    for block in range(R * 2):
        band = fan(rows_first[block : block + 1, :], NX, 0)
        band_first[block * NX : (block + 1) * NX, :] = jnp.where(near, band, 0.0).astype(jnp.bfloat16)

    left = lax.broadcasted_iota(jnp.int32, (LANES, LANES), 1) < QUARTER
    for region in range(R):
        tap_real = rows_second[2 * region : 2 * region + 1, :]
        tap_imag = rows_second[2 * region + 1 : 2 * region + 2, :]
        cols = slice(region * LANES, (region + 1) * LANES)
        for part, (to_real, to_imag) in enumerate(((tap_real, tap_imag), (-tap_imag, tap_real))):
            rows = slice(part * LANES, (part + 1) * LANES)
            real_band = fan(to_real, LANES, 0)
            imag_band = fan(to_imag, LANES, QUARTER)
            band_even[rows, cols] = jnp.where(left, real_band, imag_band).astype(jnp.bfloat16)
            band_odd[rows, cols] = jnp.where(left, imag_band, real_band).astype(jnp.bfloat16)


def pick(masks, values):
    out = values[R - 1]
    for region in range(R - 2, -1, -1):
        out = jnp.where(masks[region], values[region], out)
    return out


def chain_kernel(scalar_ref, band_first, band_even, band_odd, surface_ref, regions_ref, out_ref, state):
    state[:NX, :] = surface_ref[scalar_ref[1], 0]
    state[NX:, :] = surface_ref[scalar_ref[1], 1]
    blocks = scalar_ref[0]
    lane = lax.broadcasted_iota(jnp.int32, (NX, LANES), 1)
    left = lane < QUARTER
    low = lane < 96
    high = lane >= 32

    def split(values):
        return [values == float(r) for r in range(R - 1)]

    def step(b, slot):
        region = regions_ref[slot, blocks - 1 - b].astype(jnp.float32)
        halves = [region[:, :LANES], region[:, LANES:]]
        turned = [pltpu.roll(half, QUARTER, 1) for half in halves]
        full = split(region)
        even_mask = split(jnp.concatenate([jnp.where(left, a, b) for a, b in zip(halves, turned)], axis=0))
        odd_mask = split(jnp.concatenate([jnp.where(left, b, a) for a, b in zip(halves, turned)], axis=0))

        field = [
            jnp.dot(band_first[rows], state[...], preferred_element_type=jnp.float32)
            for rows in (slice(0, 4 * NX), slice(4 * NX, 8 * NX))
        ]
        field = jnp.concatenate(field, axis=0)
        even_in, odd_in = [], []
        for part in range(2):
            values = [field[(r * 2 + part) * NX : (r * 2 + part + 1) * NX] for r in range(R)]
            between = pick(full, values)
            a, b = between[:, :LANES], between[:, LANES:]
            even_in.append(jnp.concatenate([jnp.where(low, a, 0.0), jnp.where(low, b, a)], axis=0).astype(jnp.bfloat16))
            odd_in.append(jnp.concatenate([jnp.where(high, a, b), jnp.where(high, b, 0.0)], axis=0).astype(jnp.bfloat16))
        wide = jnp.dot(jnp.concatenate(even_in, axis=1), band_even[...], preferred_element_type=jnp.float32)
        even = pick(even_mask, [wide[:, r * LANES : (r + 1) * LANES] for r in range(R)])
        wide = jnp.dot(jnp.concatenate(odd_in, axis=1), band_odd[...], preferred_element_type=jnp.float32)
        odd = pick(odd_mask, [wide[:, r * LANES : (r + 1) * LANES] for r in range(R)])
        for half in range(2):
            rows = slice(half * NX, (half + 1) * NX)
            cols = slice(half * LANES, (half + 1) * LANES)
            e, o = even[rows], odd[rows]
            out_ref[slot * 4 + half * 2] = e.astype(jnp.bfloat16)
            out_ref[slot * 4 + half * 2 + 1] = o.astype(jnp.bfloat16)
            state[:NX, cols] = jnp.where(left, e, o).astype(jnp.bfloat16)
            state[NX:, cols] = pltpu.roll(jnp.where(left, o, e), QUARTER, 1).astype(jnp.bfloat16)

    def block(b, carry):
        for slot in range(GROUP):
            step(b, slot)
        return carry

    lax.fori_loop(0, blocks, block, 0)


def spread_kernel(*refs):
    out_ref = refs[-1]
    for i in range(out_ref.shape[0]):
        for slot, ref in enumerate(refs[:-1]):
            out_ref[i, slot] = ref[...]


def pack_kernel(quarter_ref, source_ref, *refs):
    own_ref, core_ref, chip_ref, packed = refs
    row_at = lax.broadcasted_iota(jnp.int32, (NX, NX), 0)
    col_at = lax.broadcasted_iota(jnp.int32, (NX, NX), 1)
    flip = (row_at + col_at == NX - 1).astype(jnp.bfloat16)
    left = lax.broadcasted_iota(jnp.int32, (NX, LANES), 1) < QUARTER
    for f in range(GROUP):
        real = jnp.dot(flip, source_ref[f, 0], preferred_element_type=jnp.float32)
        imag = jnp.dot(flip, source_ref[f, 1], preferred_element_type=jnp.float32)
        for half in range(2):
            cols = slice(half * LANES, (half + 1) * LANES)
            a = real[:, cols]
            b = pltpu.roll(imag[:, cols], QUARTER, 1)
            packed[half * 2, f] = jnp.where(left, a, b).astype(jnp.bfloat16)
            packed[half * 2 + 1, f] = jnp.where(left, b, a).astype(jnp.bfloat16)
    mine = quarter_ref[0]
    own_ref[...] = packed[mine]
    core_ref[0] = packed[mine ^ 1]
    core_ref[1] = packed[mine ^ 3]
    chip_ref[0] = packed[mine ^ 2]


def image_kernel(scale, quarter_ref, wave_ref, own_ref, core_ref, chip_ref, out_ref, wave, src, totals):
    sources = [own_ref, core_ref.at[0], chip_ref.at[0], chip_ref.at[1]]
    edge = jnp.zeros((4 * GROUP, REACH, LANES), jnp.float32)
    for ref in (wave, src):
        ref[:, :REACH, :] = edge
        ref[:, REACH + NX :, :] = edge
    for k in range(4):
        group = (quarter_ref[0] ^ k) * GROUP
        for f in range(GROUP):
            wave[k * GROUP + f, REACH : REACH + NX, :] = wave_ref[f * 4 + k].astype(jnp.float32)
            src[group + f, REACH : REACH + NX, :] = sources[k][f].astype(jnp.float32)

    tall, deep = NX // 8, H // 8
    inside = range(1, tall + deep - 2)

    def rows_from(start, carry):
        sums = {}
        for i in range(4 * GROUP):
            waves = {j: wave[i, pl.ds(start + 8 * j, 8), :] for j in inside}
            sources = {j: src[i, pl.ds(7 - start + 8 * j, 8), :] for j in inside}
            for m in range(tall):
                for n in range(deep):
                    j, k = m + n, tall - 1 - m + n
                    if j in inside and k in inside:
                        term = waves[j] * sources[k]
                        sums[m, n] = sums[m, n] + term if i else term
        for m in range(tall):
            for n in range(deep):
                value = sums.get((m, n))
                totals[start + 8 * m, 8 * n : 8 * n + 8, :] = jnp.zeros((8, LANES), jnp.float32) if value is None else value
        return carry

    lax.fori_loop(0, 8, rows_from, 0)
    left = lax.broadcasted_iota(jnp.int32, (REACH, LANES), 1) < QUARTER

    def fold(x, carry):
        total = totals[x]
        total = (total + pltpu.roll(total, QUARTER, 1)) * scale
        out_ref[x] = jnp.where(left, total[:REACH], total[REACH:]).astype(jnp.bfloat16)
        return carry

    lax.fori_loop(0, NX, fold, 0, unroll=8)


def sum_kernel(part_ref, out_ref):
    groups = part_ref.shape[0] // 4
    left = lax.broadcasted_iota(jnp.int32, (REACH, LANES), 1) < QUARTER
    for half in range(2):
        totals = []
        for q in (2 * half, 2 * half + 1):
            total = part_ref[q].astype(jnp.float32)
            for i in range(1, groups):
                total = total + part_ref[4 * i + q].astype(jnp.float32)
            totals.append(total)
        a, b = totals
        cols = slice(half * LANES, (half + 1) * LANES)
        out_ref[0, :REACH, 0, cols] = jnp.where(left, a, pltpu.roll(b, QUARTER, 1))
        out_ref[0, REACH:, 0, cols] = jnp.where(left, pltpu.roll(a, QUARTER, 1), b)


VMEM = pl.BlockSpec(memory_space=pltpu.VMEM)
SMEM = pl.BlockSpec(memory_space=pltpu.SMEM)
PARAMS = pltpu.CompilerParams(vmem_limit_bytes=24 << 20)


def cost(flops, moved):
    return pl.CostEstimate(flops=flops, bytes_accessed=moved, transcendentals=0)


def body(surface, regions, table, source):
    zh = lax.axis_index("zh")
    mine_x = lax.axis_index("x")
    core = lax.axis_index("core")
    blocks = lax.axis_size("zh")
    local, local_source = lax.optimization_barrier((regions[0].astype(jnp.bfloat16), source[0]))
    earlier = [
        lax.ppermute(local, "zh", [(i, i + k) for i in range(blocks - k)]) for k in range(1, blocks)
    ]
    quarter = (lax.axis_index("zp") * 2 + core).astype(jnp.int32).reshape(1)
    four = jax.ShapeDtypeStruct((GROUP, NX, LANES), jnp.bfloat16)
    pair = jax.ShapeDtypeStruct((2, GROUP, NX, LANES), jnp.bfloat16)
    one = jax.ShapeDtypeStruct((1, GROUP, NX, LANES), jnp.bfloat16)
    packed, to_core, to_chip = pl.pallas_call(
        pack_kernel,
        out_shape=(four, pair, one),
        in_specs=[SMEM, VMEM],
        out_specs=(VMEM,) * 3,
        scratch_shapes=[pltpu.VMEM((4, GROUP, NX, LANES), jnp.bfloat16)],
        compiler_params=PARAMS,
        cost_estimate=cost(20_000_000, 1_000_000),
        name="pack",
    )(quarter, local_source)
    copies = pl.pallas_call(
        spread_kernel,
        out_shape=jax.ShapeDtypeStruct((GROUP, blocks, NX, NY), jnp.bfloat16),
        in_specs=[VMEM] * blocks,
        out_specs=VMEM,
        compiler_params=PARAMS,
        cost_estimate=cost(1_000_000, 500_000),
        name="spread",
    )(local, *earlier)
    copies, to_core, table = lax.optimization_barrier((copies, to_core, table))
    from_core = lax.ppermute(to_core, "core", [(0, 1), (1, 0)])
    from_chip = lax.ppermute(
        jnp.concatenate([to_chip, from_core[1:]], axis=0), "zp", [(0, 1), (1, 0)]
    )
    all_regions = lax.all_to_all(copies, "x", 0, 0, tiled=True)

    padded = jnp.pad(table.reshape(GROUP * R * 4, TAPS), ((0, 0), (0, LANES - TAPS)))
    bands = pl.pallas_call(
        bands_kernel,
        out_shape=(
            jax.ShapeDtypeStruct((R * 2 * NX, LANES), jnp.bfloat16),
            jax.ShapeDtypeStruct((2 * LANES, R * LANES), jnp.bfloat16),
            jax.ShapeDtypeStruct((2 * LANES, R * LANES), jnp.bfloat16),
        ),
        in_specs=[SMEM, VMEM],
        out_specs=(VMEM,) * 3,
        compiler_params=PARAMS,
        cost_estimate=cost(10_000_000, 1_000_000),
        name="bands",
    )(mine_x.astype(jnp.int32).reshape(1), padded)

    scalars = jnp.stack([zh + 1, mine_x]).astype(jnp.int32)
    waves = pl.pallas_call(
        chain_kernel,
        out_shape=jax.ShapeDtypeStruct((GROUP * 4, NX, LANES), jnp.bfloat16),
        in_specs=[SMEM] + [VMEM] * 5,
        out_specs=VMEM,
        scratch_shapes=[pltpu.VMEM((2 * NX, NY), jnp.bfloat16)],
        compiler_params=PARAMS,
        cost_estimate=cost(4_000_000_000, 4_000_000),
        name="chain",
    )(scalars, *bands, surface, all_regions)

    waves, from_chip = lax.optimization_barrier((waves, from_chip))
    waves = lax.all_to_all(waves, ("x",) + QUAD, 0, 0, tiled=True)

    scale = 1.0 / math.sqrt(surface.shape[0] * lax.axis_size(FREQ))
    partial_image = pl.pallas_call(
        lambda *refs: image_kernel(scale, *refs),
        out_shape=jax.ShapeDtypeStruct((NX, REACH, LANES), jnp.bfloat16),
        in_specs=[SMEM] + [VMEM] * 4,
        out_specs=VMEM,
        scratch_shapes=[pltpu.VMEM((4 * GROUP, NX + H, LANES), jnp.float32)] * 2
        + [pltpu.VMEM((NX, H, LANES), jnp.float32)],
        compiler_params=PARAMS,
        cost_estimate=cost(10_000_000, 2_000_000),
        name="image",
    )(quarter, waves, packed, from_core, from_chip)

    parts = lax.all_to_all(partial_image, FREQ, 0, 0, tiled=True)

    return pl.pallas_call(
        sum_kernel,
        out_shape=jax.ShapeDtypeStruct((1, H, 1, NY), jnp.float32),
        in_specs=[VMEM],
        out_specs=VMEM,
        compiler_params=PARAMS,
        name="total",
    )(parts)


def solution(mesh):
    wide = Mesh(np.asarray(mesh.devices).reshape(3, 4, 8, 2, 2, 2), AXES)
    in_specs = (
        P(FREQ, None, None, None),
        P(DEPTH, None, None),
        P(FREQ, None, None, None, None),
        P(DEPTH, FREQ, None, None, None),
    )
    out_specs = P(DEPTH, None, FREQ, None)
    return jax.shard_map(body, mesh=wide, in_specs=in_specs, out_specs=out_specs, check_vma=False)
```

```python
import math

import jax
import jax.numpy as jnp
import numpy as np
from jax import lax
from jax.experimental import pallas as pl
from jax.experimental.pallas import tpu as pltpu
from jax.sharding import Mesh
from jax.sharding import PartitionSpec as P

H = 32
REACH = H // 2
NX = 64
NY = 256
LANES = 128
QUARTER = 64
R = 4
TAPS = 25
MID = TAPS // 2
GROUP = 4

AXES = ("zh", "x", "y", "zq", "zp", "core")
DEPTH = ("zh", "x")
FREQ = ("y", "zq", "zp", "core")
QUAD = ("zp", "core")


def onehot(shape, fit, value=1.0):
    row_at = lax.broadcasted_iota(jnp.int32, shape, 0)
    col_at = lax.broadcasted_iota(jnp.int32, shape, 1)
    return jnp.where(fit(row_at, col_at), value, 0.0).astype(jnp.bfloat16)


def exact(a, b):
    return jnp.dot(a, b, preferred_element_type=jnp.float32)


def tap_rows(taps):
    many = R * 2

    def row(pass_at, part):
        return lambda i, j: j == (i >> 1) * 4 + pass_at * 2 + part(i & 1)

    def lanes(shift, sign=1):
        return onehot((LANES, LANES), lambda k, n: k == ((sign * n + shift) & (LANES - 1)))

    def chosen(fit):
        return exact(fit, taps).astype(jnp.bfloat16)

    shape = (many, 2 * many)
    straight = chosen(onehot(shape, row(0, lambda p: p)))
    row_at = lax.broadcasted_iota(jnp.int32, (many, LANES), 0)
    crossed = exact(chosen(onehot(shape, row(0, lambda p: 1 - p))), lanes(-(QUARTER - MID)))
    crossed = jnp.where((row_at & 1) == 0, -crossed, crossed)
    rows_first = exact(straight, lanes(MID)) + crossed
    rows_second = exact(chosen(onehot(shape, row(1, lambda p: p))), lanes(MID, -1))
    return rows_first, rows_second


def fan(row, height, shift):
    wide = jnp.broadcast_to(row, (height, row.shape[-1]))
    return pltpu.roll(wide, shift, 1, stride=1, stride_axis=0)


def bands_kernel(index_ref, table_ref, band_first, band_even, band_odd):
    taps = table_ref[pl.ds(pl.multiple_of(index_ref[0] * 16, 16), 16), :]
    rows_first, rows_second = tap_rows(taps)
    row_at = lax.broadcasted_iota(jnp.int32, (NX, LANES), 0)
    lane_at = lax.broadcasted_iota(jnp.int32, (NX, LANES), 1)
    near = jnp.abs((lane_at & (NX - 1)) - row_at) <= MID
    for block in range(R * 2):
        band = fan(rows_first[block : block + 1, :], NX, 0)
        band_first[block * NX : (block + 1) * NX, :] = jnp.where(near, band, 0.0).astype(jnp.bfloat16)

    left = lax.broadcasted_iota(jnp.int32, (LANES, LANES), 1) < QUARTER
    for region in range(R):
        tap_real = rows_second[2 * region : 2 * region + 1, :]
        tap_imag = rows_second[2 * region + 1 : 2 * region + 2, :]
        cols = slice(region * LANES, (region + 1) * LANES)
        for part, (to_real, to_imag) in enumerate(((tap_real, tap_imag), (-tap_imag, tap_real))):
            rows = slice(part * LANES, (part + 1) * LANES)
            real_band = fan(to_real, LANES, 0)
            imag_band = fan(to_imag, LANES, QUARTER)
            band_even[rows, cols] = jnp.where(left, real_band, imag_band).astype(jnp.bfloat16)
            band_odd[rows, cols] = jnp.where(left, imag_band, real_band).astype(jnp.bfloat16)


def pick(masks, values):
    out = values[R - 1]
    for region in range(R - 2, -1, -1):
        out = jnp.where(masks[region], values[region], out)
    return out


def chain_kernel(scalar_ref, band_first, band_even, band_odd, surface_ref, *refs):
    columns, out_ref, state, regions_ref = refs[:GROUP], refs[GROUP], refs[GROUP + 1], refs[GROUP + 2]
    for k in range(GROUP):
        regions_ref[scalar_ref[1] ^ k] = columns[k][...]
    state[:NX, :] = surface_ref[scalar_ref[1], 0]
    state[NX:, :] = surface_ref[scalar_ref[1], 1]
    blocks = scalar_ref[0]
    lane = lax.broadcasted_iota(jnp.int32, (NX, LANES), 1)
    left = lane < QUARTER
    low = lane < 96
    high = lane >= 32

    def split(values):
        return [values == float(r) for r in range(R - 1)]

    def step(b, slot):
        region = regions_ref[slot, blocks - 1 - b].astype(jnp.float32)
        halves = [region[:, :LANES], region[:, LANES:]]
        turned = [pltpu.roll(half, QUARTER, 1) for half in halves]
        full = split(region)
        even_mask = split(jnp.concatenate([jnp.where(left, a, b) for a, b in zip(halves, turned)], axis=0))
        odd_mask = split(jnp.concatenate([jnp.where(left, b, a) for a, b in zip(halves, turned)], axis=0))

        field = [
            jnp.dot(band_first[rows], state[...], preferred_element_type=jnp.float32)
            for rows in (slice(0, 4 * NX), slice(4 * NX, 8 * NX))
        ]
        field = jnp.concatenate(field, axis=0)
        even_in, odd_in = [], []
        for part in range(2):
            values = [field[(r * 2 + part) * NX : (r * 2 + part + 1) * NX] for r in range(R)]
            between = pick(full, values)
            a, b = between[:, :LANES], between[:, LANES:]
            even_in.append(jnp.concatenate([jnp.where(low, a, 0.0), jnp.where(low, b, a)], axis=0).astype(jnp.bfloat16))
            odd_in.append(jnp.concatenate([jnp.where(high, a, b), jnp.where(high, b, 0.0)], axis=0).astype(jnp.bfloat16))
        wide = jnp.dot(jnp.concatenate(even_in, axis=1), band_even[...], preferred_element_type=jnp.float32)
        even = pick(even_mask, [wide[:, r * LANES : (r + 1) * LANES] for r in range(R)])
        wide = jnp.dot(jnp.concatenate(odd_in, axis=1), band_odd[...], preferred_element_type=jnp.float32)
        odd = pick(odd_mask, [wide[:, r * LANES : (r + 1) * LANES] for r in range(R)])
        for half in range(2):
            rows = slice(half * NX, (half + 1) * NX)
            cols = slice(half * LANES, (half + 1) * LANES)
            e, o = even[rows], odd[rows]
            out_ref[slot * 4 + half * 2] = e.astype(jnp.bfloat16)
            out_ref[slot * 4 + half * 2 + 1] = o.astype(jnp.bfloat16)
            state[:NX, cols] = jnp.where(left, e, o).astype(jnp.bfloat16)
            state[NX:, cols] = pltpu.roll(jnp.where(left, o, e), QUARTER, 1).astype(jnp.bfloat16)

    def block(b, carry):
        for slot in range(GROUP):
            step(b, slot)
        return carry

    lax.fori_loop(0, blocks, block, 0)


def stack_kernel(zh_ref, local_ref, near_ref, far_ref, out_ref):
    last = zh_ref[0] == 2
    out_ref[0] = local_ref[...]

    @pl.when(last)
    def _():
        out_ref[1] = far_ref[0]
        out_ref[2] = far_ref[1]

    @pl.when(jnp.logical_not(last))
    def _():
        out_ref[1] = near_ref[...]
        out_ref[2] = near_ref[...]


def pack_kernel(quarter_ref, source_ref, *refs):
    own_ref, core_ref, chip_ref, packed = refs
    row_at = lax.broadcasted_iota(jnp.int32, (NX, NX), 0)
    col_at = lax.broadcasted_iota(jnp.int32, (NX, NX), 1)
    flip = (row_at + col_at == NX - 1).astype(jnp.bfloat16)
    left = lax.broadcasted_iota(jnp.int32, (NX, LANES), 1) < QUARTER
    for f in range(GROUP):
        real = jnp.dot(flip, source_ref[f, 0], preferred_element_type=jnp.float32)
        imag = jnp.dot(flip, source_ref[f, 1], preferred_element_type=jnp.float32)
        for half in range(2):
            cols = slice(half * LANES, (half + 1) * LANES)
            a = real[:, cols]
            b = pltpu.roll(imag[:, cols], QUARTER, 1)
            packed[half * 2, f] = jnp.where(left, a, b).astype(jnp.bfloat16)
            packed[half * 2 + 1, f] = jnp.where(left, b, a).astype(jnp.bfloat16)
    mine = quarter_ref[0]
    own_ref[...] = packed[mine]
    core_ref[0] = packed[mine ^ 1]
    core_ref[1] = packed[mine ^ 3]
    chip_ref[0] = packed[mine ^ 2]


def image_kernel(scale, quarter_ref, wave_ref, own_ref, core_ref, chip_ref, out_ref, wave, src, totals):
    sources = [own_ref, core_ref.at[0], chip_ref.at[0], chip_ref.at[1]]
    edge = jnp.zeros((4 * GROUP, REACH, LANES), jnp.float32)
    for ref in (wave, src):
        ref[:, :REACH, :] = edge
        ref[:, REACH + NX :, :] = edge
    for k in range(4):
        group = (quarter_ref[0] ^ k) * GROUP
        for f in range(GROUP):
            wave[k * GROUP + f, REACH : REACH + NX, :] = wave_ref[f * 4 + k].astype(jnp.float32)
            src[group + f, REACH : REACH + NX, :] = sources[k][f].astype(jnp.float32)

    tall, deep = NX // 8, H // 8
    inside = range(1, tall + deep - 2)

    def rows_from(start, carry):
        sums = {}
        for i in range(4 * GROUP):
            waves = {j: wave[i, pl.ds(start + 8 * j, 8), :] for j in inside}
            sources = {j: src[i, pl.ds(7 - start + 8 * j, 8), :] for j in inside}
            for m in range(tall):
                for n in range(deep):
                    j, k = m + n, tall - 1 - m + n
                    if j in inside and k in inside:
                        term = waves[j] * sources[k]
                        sums[m, n] = sums[m, n] + term if i else term
        for m in range(tall):
            for n in range(deep):
                value = sums.get((m, n))
                totals[start + 8 * m, 8 * n : 8 * n + 8, :] = jnp.zeros((8, LANES), jnp.float32) if value is None else value
        return carry

    lax.fori_loop(0, 8, rows_from, 0)
    left = lax.broadcasted_iota(jnp.int32, (REACH, LANES), 1) < QUARTER

    def fold(x, carry):
        total = totals[x]
        total = (total + pltpu.roll(total, QUARTER, 1)) * scale
        out_ref[x] = jnp.where(left, total[:REACH], total[REACH:]).astype(jnp.bfloat16)
        return carry

    lax.fori_loop(0, NX, fold, 0, unroll=8)


def sum_kernel(part_ref, out_ref):
    groups = part_ref.shape[0] // 4
    left = lax.broadcasted_iota(jnp.int32, (REACH, LANES), 1) < QUARTER
    for half in range(2):
        totals = []
        for q in (2 * half, 2 * half + 1):
            total = part_ref[q].astype(jnp.float32)
            for i in range(1, groups):
                total = total + part_ref[4 * i + q].astype(jnp.float32)
            totals.append(total)
        a, b = totals
        cols = slice(half * LANES, (half + 1) * LANES)
        out_ref[0, :REACH, 0, cols] = jnp.where(left, a, pltpu.roll(b, QUARTER, 1))
        out_ref[0, REACH:, 0, cols] = jnp.where(left, pltpu.roll(a, QUARTER, 1), b)


VMEM = pl.BlockSpec(memory_space=pltpu.VMEM)
SMEM = pl.BlockSpec(memory_space=pltpu.SMEM)
PARAMS = pltpu.CompilerParams(vmem_limit_bytes=24 << 20)


def cost(flops, moved):
    return pl.CostEstimate(flops=flops, bytes_accessed=moved, transcendentals=0)


def body(surface, regions, table, source):
    zh = lax.axis_index("zh")
    mine_x = lax.axis_index("x")
    core = lax.axis_index("core")
    blocks = lax.axis_size("zh")
    local, local_source = lax.optimization_barrier((regions[0].astype(jnp.bfloat16), source[0]))
    near = lax.ppermute(local, "zh", [(0, 1)])
    far = lax.ppermute(jnp.stack([local, near]), "zh", [(1, 2)])
    quarter = (lax.axis_index("zp") * 2 + core).astype(jnp.int32).reshape(1)
    four = jax.ShapeDtypeStruct((GROUP, NX, LANES), jnp.bfloat16)
    pair = jax.ShapeDtypeStruct((2, GROUP, NX, LANES), jnp.bfloat16)
    one = jax.ShapeDtypeStruct((1, GROUP, NX, LANES), jnp.bfloat16)
    packed, to_core, to_chip = pl.pallas_call(
        pack_kernel,
        out_shape=(four, pair, one),
        in_specs=[SMEM, VMEM],
        out_specs=(VMEM,) * 3,
        scratch_shapes=[pltpu.VMEM((4, GROUP, NX, LANES), jnp.bfloat16)],
        compiler_params=PARAMS,
        cost_estimate=cost(20_000_000, 1_000_000),
        name="pack",
    )(quarter, local_source)
    column = pl.pallas_call(
        stack_kernel,
        out_shape=jax.ShapeDtypeStruct((blocks, NX, NY), jnp.bfloat16),
        in_specs=[SMEM] + [VMEM] * 3,
        out_specs=VMEM,
        compiler_params=PARAMS,
        cost_estimate=cost(1_000_000, 500_000),
        name="stack",
    )(zh.astype(jnp.int32).reshape(1), local, near, far)
    from_core = lax.ppermute(to_core, "core", [(0, 1), (1, 0)])
    column, from_core, table = lax.optimization_barrier((column, from_core, table))
    from_chip = lax.ppermute(
        jnp.concatenate([to_chip, from_core[1:]], axis=0), "zp", [(0, 1), (1, 0)]
    )
    columns = [column] + [
        lax.ppermute(column, "x", [(i, i ^ k) for i in range(GROUP)]) for k in range(1, GROUP)
    ]

    padded = jnp.pad(table.reshape(GROUP * R * 4, TAPS), ((0, 0), (0, LANES - TAPS)))
    bands = pl.pallas_call(
        bands_kernel,
        out_shape=(
            jax.ShapeDtypeStruct((R * 2 * NX, LANES), jnp.bfloat16),
            jax.ShapeDtypeStruct((2 * LANES, R * LANES), jnp.bfloat16),
            jax.ShapeDtypeStruct((2 * LANES, R * LANES), jnp.bfloat16),
        ),
        in_specs=[SMEM, VMEM],
        out_specs=(VMEM,) * 3,
        compiler_params=PARAMS,
        cost_estimate=cost(10_000_000, 1_000_000),
        name="bands",
    )(mine_x.astype(jnp.int32).reshape(1), padded)

    scalars = jnp.stack([zh + 1, mine_x]).astype(jnp.int32)
    waves = pl.pallas_call(
        chain_kernel,
        out_shape=jax.ShapeDtypeStruct((GROUP * 4, NX, LANES), jnp.bfloat16),
        in_specs=[SMEM] + [VMEM] * (4 + GROUP),
        out_specs=VMEM,
        scratch_shapes=[
            pltpu.VMEM((2 * NX, NY), jnp.bfloat16),
            pltpu.VMEM((GROUP, blocks, NX, NY), jnp.bfloat16),
        ],
        compiler_params=PARAMS,
        cost_estimate=cost(4_000_000_000, 4_000_000),
        name="chain",
    )(scalars, *bands, surface, *columns)

    waves, from_chip = lax.optimization_barrier((waves, from_chip))
    waves = lax.all_to_all(waves, ("x",) + QUAD, 0, 0, tiled=True)

    scale = 1.0 / math.sqrt(surface.shape[0] * lax.axis_size(FREQ))
    partial_image = pl.pallas_call(
        lambda *refs: image_kernel(scale, *refs),
        out_shape=jax.ShapeDtypeStruct((NX, REACH, LANES), jnp.bfloat16),
        in_specs=[SMEM] + [VMEM] * 4,
        out_specs=VMEM,
        scratch_shapes=[pltpu.VMEM((4 * GROUP, NX + H, LANES), jnp.float32)] * 2
        + [pltpu.VMEM((NX, H, LANES), jnp.float32)],
        compiler_params=PARAMS,
        cost_estimate=cost(10_000_000, 2_000_000),
        name="image",
    )(quarter, waves, packed, from_core, from_chip)

    parts = lax.all_to_all(partial_image, FREQ, 0, 0, tiled=True)

    return pl.pallas_call(
        sum_kernel,
        out_shape=jax.ShapeDtypeStruct((1, H, 1, NY), jnp.float32),
        in_specs=[VMEM],
        out_specs=VMEM,
        compiler_params=PARAMS,
        name="total",
    )(parts)


def solution(mesh):
    wide = Mesh(np.asarray(mesh.devices).reshape(3, 4, 8, 2, 2, 2), AXES)
    in_specs = (
        P(FREQ, None, None, None),
        P(DEPTH, None, None),
        P(FREQ, None, None, None, None),
        P(DEPTH, FREQ, None, None, None),
    )
    out_specs = P(DEPTH, None, FREQ, None)
    return jax.shard_map(body, mesh=wide, in_specs=in_specs, out_specs=out_specs, check_vma=False)
```

```python
import math

import jax
import jax.numpy as jnp
import numpy as np
from jax import lax
from jax.experimental import pallas as pl
from jax.experimental.pallas import tpu as pltpu
from jax.sharding import Mesh
from jax.sharding import PartitionSpec as P

H = 32
REACH = H // 2
NX = 64
NY = 256
LANES = 128
QUARTER = 64
R = 4
TAPS = 25
MID = TAPS // 2
GROUP = 4

AXES = ("zh", "x", "y", "zq", "zp", "core")
DEPTH = ("zh", "x")
FREQ = ("y", "zq", "zp", "core")
QUAD = ("zp", "core")


def onehot(shape, fit, value=1.0):
    row_at = lax.broadcasted_iota(jnp.int32, shape, 0)
    col_at = lax.broadcasted_iota(jnp.int32, shape, 1)
    return jnp.where(fit(row_at, col_at), value, 0.0).astype(jnp.bfloat16)


def exact(a, b):
    return jnp.dot(a, b, preferred_element_type=jnp.float32)


def tap_rows(taps):
    many = R * 2

    def row(pass_at, part):
        return lambda i, j: j == (i >> 1) * 4 + pass_at * 2 + part(i & 1)

    def lanes(shift, sign=1):
        return onehot((LANES, LANES), lambda k, n: k == ((sign * n + shift) & (LANES - 1)))

    def chosen(fit):
        return exact(fit, taps).astype(jnp.bfloat16)

    shape = (many, 2 * many)
    straight = chosen(onehot(shape, row(0, lambda p: p)))
    row_at = lax.broadcasted_iota(jnp.int32, (many, LANES), 0)
    crossed = exact(chosen(onehot(shape, row(0, lambda p: 1 - p))), lanes(-(QUARTER - MID)))
    crossed = jnp.where((row_at & 1) == 0, -crossed, crossed)
    rows_first = exact(straight, lanes(MID)) + crossed
    rows_second = exact(chosen(onehot(shape, row(1, lambda p: p))), lanes(MID, -1))
    return rows_first, rows_second


def fan(row, height, shift):
    wide = jnp.broadcast_to(row, (height, row.shape[-1]))
    return pltpu.roll(wide, shift, 1, stride=1, stride_axis=0)


def bands_kernel(index_ref, table_ref, band_first, band_even, band_odd):
    taps = table_ref[pl.ds(pl.multiple_of(index_ref[0] * 16, 16), 16), :]
    rows_first, rows_second = tap_rows(taps)
    row_at = lax.broadcasted_iota(jnp.int32, (NX, LANES), 0)
    lane_at = lax.broadcasted_iota(jnp.int32, (NX, LANES), 1)
    near = jnp.abs((lane_at & (NX - 1)) - row_at) <= MID
    for block in range(R * 2):
        band = fan(rows_first[block : block + 1, :], NX, 0)
        band_first[block * NX : (block + 1) * NX, :] = jnp.where(near, band, 0.0).astype(jnp.bfloat16)

    left = lax.broadcasted_iota(jnp.int32, (LANES, LANES), 1) < QUARTER
    for region in range(R):
        tap_real = rows_second[2 * region : 2 * region + 1, :]
        tap_imag = rows_second[2 * region + 1 : 2 * region + 2, :]
        cols = slice(region * LANES, (region + 1) * LANES)
        for part, (to_real, to_imag) in enumerate(((tap_real, tap_imag), (-tap_imag, tap_real))):
            rows = slice(part * LANES, (part + 1) * LANES)
            real_band = fan(to_real, LANES, 0)
            imag_band = fan(to_imag, LANES, QUARTER)
            band_even[rows, cols] = jnp.where(left, real_band, imag_band).astype(jnp.bfloat16)
            band_odd[rows, cols] = jnp.where(left, imag_band, real_band).astype(jnp.bfloat16)


def pick(masks, values):
    out = values[R - 1]
    for region in range(R - 2, -1, -1):
        out = jnp.where(masks[region], values[region], out)
    return out


def chain_kernel(turn_ref, band_first, band_even, band_odd, entering_ref, regions_ref, *refs):
    out_ref, state = refs[-2:]
    active = turn_ref[0] == 1

    @pl.when(active)
    def _():
        run_steps(band_first, band_even, band_odd, entering_ref, regions_ref, out_ref, state)

    @pl.when(jnp.logical_not(active))
    def _():
        out_ref[...] = refs[0][...] if len(refs) == 3 else jnp.zeros_like(out_ref)
        state[...] = jnp.zeros_like(state)


def run_steps(band_first, band_even, band_odd, entering_ref, regions_ref, out_ref, state):
    state[...] = entering_ref[...]
    lane = lax.broadcasted_iota(jnp.int32, (NX, LANES), 1)
    left = lane < QUARTER
    low = lane < 96
    high = lane >= 32

    def split(values):
        return [values == float(r) for r in range(R - 1)]

    for slot in range(GROUP):
        region = regions_ref[slot].astype(jnp.float32)
        halves = [region[:, :LANES], region[:, LANES:]]
        turned = [pltpu.roll(half, QUARTER, 1) for half in halves]
        full = split(region)
        even_mask = split(jnp.concatenate([jnp.where(left, a, b) for a, b in zip(halves, turned)], axis=0))
        odd_mask = split(jnp.concatenate([jnp.where(left, b, a) for a, b in zip(halves, turned)], axis=0))

        field = [
            jnp.dot(band_first[rows], state[...], preferred_element_type=jnp.float32)
            for rows in (slice(0, 4 * NX), slice(4 * NX, 8 * NX))
        ]
        field = jnp.concatenate(field, axis=0)
        even_in, odd_in = [], []
        for part in range(2):
            values = [field[(r * 2 + part) * NX : (r * 2 + part + 1) * NX] for r in range(R)]
            between = pick(full, values)
            a, b = between[:, :LANES], between[:, LANES:]
            even_in.append(jnp.concatenate([jnp.where(low, a, 0.0), jnp.where(low, b, a)], axis=0).astype(jnp.bfloat16))
            odd_in.append(jnp.concatenate([jnp.where(high, a, b), jnp.where(high, b, 0.0)], axis=0).astype(jnp.bfloat16))
        wide = jnp.dot(jnp.concatenate(even_in, axis=1), band_even[...], preferred_element_type=jnp.float32)
        even = pick(even_mask, [wide[:, r * LANES : (r + 1) * LANES] for r in range(R)])
        wide = jnp.dot(jnp.concatenate(odd_in, axis=1), band_odd[...], preferred_element_type=jnp.float32)
        odd = pick(odd_mask, [wide[:, r * LANES : (r + 1) * LANES] for r in range(R)])
        for half in range(2):
            rows = slice(half * NX, (half + 1) * NX)
            cols = slice(half * LANES, (half + 1) * LANES)
            e, o = even[rows], odd[rows]
            out_ref[slot * 4 + half * 2] = e.astype(jnp.bfloat16)
            out_ref[slot * 4 + half * 2 + 1] = o.astype(jnp.bfloat16)
            state[:NX, cols] = jnp.where(left, e, o).astype(jnp.bfloat16)
            state[NX:, cols] = pltpu.roll(jnp.where(left, o, e), QUARTER, 1).astype(jnp.bfloat16)


def pack_kernel(quarter_ref, source_ref, *refs):
    own_ref, core_ref, chip_ref, packed = refs
    row_at = lax.broadcasted_iota(jnp.int32, (NX, NX), 0)
    col_at = lax.broadcasted_iota(jnp.int32, (NX, NX), 1)
    flip = (row_at + col_at == NX - 1).astype(jnp.bfloat16)
    left = lax.broadcasted_iota(jnp.int32, (NX, LANES), 1) < QUARTER
    for f in range(GROUP):
        real = jnp.dot(flip, source_ref[f, 0], preferred_element_type=jnp.float32)
        imag = jnp.dot(flip, source_ref[f, 1], preferred_element_type=jnp.float32)
        for half in range(2):
            cols = slice(half * LANES, (half + 1) * LANES)
            a = real[:, cols]
            b = pltpu.roll(imag[:, cols], QUARTER, 1)
            packed[half * 2, f] = jnp.where(left, a, b).astype(jnp.bfloat16)
            packed[half * 2 + 1, f] = jnp.where(left, b, a).astype(jnp.bfloat16)
    mine = quarter_ref[0]
    own_ref[...] = packed[mine]
    core_ref[0] = packed[mine ^ 1]
    core_ref[1] = packed[mine ^ 3]
    chip_ref[0] = packed[mine ^ 2]


def image_kernel(scale, quarter_ref, wave_ref, own_ref, core_ref, chip_ref, out_ref, wave, src, totals):
    sources = [own_ref, core_ref.at[0], chip_ref.at[0], chip_ref.at[1]]
    edge = jnp.zeros((4 * GROUP, REACH, LANES), jnp.float32)
    for ref in (wave, src):
        ref[:, :REACH, :] = edge
        ref[:, REACH + NX :, :] = edge
    for k in range(4):
        group = (quarter_ref[0] ^ k) * GROUP
        for f in range(GROUP):
            wave[k * GROUP + f, REACH : REACH + NX, :] = wave_ref[f * 4 + k].astype(jnp.float32)
            src[group + f, REACH : REACH + NX, :] = sources[k][f].astype(jnp.float32)

    tall, deep = NX // 8, H // 8
    inside = range(1, tall + deep - 2)

    def rows_from(start, carry):
        sums = {}
        for i in range(4 * GROUP):
            waves = {j: wave[i, pl.ds(start + 8 * j, 8), :] for j in inside}
            sources = {j: src[i, pl.ds(7 - start + 8 * j, 8), :] for j in inside}
            for m in range(tall):
                for n in range(deep):
                    j, k = m + n, tall - 1 - m + n
                    if j in inside and k in inside:
                        term = waves[j] * sources[k]
                        sums[m, n] = sums[m, n] + term if i else term
        for m in range(tall):
            for n in range(deep):
                value = sums.get((m, n))
                totals[start + 8 * m, 8 * n : 8 * n + 8, :] = jnp.zeros((8, LANES), jnp.float32) if value is None else value
        return carry

    lax.fori_loop(0, 8, rows_from, 0)
    left = lax.broadcasted_iota(jnp.int32, (REACH, LANES), 1) < QUARTER

    def fold(x, carry):
        total = totals[x]
        total = (total + pltpu.roll(total, QUARTER, 1)) * scale
        out_ref[x] = jnp.where(left, total[:REACH], total[REACH:]).astype(jnp.bfloat16)
        return carry

    lax.fori_loop(0, NX, fold, 0, unroll=8)


def sum_kernel(part_ref, out_ref):
    groups = part_ref.shape[0] // 4
    left = lax.broadcasted_iota(jnp.int32, (REACH, LANES), 1) < QUARTER
    for half in range(2):
        totals = []
        for q in (2 * half, 2 * half + 1):
            total = part_ref[q].astype(jnp.float32)
            for i in range(1, groups):
                total = total + part_ref[4 * i + q].astype(jnp.float32)
            totals.append(total)
        a, b = totals
        cols = slice(half * LANES, (half + 1) * LANES)
        out_ref[0, :REACH, 0, cols] = jnp.where(left, a, pltpu.roll(b, QUARTER, 1))
        out_ref[0, REACH:, 0, cols] = jnp.where(left, pltpu.roll(a, QUARTER, 1), b)


VMEM = pl.BlockSpec(memory_space=pltpu.VMEM)
SMEM = pl.BlockSpec(memory_space=pltpu.SMEM)
PARAMS = pltpu.CompilerParams(vmem_limit_bytes=24 << 20)


def cost(flops, moved):
    return pl.CostEstimate(flops=flops, bytes_accessed=moved, transcendentals=0)


def body(surface, regions, table, source):
    zh = lax.axis_index("zh")
    mine_x = lax.axis_index("x")
    core = lax.axis_index("core")
    blocks = lax.axis_size("zh")
    local = regions[0].astype(jnp.bfloat16)
    copies = jnp.broadcast_to(local[None], (GROUP, NX, NY))
    copies, local_source, table = lax.optimization_barrier((copies, source[0], table))
    all_regions = lax.all_to_all(copies, "x", 0, 0, tiled=True)
    quarter = (lax.axis_index("zp") * 2 + core).astype(jnp.int32).reshape(1)
    four = jax.ShapeDtypeStruct((GROUP, NX, LANES), jnp.bfloat16)
    pair = jax.ShapeDtypeStruct((2, GROUP, NX, LANES), jnp.bfloat16)
    one = jax.ShapeDtypeStruct((1, GROUP, NX, LANES), jnp.bfloat16)
    packed, to_core, to_chip = pl.pallas_call(
        pack_kernel,
        out_shape=(four, pair, one),
        in_specs=[SMEM, VMEM],
        out_specs=(VMEM,) * 3,
        scratch_shapes=[pltpu.VMEM((4, GROUP, NX, LANES), jnp.bfloat16)],
        compiler_params=PARAMS,
        cost_estimate=cost(20_000_000, 1_000_000),
        name="pack",
    )(quarter, local_source)
    from_core = lax.ppermute(to_core, "core", [(0, 1), (1, 0)])
    from_chip = lax.ppermute(
        jnp.concatenate([to_chip, from_core[1:]], axis=0), "zp", [(0, 1), (1, 0)]
    )

    padded = jnp.pad(table.reshape(GROUP * R * 4, TAPS), ((0, 0), (0, LANES - TAPS)))
    bands = pl.pallas_call(
        bands_kernel,
        out_shape=(
            jax.ShapeDtypeStruct((R * 2 * NX, LANES), jnp.bfloat16),
            jax.ShapeDtypeStruct((2 * LANES, R * LANES), jnp.bfloat16),
            jax.ShapeDtypeStruct((2 * LANES, R * LANES), jnp.bfloat16),
        ),
        in_specs=[SMEM, VMEM],
        out_specs=(VMEM,) * 3,
        compiler_params=PARAMS,
        cost_estimate=cost(10_000_000, 1_000_000),
        name="bands",
    )(mine_x.astype(jnp.int32).reshape(1), padded)

    entering = lax.dynamic_index_in_dim(surface, mine_x, 0, keepdims=False).reshape(2 * NX, NY)
    before = ()
    for block in range(blocks):
        waves, leaving = pl.pallas_call(
            chain_kernel,
            out_shape=(
                jax.ShapeDtypeStruct((GROUP * 4, NX, LANES), jnp.bfloat16),
                jax.ShapeDtypeStruct((2 * NX, NY), jnp.bfloat16),
            ),
            in_specs=[SMEM] + [VMEM] * (5 + len(before)),
            out_specs=(VMEM,) * 2,
            compiler_params=PARAMS,
            cost_estimate=cost(300_000_000, 4_000_000),
            name="chain",
        )((zh == block).astype(jnp.int32).reshape(1), *bands, entering, all_regions, *before)
        before = (waves,)
        if block + 1 < blocks:
            entering = lax.ppermute(leaving, "zh", [(block, block + 1)])

    waves, from_chip = lax.optimization_barrier((waves, from_chip))
    waves = lax.all_to_all(waves, ("x",) + QUAD, 0, 0, tiled=True)

    scale = 1.0 / math.sqrt(surface.shape[0] * lax.axis_size(FREQ))
    partial_image = pl.pallas_call(
        lambda *refs: image_kernel(scale, *refs),
        out_shape=jax.ShapeDtypeStruct((NX, REACH, LANES), jnp.bfloat16),
        in_specs=[SMEM] + [VMEM] * 4,
        out_specs=VMEM,
        scratch_shapes=[pltpu.VMEM((4 * GROUP, NX + H, LANES), jnp.float32)] * 2
        + [pltpu.VMEM((NX, H, LANES), jnp.float32)],
        compiler_params=PARAMS,
        cost_estimate=cost(10_000_000, 2_000_000),
        name="image",
    )(quarter, waves, packed, from_core, from_chip)

    parts = lax.all_to_all(partial_image, FREQ, 0, 0, tiled=True)

    return pl.pallas_call(
        sum_kernel,
        out_shape=jax.ShapeDtypeStruct((1, H, 1, NY), jnp.float32),
        in_specs=[VMEM],
        out_specs=VMEM,
        compiler_params=PARAMS,
        name="total",
    )(parts)


def solution(mesh):
    wide = Mesh(np.asarray(mesh.devices).reshape(3, 4, 8, 2, 2, 2), AXES)
    in_specs = (
        P(FREQ, None, None, None),
        P(DEPTH, None, None),
        P(FREQ, None, None, None, None),
        P(DEPTH, FREQ, None, None, None),
    )
    out_specs = P(DEPTH, None, FREQ, None)
    return jax.shard_map(body, mesh=wide, in_specs=in_specs, out_specs=out_specs, check_vma=False)
```

```python
import math

import jax
import jax.numpy as jnp
import numpy as np
from jax import lax
from jax.experimental import pallas as pl
from jax.experimental.pallas import tpu as pltpu
from jax.sharding import Mesh
from jax.sharding import PartitionSpec as P

H = 32
REACH = H // 2
NX = 64
NY = 256
LANES = 128
QUARTER = 64
R = 4
TAPS = 25
MID = TAPS // 2
GROUP = 4

AXES = ("zh", "x", "yq", "yp", "zl", "core")
DEPTH = ("zh", "x")
FREQ = ("yq", "yp", "zl", "core")
QUAD = ("yp", "core")


def onehot(shape, fit, value=1.0):
    row_at = lax.broadcasted_iota(jnp.int32, shape, 0)
    col_at = lax.broadcasted_iota(jnp.int32, shape, 1)
    return jnp.where(fit(row_at, col_at), value, 0.0).astype(jnp.bfloat16)


def exact(a, b):
    return jnp.dot(a, b, preferred_element_type=jnp.float32)


def tap_rows(taps):
    many = R * 2

    def row(pass_at, part):
        return lambda i, j: j == (i >> 1) * 4 + pass_at * 2 + part(i & 1)

    def lanes(shift, sign=1):
        return onehot((LANES, LANES), lambda k, n: k == ((sign * n + shift) & (LANES - 1)))

    def chosen(fit):
        return exact(fit, taps).astype(jnp.bfloat16)

    shape = (many, 2 * many)
    straight = chosen(onehot(shape, row(0, lambda p: p)))
    row_at = lax.broadcasted_iota(jnp.int32, (many, LANES), 0)
    crossed = exact(chosen(onehot(shape, row(0, lambda p: 1 - p))), lanes(-(QUARTER - MID)))
    crossed = jnp.where((row_at & 1) == 0, -crossed, crossed)
    rows_first = exact(straight, lanes(MID)) + crossed
    rows_second = exact(chosen(onehot(shape, row(1, lambda p: p))), lanes(MID, -1))
    return rows_first, rows_second


def fan(row, height, shift):
    wide = jnp.broadcast_to(row, (height, row.shape[-1]))
    return pltpu.roll(wide, shift, 1, stride=1, stride_axis=0)


def bands_kernel(index_ref, table_ref, band_first, band_even, band_odd):
    taps = table_ref[pl.ds(pl.multiple_of(index_ref[0] * 16, 16), 16), :]
    rows_first, rows_second = tap_rows(taps)
    row_at = lax.broadcasted_iota(jnp.int32, (NX, LANES), 0)
    lane_at = lax.broadcasted_iota(jnp.int32, (NX, LANES), 1)
    near = jnp.abs((lane_at & (NX - 1)) - row_at) <= MID
    for block in range(R * 2):
        band = fan(rows_first[block : block + 1, :], NX, 0)
        band_first[block * NX : (block + 1) * NX, :] = jnp.where(near, band, 0.0).astype(jnp.bfloat16)

    left = lax.broadcasted_iota(jnp.int32, (LANES, LANES), 1) < QUARTER
    for region in range(R):
        tap_real = rows_second[2 * region : 2 * region + 1, :]
        tap_imag = rows_second[2 * region + 1 : 2 * region + 2, :]
        cols = slice(region * LANES, (region + 1) * LANES)
        for part, (to_real, to_imag) in enumerate(((tap_real, tap_imag), (-tap_imag, tap_real))):
            rows = slice(part * LANES, (part + 1) * LANES)
            real_band = fan(to_real, LANES, 0)
            imag_band = fan(to_imag, LANES, QUARTER)
            band_even[rows, cols] = jnp.where(left, real_band, imag_band).astype(jnp.bfloat16)
            band_odd[rows, cols] = jnp.where(left, imag_band, real_band).astype(jnp.bfloat16)


def pick(masks, values):
    out = values[R - 1]
    for region in range(R - 2, -1, -1):
        out = jnp.where(masks[region], values[region], out)
    return out


def chain_kernel(turn_ref, band_first, band_even, band_odd, entering_ref, regions_ref, *refs):
    out_ref, state = refs[-2:]
    active = turn_ref[0] == 1

    @pl.when(active)
    def _():
        run_steps(band_first, band_even, band_odd, entering_ref, regions_ref, out_ref, state)

    @pl.when(jnp.logical_not(active))
    def _():
        out_ref[...] = refs[0][...] if len(refs) == 3 else jnp.zeros_like(out_ref)
        state[...] = jnp.zeros_like(state)


def run_steps(band_first, band_even, band_odd, entering_ref, regions_ref, out_ref, state):
    state[...] = entering_ref[...]
    lane = lax.broadcasted_iota(jnp.int32, (NX, LANES), 1)
    left = lane < QUARTER
    low = lane < 96
    high = lane >= 32

    def split(values):
        return [values == float(r) for r in range(R - 1)]

    for slot in range(GROUP):
        region = regions_ref[slot].astype(jnp.float32)
        halves = [region[:, :LANES], region[:, LANES:]]
        turned = [pltpu.roll(half, QUARTER, 1) for half in halves]
        full = split(region)
        even_mask = split(jnp.concatenate([jnp.where(left, a, b) for a, b in zip(halves, turned)], axis=0))
        odd_mask = split(jnp.concatenate([jnp.where(left, b, a) for a, b in zip(halves, turned)], axis=0))

        field = [
            jnp.dot(band_first[rows], state[...], preferred_element_type=jnp.float32)
            for rows in (slice(0, 4 * NX), slice(4 * NX, 8 * NX))
        ]
        field = jnp.concatenate(field, axis=0)
        even_in, odd_in = [], []
        for part in range(2):
            values = [field[(r * 2 + part) * NX : (r * 2 + part + 1) * NX] for r in range(R)]
            between = pick(full, values)
            a, b = between[:, :LANES], between[:, LANES:]
            even_in.append(jnp.concatenate([jnp.where(low, a, 0.0), jnp.where(low, b, a)], axis=0).astype(jnp.bfloat16))
            odd_in.append(jnp.concatenate([jnp.where(high, a, b), jnp.where(high, b, 0.0)], axis=0).astype(jnp.bfloat16))
        wide = jnp.dot(jnp.concatenate(even_in, axis=1), band_even[...], preferred_element_type=jnp.float32)
        even = pick(even_mask, [wide[:, r * LANES : (r + 1) * LANES] for r in range(R)])
        wide = jnp.dot(jnp.concatenate(odd_in, axis=1), band_odd[...], preferred_element_type=jnp.float32)
        odd = pick(odd_mask, [wide[:, r * LANES : (r + 1) * LANES] for r in range(R)])
        for half in range(2):
            rows = slice(half * NX, (half + 1) * NX)
            cols = slice(half * LANES, (half + 1) * LANES)
            e, o = even[rows], odd[rows]
            out_ref[slot * 4 + half * 2] = e.astype(jnp.bfloat16)
            out_ref[slot * 4 + half * 2 + 1] = o.astype(jnp.bfloat16)
            state[:NX, cols] = jnp.where(left, e, o).astype(jnp.bfloat16)
            state[NX:, cols] = pltpu.roll(jnp.where(left, o, e), QUARTER, 1).astype(jnp.bfloat16)


def pack_kernel(quarter_ref, source_ref, *refs):
    own_ref, core_ref, chip_ref, packed = refs
    row_at = lax.broadcasted_iota(jnp.int32, (NX, NX), 0)
    col_at = lax.broadcasted_iota(jnp.int32, (NX, NX), 1)
    flip = (row_at + col_at == NX - 1).astype(jnp.bfloat16)
    left = lax.broadcasted_iota(jnp.int32, (NX, LANES), 1) < QUARTER
    for f in range(GROUP):
        real = jnp.dot(flip, source_ref[f, 0], preferred_element_type=jnp.float32)
        imag = jnp.dot(flip, source_ref[f, 1], preferred_element_type=jnp.float32)
        for half in range(2):
            cols = slice(half * LANES, (half + 1) * LANES)
            a = real[:, cols]
            b = pltpu.roll(imag[:, cols], QUARTER, 1)
            packed[half * 2, f] = jnp.where(left, a, b).astype(jnp.bfloat16)
            packed[half * 2 + 1, f] = jnp.where(left, b, a).astype(jnp.bfloat16)
    mine = quarter_ref[0]
    own_ref[...] = packed[mine]
    core_ref[0] = packed[mine ^ 1]
    core_ref[1] = packed[mine ^ 3]
    chip_ref[0] = packed[mine ^ 2]


def image_kernel(scale, quarter_ref, wave_ref, own_ref, core_ref, chip_ref, out_ref, wave, src, totals):
    sources = [own_ref, core_ref.at[0], chip_ref.at[0], chip_ref.at[1]]
    edge = jnp.zeros((4 * GROUP, REACH, LANES), jnp.float32)
    for ref in (wave, src):
        ref[:, :REACH, :] = edge
        ref[:, REACH + NX :, :] = edge
    for k in range(4):
        group = (quarter_ref[0] ^ k) * GROUP
        for f in range(GROUP):
            wave[k * GROUP + f, REACH : REACH + NX, :] = wave_ref[f * 4 + k].astype(jnp.float32)
            src[group + f, REACH : REACH + NX, :] = sources[k][f].astype(jnp.float32)

    tall, deep = NX // 8, H // 8
    inside = range(1, tall + deep - 2)

    def rows_from(start, carry):
        sums = {}
        for i in range(4 * GROUP):
            waves = {j: wave[i, pl.ds(start + 8 * j, 8), :] for j in inside}
            sources = {j: src[i, pl.ds(7 - start + 8 * j, 8), :] for j in inside}
            for m in range(tall):
                for n in range(deep):
                    j, k = m + n, tall - 1 - m + n
                    if j in inside and k in inside:
                        term = waves[j] * sources[k]
                        sums[m, n] = sums[m, n] + term if i else term
        for m in range(tall):
            for n in range(deep):
                value = sums.get((m, n))
                totals[start + 8 * m, 8 * n : 8 * n + 8, :] = jnp.zeros((8, LANES), jnp.float32) if value is None else value
        return carry

    lax.fori_loop(0, 8, rows_from, 0)
    left = lax.broadcasted_iota(jnp.int32, (REACH, LANES), 1) < QUARTER

    def fold(x, carry):
        total = totals[x]
        total = (total + pltpu.roll(total, QUARTER, 1)) * scale
        out_ref[x] = jnp.where(left, total[:REACH], total[REACH:]).astype(jnp.bfloat16)
        return carry

    lax.fori_loop(0, NX, fold, 0, unroll=8)


def sum_kernel(part_ref, out_ref):
    many, line = part_ref.shape[0], 8
    left = lax.broadcasted_iota(jnp.int32, (REACH, LANES), 1) < QUARTER
    for half in range(2):
        totals = []
        for q in (2 * half, 2 * half + 1):
            pair, core = divmod(q, 2)
            total = jnp.zeros((REACH, LANES), jnp.float32)
            for start in range(pair * line, many, 2 * line):
                for i in range(start + core, start + line, 2):
                    total = total + part_ref[i].astype(jnp.float32)
            totals.append(total)
        a, b = totals
        cols = slice(half * LANES, (half + 1) * LANES)
        out_ref[0, :REACH, 0, cols] = jnp.where(left, a, pltpu.roll(b, QUARTER, 1))
        out_ref[0, REACH:, 0, cols] = jnp.where(left, pltpu.roll(a, QUARTER, 1), b)


VMEM = pl.BlockSpec(memory_space=pltpu.VMEM)
SMEM = pl.BlockSpec(memory_space=pltpu.SMEM)
PARAMS = pltpu.CompilerParams(vmem_limit_bytes=24 << 20)


def cost(flops, moved):
    return pl.CostEstimate(flops=flops, bytes_accessed=moved, transcendentals=0)


def body(surface, regions, table, source):
    zh = lax.axis_index("zh")
    mine_x = lax.axis_index("x")
    core = lax.axis_index("core")
    blocks = lax.axis_size("zh")
    local = regions[0].astype(jnp.bfloat16)
    copies = jnp.broadcast_to(local[None], (GROUP, NX, NY))
    copies, local_source, table = lax.optimization_barrier((copies, source[0], table))
    all_regions = lax.all_to_all(copies, "x", 0, 0, tiled=True)
    quarter = (lax.axis_index("yp") * 2 + core).astype(jnp.int32).reshape(1)
    four = jax.ShapeDtypeStruct((GROUP, NX, LANES), jnp.bfloat16)
    pair = jax.ShapeDtypeStruct((2, GROUP, NX, LANES), jnp.bfloat16)
    one = jax.ShapeDtypeStruct((1, GROUP, NX, LANES), jnp.bfloat16)
    packed, to_core, to_chip = pl.pallas_call(
        pack_kernel,
        out_shape=(four, pair, one),
        in_specs=[SMEM, VMEM],
        out_specs=(VMEM,) * 3,
        scratch_shapes=[pltpu.VMEM((4, GROUP, NX, LANES), jnp.bfloat16)],
        compiler_params=PARAMS,
        cost_estimate=cost(20_000_000, 1_000_000),
        name="pack",
    )(quarter, local_source)
    from_core = lax.ppermute(to_core, "core", [(0, 1), (1, 0)])
    from_chip = lax.ppermute(
        jnp.concatenate([to_chip, from_core[1:]], axis=0), "yp", [(0, 1), (1, 0)]
    )

    padded = jnp.pad(table.reshape(GROUP * R * 4, TAPS), ((0, 0), (0, LANES - TAPS)))
    bands = pl.pallas_call(
        bands_kernel,
        out_shape=(
            jax.ShapeDtypeStruct((R * 2 * NX, LANES), jnp.bfloat16),
            jax.ShapeDtypeStruct((2 * LANES, R * LANES), jnp.bfloat16),
            jax.ShapeDtypeStruct((2 * LANES, R * LANES), jnp.bfloat16),
        ),
        in_specs=[SMEM, VMEM],
        out_specs=(VMEM,) * 3,
        compiler_params=PARAMS,
        cost_estimate=cost(10_000_000, 1_000_000),
        name="bands",
    )(mine_x.astype(jnp.int32).reshape(1), padded)

    entering = lax.dynamic_index_in_dim(surface, mine_x, 0, keepdims=False).reshape(2 * NX, NY)
    before = ()
    for block in range(blocks):
        waves, leaving = pl.pallas_call(
            chain_kernel,
            out_shape=(
                jax.ShapeDtypeStruct((GROUP * 4, NX, LANES), jnp.bfloat16),
                jax.ShapeDtypeStruct((2 * NX, NY), jnp.bfloat16),
            ),
            in_specs=[SMEM] + [VMEM] * (5 + len(before)),
            out_specs=(VMEM,) * 2,
            compiler_params=PARAMS,
            cost_estimate=cost(300_000_000, 4_000_000),
            name="chain",
        )((zh == block).astype(jnp.int32).reshape(1), *bands, entering, all_regions, *before)
        before = (waves,)
        if block + 1 < blocks:
            entering = lax.ppermute(leaving, "zh", [(block, block + 1)])

    waves, from_chip = lax.optimization_barrier((waves, from_chip))
    waves = lax.all_to_all(waves, ("x",) + QUAD, 0, 0, tiled=True)

    scale = 1.0 / math.sqrt(surface.shape[0] * lax.axis_size(FREQ))
    partial_image = pl.pallas_call(
        lambda *refs: image_kernel(scale, *refs),
        out_shape=jax.ShapeDtypeStruct((NX, REACH, LANES), jnp.bfloat16),
        in_specs=[SMEM] + [VMEM] * 4,
        out_specs=VMEM,
        scratch_shapes=[pltpu.VMEM((4 * GROUP, NX + H, LANES), jnp.float32)] * 2
        + [pltpu.VMEM((NX, H, LANES), jnp.float32)],
        compiler_params=PARAMS,
        cost_estimate=cost(10_000_000, 2_000_000),
        name="image",
    )(quarter, waves, packed, from_core, from_chip)

    parts = lax.all_to_all(partial_image, FREQ, 0, 0, tiled=True)

    return pl.pallas_call(
        sum_kernel,
        out_shape=jax.ShapeDtypeStruct((1, H, 1, NY), jnp.float32),
        in_specs=[VMEM],
        out_specs=VMEM,
        compiler_params=PARAMS,
        name="total",
    )(parts)


def solution(mesh):
    wide = Mesh(np.asarray(mesh.devices).reshape(3, 4, 4, 2, 4, 2), AXES)
    in_specs = (
        P(FREQ, None, None, None),
        P(DEPTH, None, None),
        P(FREQ, None, None, None, None),
        P(DEPTH, FREQ, None, None, None),
    )
    out_specs = P(DEPTH, None, FREQ, None)
    return jax.shard_map(body, mesh=wide, in_specs=in_specs, out_specs=out_specs, check_vma=False)
```

```python
import functools
import math

import jax
import jax.numpy as jnp
import numpy as np
from jax import lax
from jax.experimental import pallas as pl
from jax.experimental.pallas import tpu as pltpu
from jax.sharding import Mesh
from jax.sharding import PartitionSpec as P

H = 32
REACH = H // 2
NX = 64
NY = 256
LANES = 128
QUARTER = 64
R = 4
TAPS = 25
MID = TAPS // 2
GROUP = 4

AXES = ("zh", "x", "yq", "yp", "zl", "core")
DEPTH = ("zh", "x")
FREQ = ("yq", "yp", "zl", "core")
QUAD = ("yp", "core")


def onehot(shape, fit, value=1.0):
    row_at = lax.broadcasted_iota(jnp.int32, shape, 0)
    col_at = lax.broadcasted_iota(jnp.int32, shape, 1)
    return jnp.where(fit(row_at, col_at), value, 0.0).astype(jnp.bfloat16)


def exact(a, b):
    return jnp.dot(a, b, preferred_element_type=jnp.float32)


def tap_rows(taps):
    many = R * 2

    def row(pass_at, part):
        return lambda i, j: j == (i >> 1) * 4 + pass_at * 2 + part(i & 1)

    def lanes(shift, sign=1):
        return onehot((LANES, LANES), lambda k, n: k == ((sign * n + shift) & (LANES - 1)))

    def chosen(fit):
        return exact(fit, taps).astype(jnp.bfloat16)

    shape = (many, 2 * many)
    straight = chosen(onehot(shape, row(0, lambda p: p)))
    row_at = lax.broadcasted_iota(jnp.int32, (many, LANES), 0)
    crossed = exact(chosen(onehot(shape, row(0, lambda p: 1 - p))), lanes(-(QUARTER - MID)))
    crossed = jnp.where((row_at & 1) == 0, -crossed, crossed)
    rows_first = exact(straight, lanes(MID)) + crossed
    rows_second = exact(chosen(onehot(shape, row(1, lambda p: p))), lanes(MID, -1))
    return rows_first, rows_second


def fan(row, height, shift):
    wide = jnp.broadcast_to(row, (height, row.shape[-1]))
    return pltpu.roll(wide, shift, 1, stride=1, stride_axis=0)


def bands_kernel(index_ref, table_ref, band_first, band_even, band_odd):
    taps = table_ref[pl.ds(pl.multiple_of(index_ref[0] * 16, 16), 16), :]
    rows_first, rows_second = tap_rows(taps)
    row_at = lax.broadcasted_iota(jnp.int32, (NX, LANES), 0)
    lane_at = lax.broadcasted_iota(jnp.int32, (NX, LANES), 1)
    near = jnp.abs((lane_at & (NX - 1)) - row_at) <= MID
    for block in range(R * 2):
        band = fan(rows_first[block : block + 1, :], NX, 0)
        band_first[block * NX : (block + 1) * NX, :] = jnp.where(near, band, 0.0).astype(jnp.bfloat16)

    left = lax.broadcasted_iota(jnp.int32, (LANES, LANES), 1) < QUARTER
    for region in range(R):
        tap_real = rows_second[2 * region : 2 * region + 1, :]
        tap_imag = rows_second[2 * region + 1 : 2 * region + 2, :]
        cols = slice(region * LANES, (region + 1) * LANES)
        for part, (to_real, to_imag) in enumerate(((tap_real, tap_imag), (-tap_imag, tap_real))):
            rows = slice(part * LANES, (part + 1) * LANES)
            real_band = fan(to_real, LANES, 0)
            imag_band = fan(to_imag, LANES, QUARTER)
            band_even[rows, cols] = jnp.where(left, real_band, imag_band).astype(jnp.bfloat16)
            band_odd[rows, cols] = jnp.where(left, imag_band, real_band).astype(jnp.bfloat16)


def pick(masks, values):
    out = values[R - 1]
    for region in range(R - 2, -1, -1):
        out = jnp.where(masks[region], values[region], out)
    return out


def chain_kernel(first, turn_ref, index_ref, band_first, band_even, band_odd, entering_ref, *refs):
    columns, (out_ref, state, regions_ref) = refs[:GROUP], refs[-3:]
    active = turn_ref[0] == 1

    @pl.when(active)
    def _():
        for k in range(GROUP):
            regions_ref[index_ref[0] ^ k] = columns[k][...]
        run_steps(band_first, band_even, band_odd, entering_ref, regions_ref, out_ref, state)

    @pl.when(jnp.logical_not(active))
    def _():
        out_ref[...] = jnp.zeros_like(out_ref) if first else refs[GROUP][...]
        state[...] = jnp.zeros_like(state)


def run_steps(band_first, band_even, band_odd, entering_ref, regions_ref, out_ref, state):
    state[...] = entering_ref[...]
    lane = lax.broadcasted_iota(jnp.int32, (NX, LANES), 1)
    left = lane < QUARTER
    low = lane < 96
    high = lane >= 32

    def split(values):
        return [values == float(r) for r in range(R - 1)]

    for slot in range(GROUP):
        region = regions_ref[slot].astype(jnp.float32)
        halves = [region[:, :LANES], region[:, LANES:]]
        turned = [pltpu.roll(half, QUARTER, 1) for half in halves]
        full = split(region)
        even_mask = split(jnp.concatenate([jnp.where(left, a, b) for a, b in zip(halves, turned)], axis=0))
        odd_mask = split(jnp.concatenate([jnp.where(left, b, a) for a, b in zip(halves, turned)], axis=0))

        field = [
            jnp.dot(band_first[rows], state[...], preferred_element_type=jnp.float32)
            for rows in (slice(0, 4 * NX), slice(4 * NX, 8 * NX))
        ]
        field = jnp.concatenate(field, axis=0)
        even_in, odd_in = [], []
        for part in range(2):
            values = [field[(r * 2 + part) * NX : (r * 2 + part + 1) * NX] for r in range(R)]
            between = pick(full, values)
            a, b = between[:, :LANES], between[:, LANES:]
            even_in.append(jnp.concatenate([jnp.where(low, a, 0.0), jnp.where(low, b, a)], axis=0).astype(jnp.bfloat16))
            odd_in.append(jnp.concatenate([jnp.where(high, a, b), jnp.where(high, b, 0.0)], axis=0).astype(jnp.bfloat16))
        wide = jnp.dot(jnp.concatenate(even_in, axis=1), band_even[...], preferred_element_type=jnp.float32)
        even = pick(even_mask, [wide[:, r * LANES : (r + 1) * LANES] for r in range(R)])
        wide = jnp.dot(jnp.concatenate(odd_in, axis=1), band_odd[...], preferred_element_type=jnp.float32)
        odd = pick(odd_mask, [wide[:, r * LANES : (r + 1) * LANES] for r in range(R)])
        for half in range(2):
            rows = slice(half * NX, (half + 1) * NX)
            cols = slice(half * LANES, (half + 1) * LANES)
            e, o = even[rows], odd[rows]
            out_ref[slot * 4 + half * 2] = e.astype(jnp.bfloat16)
            out_ref[slot * 4 + half * 2 + 1] = o.astype(jnp.bfloat16)
            state[:NX, cols] = jnp.where(left, e, o).astype(jnp.bfloat16)
            state[NX:, cols] = pltpu.roll(jnp.where(left, o, e), QUARTER, 1).astype(jnp.bfloat16)


def pack_kernel(quarter_ref, source_ref, *refs):
    own_ref, core_ref, chip_ref, packed = refs
    row_at = lax.broadcasted_iota(jnp.int32, (NX, NX), 0)
    col_at = lax.broadcasted_iota(jnp.int32, (NX, NX), 1)
    flip = (row_at + col_at == NX - 1).astype(jnp.bfloat16)
    left = lax.broadcasted_iota(jnp.int32, (NX, LANES), 1) < QUARTER
    for f in range(GROUP):
        real = jnp.dot(flip, source_ref[f, 0], preferred_element_type=jnp.float32)
        imag = jnp.dot(flip, source_ref[f, 1], preferred_element_type=jnp.float32)
        for half in range(2):
            cols = slice(half * LANES, (half + 1) * LANES)
            a = real[:, cols]
            b = pltpu.roll(imag[:, cols], QUARTER, 1)
            packed[half * 2, f] = jnp.where(left, a, b).astype(jnp.bfloat16)
            packed[half * 2 + 1, f] = jnp.where(left, b, a).astype(jnp.bfloat16)
    mine = quarter_ref[0]
    own_ref[...] = packed[mine]
    core_ref[0] = packed[mine ^ 1]
    core_ref[1] = packed[mine ^ 3]
    chip_ref[0] = packed[mine ^ 2]


def image_kernel(scale, quarter_ref, wave_ref, own_ref, core_ref, chip_ref, out_ref, wave, src, totals):
    sources = [own_ref, core_ref.at[0], chip_ref.at[0], chip_ref.at[1]]
    edge = jnp.zeros((4 * GROUP, REACH, LANES), jnp.float32)
    for ref in (wave, src):
        ref[:, :REACH, :] = edge
        ref[:, REACH + NX :, :] = edge
    for k in range(4):
        group = (quarter_ref[0] ^ k) * GROUP
        for f in range(GROUP):
            wave[k * GROUP + f, REACH : REACH + NX, :] = wave_ref[f * 4 + k].astype(jnp.float32)
            src[group + f, REACH : REACH + NX, :] = sources[k][f].astype(jnp.float32)

    tall, deep = NX // 8, H // 8
    inside = range(1, tall + deep - 2)

    def rows_from(start, carry):
        sums = {}
        for i in range(4 * GROUP):
            waves = {j: wave[i, pl.ds(start + 8 * j, 8), :] for j in inside}
            sources = {j: src[i, pl.ds(7 - start + 8 * j, 8), :] for j in inside}
            for m in range(tall):
                for n in range(deep):
                    j, k = m + n, tall - 1 - m + n
                    if j in inside and k in inside:
                        term = waves[j] * sources[k]
                        sums[m, n] = sums[m, n] + term if i else term
        for m in range(tall):
            for n in range(deep):
                value = sums.get((m, n))
                totals[start + 8 * m, 8 * n : 8 * n + 8, :] = jnp.zeros((8, LANES), jnp.float32) if value is None else value
        return carry

    lax.fori_loop(0, 8, rows_from, 0)
    left = lax.broadcasted_iota(jnp.int32, (REACH, LANES), 1) < QUARTER

    def fold(x, carry):
        total = totals[x]
        total = (total + pltpu.roll(total, QUARTER, 1)) * scale
        out_ref[x] = jnp.where(left, total[:REACH], total[REACH:]).astype(jnp.bfloat16)
        return carry

    lax.fori_loop(0, NX, fold, 0, unroll=32)


def sum_kernel(part_ref, out_ref):
    many, line = part_ref.shape[0], 8
    left = lax.broadcasted_iota(jnp.int32, (REACH, LANES), 1) < QUARTER
    for half in range(2):
        totals = []
        for q in (2 * half, 2 * half + 1):
            pair, core = divmod(q, 2)
            total = jnp.zeros((REACH, LANES), jnp.float32)
            for start in range(pair * line, many, 2 * line):
                for i in range(start + core, start + line, 2):
                    total = total + part_ref[i].astype(jnp.float32)
            totals.append(total)
        a, b = totals
        cols = slice(half * LANES, (half + 1) * LANES)
        out_ref[0, :REACH, 0, cols] = jnp.where(left, a, pltpu.roll(b, QUARTER, 1))
        out_ref[0, REACH:, 0, cols] = jnp.where(left, pltpu.roll(a, QUARTER, 1), b)


VMEM = pl.BlockSpec(memory_space=pltpu.VMEM)
SMEM = pl.BlockSpec(memory_space=pltpu.SMEM)
PARAMS = pltpu.CompilerParams(vmem_limit_bytes=24 << 20)


def cost(flops, moved):
    return pl.CostEstimate(flops=flops, bytes_accessed=moved, transcendentals=0)


def body(surface, regions, table, source):
    zh = lax.axis_index("zh")
    mine_x = lax.axis_index("x")
    core = lax.axis_index("core")
    blocks = lax.axis_size("zh")
    local = regions[0].astype(jnp.bfloat16)
    local, local_source, table = lax.optimization_barrier((local, source[0], table))
    columns = [local] + [
        lax.ppermute(local, "x", [(i, i ^ k) for i in range(GROUP)]) for k in range(1, GROUP)
    ]
    quarter = (lax.axis_index("yp") * 2 + core).astype(jnp.int32).reshape(1)
    four = jax.ShapeDtypeStruct((GROUP, NX, LANES), jnp.bfloat16)
    pair = jax.ShapeDtypeStruct((2, GROUP, NX, LANES), jnp.bfloat16)
    one = jax.ShapeDtypeStruct((1, GROUP, NX, LANES), jnp.bfloat16)
    packed, to_core, to_chip = pl.pallas_call(
        pack_kernel,
        out_shape=(four, pair, one),
        in_specs=[SMEM, VMEM],
        out_specs=(VMEM,) * 3,
        scratch_shapes=[pltpu.VMEM((4, GROUP, NX, LANES), jnp.bfloat16)],
        compiler_params=PARAMS,
        cost_estimate=cost(20_000_000, 1_000_000),
        name="pack",
    )(quarter, local_source)
    from_core = lax.ppermute(to_core, "core", [(0, 1), (1, 0)])
    from_chip = lax.ppermute(
        jnp.concatenate([to_chip, from_core[1:]], axis=0), "yp", [(0, 1), (1, 0)]
    )

    padded = jnp.pad(table.reshape(GROUP * R * 4, TAPS), ((0, 0), (0, LANES - TAPS)))
    bands = pl.pallas_call(
        bands_kernel,
        out_shape=(
            jax.ShapeDtypeStruct((R * 2 * NX, LANES), jnp.bfloat16),
            jax.ShapeDtypeStruct((2 * LANES, R * LANES), jnp.bfloat16),
            jax.ShapeDtypeStruct((2 * LANES, R * LANES), jnp.bfloat16),
        ),
        in_specs=[SMEM, VMEM],
        out_specs=(VMEM,) * 3,
        compiler_params=PARAMS,
        cost_estimate=cost(10_000_000, 1_000_000),
        name="bands",
    )(mine_x.astype(jnp.int32).reshape(1), padded)

    entering = lax.dynamic_index_in_dim(surface, mine_x, 0, keepdims=False).reshape(2 * NX, NY)
    before = ()
    for block in range(blocks):
        wave_shape = jax.ShapeDtypeStruct((GROUP * 4, NX, LANES), jnp.bfloat16)
        state_shape = (2 * NX, NY)
        last = block + 1 == blocks
        waves, *leaving = pl.pallas_call(
            functools.partial(chain_kernel, block == 0),
            out_shape=(wave_shape,) + (() if last else (jax.ShapeDtypeStruct(state_shape, jnp.bfloat16),)),
            in_specs=[SMEM] * 2 + [VMEM] * (4 + GROUP + len(before)),
            out_specs=(VMEM,) * (1 if last else 2),
            scratch_shapes=([pltpu.VMEM(state_shape, jnp.bfloat16)] if last else [])
            + [pltpu.VMEM((GROUP, NX, NY), jnp.bfloat16)],
            compiler_params=PARAMS,
            cost_estimate=cost(100_000_000, 4_000_000),
            name="chain",
        )((zh == block).astype(jnp.int32).reshape(1), mine_x.astype(jnp.int32).reshape(1), *bands, entering, *columns, *before)
        before = (waves,)
        if not last:
            entering = lax.ppermute(leaving[0], "zh", [(block, block + 1)])

    waves, from_chip = lax.optimization_barrier((waves, from_chip))
    waves = lax.all_to_all(waves, ("x",) + QUAD, 0, 0, tiled=True)

    scale = 1.0 / math.sqrt(surface.shape[0] * lax.axis_size(FREQ))
    partial_image = pl.pallas_call(
        lambda *refs: image_kernel(scale, *refs),
        out_shape=jax.ShapeDtypeStruct((NX, REACH, LANES), jnp.bfloat16),
        in_specs=[SMEM] + [VMEM] * 4,
        out_specs=VMEM,
        scratch_shapes=[pltpu.VMEM((4 * GROUP, NX + H, LANES), jnp.float32)] * 2
        + [pltpu.VMEM((NX, H, LANES), jnp.float32)],
        compiler_params=PARAMS,
        cost_estimate=cost(10_000_000, 2_000_000),
        name="image",
    )(quarter, waves, packed, from_core, from_chip)

    parts = lax.all_to_all(partial_image, FREQ, 0, 0, tiled=True)

    return pl.pallas_call(
        sum_kernel,
        out_shape=jax.ShapeDtypeStruct((1, H, 1, NY), jnp.float32),
        in_specs=[VMEM],
        out_specs=VMEM,
        compiler_params=PARAMS,
        name="total",
    )(parts)


def solution(mesh):
    wide = Mesh(np.asarray(mesh.devices).reshape(3, 4, 4, 2, 4, 2), AXES)
    in_specs = (
        P(FREQ, None, None, None),
        P(DEPTH, None, None),
        P(FREQ, None, None, None, None),
        P(DEPTH, FREQ, None, None, None),
    )
    out_specs = P(DEPTH, None, FREQ, None)
    return jax.shard_map(body, mesh=wide, in_specs=in_specs, out_specs=out_specs, check_vma=False)
```

```python
import functools
import math

import jax
import jax.numpy as jnp
import numpy as np
from jax import lax
from jax.experimental import pallas as pl
from jax.experimental.pallas import tpu as pltpu
from jax.sharding import Mesh
from jax.sharding import PartitionSpec as P

H = 32
REACH = H // 2
NX = 64
NY = 256
LANES = 128
QUARTER = 64
R = 4
TAPS = 25
MID = TAPS // 2
GROUP = 4

AXES = ("zh", "x", "yq", "yp", "zl", "core")
DEPTH = ("zh", "x")
FREQ = ("yq", "yp", "zl", "core")
QUAD = ("yp", "core")


def onehot(shape, fit, value=1.0):
    row_at = lax.broadcasted_iota(jnp.int32, shape, 0)
    col_at = lax.broadcasted_iota(jnp.int32, shape, 1)
    return jnp.where(fit(row_at, col_at), value, 0.0).astype(jnp.bfloat16)


def exact(a, b):
    return jnp.dot(a, b, preferred_element_type=jnp.float32)


def tap_rows(taps):
    many = R * 2

    def row(pass_at, part):
        return lambda i, j: j == (i >> 1) * 4 + pass_at * 2 + part(i & 1)

    def lanes(shift, sign=1):
        return onehot((LANES, LANES), lambda k, n: k == ((sign * n + shift) & (LANES - 1)))

    def chosen(fit):
        return exact(fit, taps).astype(jnp.bfloat16)

    shape = (many, 2 * many)
    straight = chosen(onehot(shape, row(0, lambda p: p)))
    row_at = lax.broadcasted_iota(jnp.int32, (many, LANES), 0)
    crossed = exact(chosen(onehot(shape, row(0, lambda p: 1 - p))), lanes(-(QUARTER - MID)))
    crossed = jnp.where((row_at & 1) == 0, -crossed, crossed)
    rows_first = exact(straight, lanes(MID)) + crossed
    rows_second = exact(chosen(onehot(shape, row(1, lambda p: p))), lanes(MID, -1))
    return rows_first, rows_second


def fan(row, height, shift):
    wide = jnp.broadcast_to(row, (height, row.shape[-1]))
    return pltpu.roll(wide, shift, 1, stride=1, stride_axis=0)


def bands_kernel(index_ref, table_ref, band_first, band_even, band_odd):
    taps = table_ref[pl.ds(pl.multiple_of(index_ref[0] * 16, 16), 16), :]
    rows_first, rows_second = tap_rows(taps)
    row_at = lax.broadcasted_iota(jnp.int32, (NX, LANES), 0)
    lane_at = lax.broadcasted_iota(jnp.int32, (NX, LANES), 1)
    near = jnp.abs((lane_at & (NX - 1)) - row_at) <= MID
    for block in range(R * 2):
        band = fan(rows_first[block : block + 1, :], NX, 0)
        band_first[block * NX : (block + 1) * NX, :] = jnp.where(near, band, 0.0).astype(jnp.bfloat16)

    left = lax.broadcasted_iota(jnp.int32, (LANES, LANES), 1) < QUARTER
    for region in range(R):
        tap_real = rows_second[2 * region : 2 * region + 1, :]
        tap_imag = rows_second[2 * region + 1 : 2 * region + 2, :]
        cols = slice(region * LANES, (region + 1) * LANES)
        for part, (to_real, to_imag) in enumerate(((tap_real, tap_imag), (-tap_imag, tap_real))):
            rows = slice(part * LANES, (part + 1) * LANES)
            real_band = fan(to_real, LANES, 0)
            imag_band = fan(to_imag, LANES, QUARTER)
            band_even[rows, cols] = jnp.where(left, real_band, imag_band).astype(jnp.bfloat16)
            band_odd[rows, cols] = jnp.where(left, imag_band, real_band).astype(jnp.bfloat16)


def pick(masks, values):
    out = values[R - 1]
    for region in range(R - 2, -1, -1):
        out = jnp.where(masks[region], values[region], out)
    return out


def chain_kernel(first, turn_ref, band_first, band_even, band_odd, entering_ref, regions_ref, *refs):
    out_ref, state = refs[-2:]
    active = turn_ref[0] == 1

    @pl.when(active)
    def _():
        run_steps(band_first, band_even, band_odd, entering_ref, regions_ref, out_ref, state)

    @pl.when(jnp.logical_not(active))
    def _():
        out_ref[...] = jnp.zeros_like(out_ref) if first else refs[0][...]
        state[...] = jnp.zeros_like(state)


def run_steps(band_first, band_even, band_odd, entering_ref, regions_ref, out_ref, state):
    state[...] = entering_ref[...]
    lane = lax.broadcasted_iota(jnp.int32, (NX, LANES), 1)
    left = lane < QUARTER
    low = lane < 96
    high = lane >= 32

    def split(values):
        return [values == float(r) for r in range(R - 1)]

    for slot in range(GROUP):
        region = regions_ref[slot].astype(jnp.float32)
        halves = [region[:, :LANES], region[:, LANES:]]
        turned = [pltpu.roll(half, QUARTER, 1) for half in halves]
        full = split(region)
        even_mask = split(jnp.concatenate([jnp.where(left, a, b) for a, b in zip(halves, turned)], axis=0))
        odd_mask = split(jnp.concatenate([jnp.where(left, b, a) for a, b in zip(halves, turned)], axis=0))

        field = [
            jnp.dot(band_first[rows], state[...], preferred_element_type=jnp.float32)
            for rows in (slice(0, 4 * NX), slice(4 * NX, 8 * NX))
        ]
        field = jnp.concatenate(field, axis=0)
        even_in, odd_in = [], []
        for part in range(2):
            values = [field[(r * 2 + part) * NX : (r * 2 + part + 1) * NX] for r in range(R)]
            between = pick(full, values)
            a, b = between[:, :LANES], between[:, LANES:]
            even_in.append(jnp.concatenate([jnp.where(low, a, 0.0), jnp.where(low, b, a)], axis=0).astype(jnp.bfloat16))
            odd_in.append(jnp.concatenate([jnp.where(high, a, b), jnp.where(high, b, 0.0)], axis=0).astype(jnp.bfloat16))
        wide = jnp.dot(jnp.concatenate(even_in, axis=1), band_even[...], preferred_element_type=jnp.float32)
        even = pick(even_mask, [wide[:, r * LANES : (r + 1) * LANES] for r in range(R)])
        wide = jnp.dot(jnp.concatenate(odd_in, axis=1), band_odd[...], preferred_element_type=jnp.float32)
        odd = pick(odd_mask, [wide[:, r * LANES : (r + 1) * LANES] for r in range(R)])
        for half in range(2):
            rows = slice(half * NX, (half + 1) * NX)
            cols = slice(half * LANES, (half + 1) * LANES)
            e, o = even[rows], odd[rows]
            out_ref[slot * 4 + half * 2] = e.astype(jnp.bfloat16)
            out_ref[slot * 4 + half * 2 + 1] = o.astype(jnp.bfloat16)
            state[:NX, cols] = jnp.where(left, e, o).astype(jnp.bfloat16)
            state[NX:, cols] = pltpu.roll(jnp.where(left, o, e), QUARTER, 1).astype(jnp.bfloat16)


def pack_kernel(quarter_ref, source_ref, *refs):
    own_ref, core_ref, chip_ref, packed = refs
    row_at = lax.broadcasted_iota(jnp.int32, (NX, NX), 0)
    col_at = lax.broadcasted_iota(jnp.int32, (NX, NX), 1)
    flip = (row_at + col_at == NX - 1).astype(jnp.bfloat16)
    left = lax.broadcasted_iota(jnp.int32, (NX, LANES), 1) < QUARTER
    for f in range(GROUP):
        real = jnp.dot(flip, source_ref[f, 0], preferred_element_type=jnp.float32)
        imag = jnp.dot(flip, source_ref[f, 1], preferred_element_type=jnp.float32)
        for half in range(2):
            cols = slice(half * LANES, (half + 1) * LANES)
            a = real[:, cols]
            b = pltpu.roll(imag[:, cols], QUARTER, 1)
            packed[half * 2, f] = jnp.where(left, a, b).astype(jnp.bfloat16)
            packed[half * 2 + 1, f] = jnp.where(left, b, a).astype(jnp.bfloat16)
    mine = quarter_ref[0]
    own_ref[...] = packed[mine]
    core_ref[0] = packed[mine ^ 1]
    core_ref[1] = packed[mine ^ 3]
    chip_ref[0] = packed[mine ^ 2]


def image_kernel(scale, quarter_ref, wave_ref, own_ref, core_ref, chip_ref, out_ref, wave, src, totals):
    sources = [own_ref, core_ref.at[0], chip_ref.at[0], chip_ref.at[1]]
    edge = jnp.zeros((4 * GROUP, REACH, LANES), jnp.float32)
    for ref in (wave, src):
        ref[:, :REACH, :] = edge
        ref[:, REACH + NX :, :] = edge
    for k in range(4):
        group = (quarter_ref[0] ^ k) * GROUP
        for f in range(GROUP):
            wave[k * GROUP + f, REACH : REACH + NX, :] = wave_ref[f * 4 + k].astype(jnp.float32)
            src[group + f, REACH : REACH + NX, :] = sources[k][f].astype(jnp.float32)

    tall, deep = NX // 8, H // 8
    inside = range(1, tall + deep - 2)

    def rows_from(start, carry):
        sums = {}
        for i in range(4 * GROUP):
            waves = {j: wave[i, pl.ds(start + 8 * j, 8), :] for j in inside}
            sources = {j: src[i, pl.ds(7 - start + 8 * j, 8), :] for j in inside}
            for m in range(tall):
                for n in range(deep):
                    j, k = m + n, tall - 1 - m + n
                    if j in inside and k in inside:
                        term = waves[j] * sources[k]
                        sums[m, n] = sums[m, n] + term if i else term
        for m in range(tall):
            for n in range(deep):
                value = sums.get((m, n))
                totals[start + 8 * m, 8 * n : 8 * n + 8, :] = jnp.zeros((8, LANES), jnp.float32) if value is None else value
        return carry

    lax.fori_loop(0, 8, rows_from, 0)
    left = lax.broadcasted_iota(jnp.int32, (REACH, LANES), 1) < QUARTER

    def fold(x, carry):
        total = totals[x]
        total = (total + pltpu.roll(total, QUARTER, 1)) * scale
        out_ref[x] = jnp.where(left, total[:REACH], total[REACH:]).astype(jnp.bfloat16)
        return carry

    lax.fori_loop(0, NX, fold, 0, unroll=32)


def sum_kernel(part_ref, out_ref):
    many, line = part_ref.shape[0], 8
    left = lax.broadcasted_iota(jnp.int32, (REACH, LANES), 1) < QUARTER
    for half in range(2):
        totals = []
        for q in (2 * half, 2 * half + 1):
            pair, core = divmod(q, 2)
            total = jnp.zeros((REACH, LANES), jnp.float32)
            for start in range(pair * line, many, 2 * line):
                for i in range(start + core, start + line, 2):
                    total = total + part_ref[i].astype(jnp.float32)
            totals.append(total)
        a, b = totals
        cols = slice(half * LANES, (half + 1) * LANES)
        out_ref[0, :REACH, 0, cols] = jnp.where(left, a, pltpu.roll(b, QUARTER, 1))
        out_ref[0, REACH:, 0, cols] = jnp.where(left, pltpu.roll(a, QUARTER, 1), b)


VMEM = pl.BlockSpec(memory_space=pltpu.VMEM)
SMEM = pl.BlockSpec(memory_space=pltpu.SMEM)
PARAMS = pltpu.CompilerParams(vmem_limit_bytes=24 << 20)


def cost(flops, moved):
    return pl.CostEstimate(flops=flops, bytes_accessed=moved, transcendentals=0)


def body(surface, regions, table, source):
    zh = lax.axis_index("zh")
    mine_x = lax.axis_index("x")
    core = lax.axis_index("core")
    blocks = lax.axis_size("zh")
    local = regions[0].astype(jnp.bfloat16)
    copies = jnp.broadcast_to(local[None], (GROUP, NX, NY))
    copies, local_source, table = lax.optimization_barrier((copies, source[0], table))
    all_regions = lax.all_to_all(copies, "x", 0, 0, tiled=True)
    quarter = (lax.axis_index("yp") * 2 + core).astype(jnp.int32).reshape(1)
    four = jax.ShapeDtypeStruct((GROUP, NX, LANES), jnp.bfloat16)
    pair = jax.ShapeDtypeStruct((2, GROUP, NX, LANES), jnp.bfloat16)
    one = jax.ShapeDtypeStruct((1, GROUP, NX, LANES), jnp.bfloat16)
    packed, to_core, to_chip = pl.pallas_call(
        pack_kernel,
        out_shape=(four, pair, one),
        in_specs=[SMEM, VMEM],
        out_specs=(VMEM,) * 3,
        scratch_shapes=[pltpu.VMEM((4, GROUP, NX, LANES), jnp.bfloat16)],
        compiler_params=PARAMS,
        cost_estimate=cost(20_000_000, 1_000_000),
        name="pack",
    )(quarter, local_source)
    from_core = lax.ppermute(to_core, "core", [(0, 1), (1, 0)])
    from_chip = lax.ppermute(
        jnp.concatenate([to_chip, from_core[1:]], axis=0), "yp", [(0, 1), (1, 0)]
    )

    padded = jnp.pad(table.reshape(GROUP * R * 4, TAPS), ((0, 0), (0, LANES - TAPS)))
    bands = pl.pallas_call(
        bands_kernel,
        out_shape=(
            jax.ShapeDtypeStruct((R * 2 * NX, LANES), jnp.bfloat16),
            jax.ShapeDtypeStruct((2 * LANES, R * LANES), jnp.bfloat16),
            jax.ShapeDtypeStruct((2 * LANES, R * LANES), jnp.bfloat16),
        ),
        in_specs=[SMEM, VMEM],
        out_specs=(VMEM,) * 3,
        compiler_params=PARAMS,
        cost_estimate=cost(10_000_000, 1_000_000),
        name="bands",
    )(mine_x.astype(jnp.int32).reshape(1), padded)

    entering = lax.dynamic_index_in_dim(surface, mine_x, 0, keepdims=False).reshape(2 * NX, NY)
    before = ()
    for block in range(blocks):
        wave_shape = jax.ShapeDtypeStruct((GROUP * 4, NX, LANES), jnp.bfloat16)
        state_shape = (2 * NX, NY)
        last = block + 1 == blocks
        waves, *leaving = pl.pallas_call(
            functools.partial(chain_kernel, block == 0),
            out_shape=(wave_shape,) + (() if last else (jax.ShapeDtypeStruct(state_shape, jnp.bfloat16),)),
            in_specs=[SMEM] + [VMEM] * (5 + len(before)),
            out_specs=(VMEM,) * (1 if last else 2),
            scratch_shapes=[pltpu.VMEM(state_shape, jnp.bfloat16)] if last else [],
            compiler_params=PARAMS,
            cost_estimate=cost(300_000_000, 4_000_000),
            name="chain",
        )((zh == block).astype(jnp.int32).reshape(1), *bands, entering, all_regions, *before)
        before = (waves,)
        if not last:
            entering = lax.ppermute(leaving[0], "zh", [(block, block + 1)])

    waves, from_chip = lax.optimization_barrier((waves, from_chip))
    waves = lax.all_to_all(waves, ("x",) + QUAD, 0, 0, tiled=True)

    scale = 1.0 / math.sqrt(surface.shape[0] * lax.axis_size(FREQ))
    partial_image = pl.pallas_call(
        lambda *refs: image_kernel(scale, *refs),
        out_shape=jax.ShapeDtypeStruct((NX, REACH, LANES), jnp.bfloat16),
        in_specs=[SMEM] + [VMEM] * 4,
        out_specs=VMEM,
        scratch_shapes=[pltpu.VMEM((4 * GROUP, NX + H, LANES), jnp.float32)] * 2
        + [pltpu.VMEM((NX, H, LANES), jnp.float32)],
        compiler_params=PARAMS,
        cost_estimate=cost(10_000_000, 2_000_000),
        name="image",
    )(quarter, waves, packed, from_core, from_chip)

    parts = lax.all_to_all(partial_image, FREQ, 0, 0, tiled=True)

    return pl.pallas_call(
        sum_kernel,
        out_shape=jax.ShapeDtypeStruct((1, H, 1, NY), jnp.float32),
        in_specs=[VMEM],
        out_specs=VMEM,
        compiler_params=PARAMS,
        name="total",
    )(parts)


def solution(mesh):
    wide = Mesh(np.asarray(mesh.devices).reshape(3, 4, 4, 2, 4, 2), AXES)
    in_specs = (
        P(FREQ, None, None, None),
        P(DEPTH, None, None),
        P(FREQ, None, None, None, None),
        P(DEPTH, FREQ, None, None, None),
    )
    out_specs = P(DEPTH, None, FREQ, None)
    return jax.shard_map(body, mesh=wide, in_specs=in_specs, out_specs=out_specs, check_vma=False)
```

```python
import functools
import math

import jax
import jax.numpy as jnp
import numpy as np
from jax import lax
from jax.experimental import pallas as pl
from jax.experimental.pallas import tpu as pltpu
from jax.sharding import Mesh
from jax.sharding import PartitionSpec as P

H = 32
REACH = H // 2
NX = 64
NY = 256
LANES = 128
QUARTER = 64
R = 4
TAPS = 25
MID = TAPS // 2
GROUP = 4

AXES = ("zh", "x", "yq", "yp", "zl", "core")
DEPTH = ("zh", "x")
FREQ = ("yq", "yp", "zl", "core")
QUAD = ("yp", "core")


def onehot(shape, fit, value=1.0):
    row_at = lax.broadcasted_iota(jnp.int32, shape, 0)
    col_at = lax.broadcasted_iota(jnp.int32, shape, 1)
    return jnp.where(fit(row_at, col_at), value, 0.0).astype(jnp.bfloat16)


def exact(a, b):
    return jnp.dot(a, b, preferred_element_type=jnp.float32)


def tap_rows(taps):
    many = R * 2

    def row(pass_at, part):
        return lambda i, j: j == (i >> 1) * 4 + pass_at * 2 + part(i & 1)

    def lanes(shift, sign=1):
        return onehot((LANES, LANES), lambda k, n: k == ((sign * n + shift) & (LANES - 1)))

    def chosen(fit):
        return exact(fit, taps).astype(jnp.bfloat16)

    shape = (many, 2 * many)
    straight = chosen(onehot(shape, row(0, lambda p: p)))
    row_at = lax.broadcasted_iota(jnp.int32, (many, LANES), 0)
    crossed = exact(chosen(onehot(shape, row(0, lambda p: 1 - p))), lanes(-(QUARTER - MID)))
    crossed = jnp.where((row_at & 1) == 0, -crossed, crossed)
    rows_first = exact(straight, lanes(MID)) + crossed
    rows_second = exact(chosen(onehot(shape, row(1, lambda p: p))), lanes(MID, -1))
    return rows_first, rows_second


def fan(row, height, shift):
    wide = jnp.broadcast_to(row, (height, row.shape[-1]))
    return pltpu.roll(wide, shift, 1, stride=1, stride_axis=0)


def bands_kernel(index_ref, table_ref, band_first, band_even, band_odd):
    taps = table_ref[pl.ds(pl.multiple_of(index_ref[0] * 16, 16), 16), :]
    rows_first, rows_second = tap_rows(taps)
    row_at = lax.broadcasted_iota(jnp.int32, (NX, LANES), 0)
    lane_at = lax.broadcasted_iota(jnp.int32, (NX, LANES), 1)
    near = jnp.abs((lane_at & (NX - 1)) - row_at) <= MID
    for block in range(R * 2):
        band = fan(rows_first[block : block + 1, :], NX, 0)
        band_first[block * NX : (block + 1) * NX, :] = jnp.where(near, band, 0.0).astype(jnp.bfloat16)

    left = lax.broadcasted_iota(jnp.int32, (LANES, LANES), 1) < QUARTER
    for region in range(R):
        tap_real = rows_second[2 * region : 2 * region + 1, :]
        tap_imag = rows_second[2 * region + 1 : 2 * region + 2, :]
        cols = slice(region * LANES, (region + 1) * LANES)
        for part, (to_real, to_imag) in enumerate(((tap_real, tap_imag), (-tap_imag, tap_real))):
            rows = slice(part * LANES, (part + 1) * LANES)
            real_band = fan(to_real, LANES, 0)
            imag_band = fan(to_imag, LANES, QUARTER)
            band_even[rows, cols] = jnp.where(left, real_band, imag_band).astype(jnp.bfloat16)
            band_odd[rows, cols] = jnp.where(left, imag_band, real_band).astype(jnp.bfloat16)


def pick(masks, values):
    out = values[R - 1]
    for region in range(R - 2, -1, -1):
        out = jnp.where(masks[region], values[region], out)
    return out


def chain_kernel(first, turn_ref, band_first, band_even, band_odd, entering_ref, regions_ref, *refs):
    out_ref, state = refs[-2:]
    active = turn_ref[0] == 1

    @pl.when(active)
    def _():
        run_steps(band_first, band_even, band_odd, entering_ref, regions_ref, out_ref, state)

    @pl.when(jnp.logical_not(active))
    def _():
        out_ref[...] = jnp.zeros_like(out_ref) if first else refs[0][...]
        state[...] = jnp.zeros_like(state)


def run_steps(band_first, band_even, band_odd, entering_ref, regions_ref, out_ref, state):
    state[...] = entering_ref[...]
    lane = lax.broadcasted_iota(jnp.int32, (NX, LANES), 1)
    left = lane < QUARTER
    low = lane < 96
    high = lane >= 32

    def split(values):
        return [values == float(r) for r in range(R - 1)]

    for slot in range(GROUP):
        region = regions_ref[slot].astype(jnp.float32)
        halves = [region[:, :LANES], region[:, LANES:]]
        turned = [pltpu.roll(half, QUARTER, 1) for half in halves]
        full = split(region)
        even_mask = split(jnp.concatenate([jnp.where(left, a, b) for a, b in zip(halves, turned)], axis=0))
        odd_mask = split(jnp.concatenate([jnp.where(left, b, a) for a, b in zip(halves, turned)], axis=0))

        field = [
            jnp.dot(band_first[rows], state[...], preferred_element_type=jnp.float32)
            for rows in (slice(0, 4 * NX), slice(4 * NX, 8 * NX))
        ]
        field = jnp.concatenate(field, axis=0)
        even_in, odd_in = [], []
        for part in range(2):
            values = [field[(r * 2 + part) * NX : (r * 2 + part + 1) * NX] for r in range(R)]
            between = pick(full, values)
            a, b = between[:, :LANES], between[:, LANES:]
            even_in.append(jnp.concatenate([jnp.where(low, a, 0.0), jnp.where(low, b, a)], axis=0).astype(jnp.bfloat16))
            odd_in.append(jnp.concatenate([jnp.where(high, a, b), jnp.where(high, b, 0.0)], axis=0).astype(jnp.bfloat16))
        wide = jnp.dot(jnp.concatenate(even_in, axis=1), band_even[...], preferred_element_type=jnp.float32)
        even = pick(even_mask, [wide[:, r * LANES : (r + 1) * LANES] for r in range(R)])
        wide = jnp.dot(jnp.concatenate(odd_in, axis=1), band_odd[...], preferred_element_type=jnp.float32)
        odd = pick(odd_mask, [wide[:, r * LANES : (r + 1) * LANES] for r in range(R)])
        for half in range(2):
            rows = slice(half * NX, (half + 1) * NX)
            cols = slice(half * LANES, (half + 1) * LANES)
            e, o = even[rows], odd[rows]
            out_ref[slot * 4 + half * 2] = e.astype(jnp.bfloat16)
            out_ref[slot * 4 + half * 2 + 1] = o.astype(jnp.bfloat16)
            state[:NX, cols] = jnp.where(left, e, o).astype(jnp.bfloat16)
            state[NX:, cols] = pltpu.roll(jnp.where(left, o, e), QUARTER, 1).astype(jnp.bfloat16)


def pack_kernel(quarter_ref, source_ref, *refs):
    own_ref, chip_ref, core_ref, packed = refs
    row_at = lax.broadcasted_iota(jnp.int32, (NX, NX), 0)
    col_at = lax.broadcasted_iota(jnp.int32, (NX, NX), 1)
    flip = (row_at + col_at == NX - 1).astype(jnp.bfloat16)
    left = lax.broadcasted_iota(jnp.int32, (NX, LANES), 1) < QUARTER
    for f in range(GROUP):
        real = jnp.dot(flip, source_ref[f, 0], preferred_element_type=jnp.float32)
        imag = jnp.dot(flip, source_ref[f, 1], preferred_element_type=jnp.float32)
        for half in range(2):
            cols = slice(half * LANES, (half + 1) * LANES)
            a = real[:, cols]
            b = pltpu.roll(imag[:, cols], QUARTER, 1)
            packed[half * 2, f] = jnp.where(left, a, b).astype(jnp.bfloat16)
            packed[half * 2 + 1, f] = jnp.where(left, b, a).astype(jnp.bfloat16)
    mine = quarter_ref[0]
    own_ref[...] = packed[mine]
    chip_ref[0] = packed[mine ^ 2]
    chip_ref[1] = packed[mine ^ 3]
    core_ref[0] = packed[mine ^ 1]


def image_kernel(scale, quarter_ref, wave_ref, own_ref, core_ref, chip_ref, out_ref, wave, src, totals):
    sources = [own_ref, core_ref.at[0], chip_ref.at[0], core_ref.at[1]]
    edge = jnp.zeros((4 * GROUP, REACH, LANES), jnp.float32)
    for ref in (wave, src):
        ref[:, :REACH, :] = edge
        ref[:, REACH + NX :, :] = edge
    for k in range(4):
        group = (quarter_ref[0] ^ k) * GROUP
        for f in range(GROUP):
            wave[k * GROUP + f, REACH : REACH + NX, :] = wave_ref[f * 4 + k].astype(jnp.float32)
            src[group + f, REACH : REACH + NX, :] = sources[k][f].astype(jnp.float32)

    tall, deep = NX // 8, H // 8
    inside = range(1, tall + deep - 2)

    def rows_from(start, carry):
        sums = {}
        for i in range(4 * GROUP):
            waves = {j: wave[i, pl.ds(start + 8 * j, 8), :] for j in inside}
            sources = {j: src[i, pl.ds(7 - start + 8 * j, 8), :] for j in inside}
            for m in range(tall):
                for n in range(deep):
                    j, k = m + n, tall - 1 - m + n
                    if j in inside and k in inside:
                        term = waves[j] * sources[k]
                        sums[m, n] = sums[m, n] + term if i else term
        for m in range(tall):
            for n in range(deep):
                value = sums.get((m, n))
                totals[start + 8 * m, 8 * n : 8 * n + 8, :] = jnp.zeros((8, LANES), jnp.float32) if value is None else value
        return carry

    lax.fori_loop(0, 8, rows_from, 0)
    left = lax.broadcasted_iota(jnp.int32, (REACH, LANES), 1) < QUARTER

    def fold(x, carry):
        total = totals[x]
        total = (total + pltpu.roll(total, QUARTER, 1)) * scale
        out_ref[x] = jnp.where(left, total[:REACH], total[REACH:]).astype(jnp.bfloat16)
        return carry

    lax.fori_loop(0, NX, fold, 0, unroll=True)


def sum_kernel(part_ref, out_ref):
    many, line = part_ref.shape[0], 8
    left = lax.broadcasted_iota(jnp.int32, (REACH, LANES), 1) < QUARTER
    for half in range(2):
        totals = []
        for q in (2 * half, 2 * half + 1):
            pair, core = divmod(q, 2)
            total = jnp.zeros((REACH, LANES), jnp.float32)
            for start in range(pair * line, many, 2 * line):
                for i in range(start + core, start + line, 2):
                    total = total + part_ref[i].astype(jnp.float32)
            totals.append(total)
        a, b = totals
        cols = slice(half * LANES, (half + 1) * LANES)
        out_ref[0, :REACH, 0, cols] = jnp.where(left, a, pltpu.roll(b, QUARTER, 1))
        out_ref[0, REACH:, 0, cols] = jnp.where(left, pltpu.roll(a, QUARTER, 1), b)


VMEM = pl.BlockSpec(memory_space=pltpu.VMEM)
SMEM = pl.BlockSpec(memory_space=pltpu.SMEM)
PARAMS = pltpu.CompilerParams(vmem_limit_bytes=24 << 20)


def cost(flops, moved):
    return pl.CostEstimate(flops=flops, bytes_accessed=moved, transcendentals=0)


def body(surface, regions, table, source):
    zh = lax.axis_index("zh")
    mine_x = lax.axis_index("x")
    core = lax.axis_index("core")
    blocks = lax.axis_size("zh")
    local = regions[0].astype(jnp.bfloat16)
    copies = jnp.broadcast_to(local[None], (GROUP, NX, NY))
    copies, local_source, table = lax.optimization_barrier((copies, source[0], table))
    all_regions = lax.all_to_all(copies, "x", 0, 0, tiled=True)
    quarter = (lax.axis_index("yp") * 2 + core).astype(jnp.int32).reshape(1)
    four = jax.ShapeDtypeStruct((GROUP, NX, LANES), jnp.bfloat16)
    pair = jax.ShapeDtypeStruct((2, GROUP, NX, LANES), jnp.bfloat16)
    one = jax.ShapeDtypeStruct((1, GROUP, NX, LANES), jnp.bfloat16)
    packed, to_chip, to_core = pl.pallas_call(
        pack_kernel,
        out_shape=(four, pair, one),
        in_specs=[SMEM, VMEM],
        out_specs=(VMEM,) * 3,
        scratch_shapes=[pltpu.VMEM((4, GROUP, NX, LANES), jnp.bfloat16)],
        compiler_params=PARAMS,
        cost_estimate=cost(20_000_000, 1_000_000),
        name="pack",
    )(quarter, local_source)
    from_chip = lax.ppermute(to_chip, "yp", [(0, 1), (1, 0)])
    from_core = lax.ppermute(
        jnp.concatenate([to_core, from_chip[1:]], axis=0), "core", [(0, 1), (1, 0)]
    )

    padded = jnp.pad(table.reshape(GROUP * R * 4, TAPS), ((0, 0), (0, LANES - TAPS)))
    bands = pl.pallas_call(
        bands_kernel,
        out_shape=(
            jax.ShapeDtypeStruct((R * 2 * NX, LANES), jnp.bfloat16),
            jax.ShapeDtypeStruct((2 * LANES, R * LANES), jnp.bfloat16),
            jax.ShapeDtypeStruct((2 * LANES, R * LANES), jnp.bfloat16),
        ),
        in_specs=[SMEM, VMEM],
        out_specs=(VMEM,) * 3,
        compiler_params=PARAMS,
        cost_estimate=cost(10_000_000, 1_000_000),
        name="bands",
    )(mine_x.astype(jnp.int32).reshape(1), padded)

    entering = lax.dynamic_index_in_dim(surface, mine_x, 0, keepdims=False).reshape(2 * NX, NY)
    before = ()
    for block in range(blocks):
        wave_shape = jax.ShapeDtypeStruct((GROUP * 4, NX, LANES), jnp.bfloat16)
        state_shape = (2 * NX, NY)
        last = block + 1 == blocks
        waves, *leaving = pl.pallas_call(
            functools.partial(chain_kernel, block == 0),
            out_shape=(wave_shape,) + (() if last else (jax.ShapeDtypeStruct(state_shape, jnp.bfloat16),)),
            in_specs=[SMEM] + [VMEM] * (5 + len(before)),
            out_specs=(VMEM,) * (1 if last else 2),
            scratch_shapes=[pltpu.VMEM(state_shape, jnp.bfloat16)] if last else [],
            compiler_params=PARAMS,
            cost_estimate=cost(300_000_000, 4_000_000),
            name="chain",
        )((zh == block).astype(jnp.int32).reshape(1), *bands, entering, all_regions, *before)
        before = (waves,)
        if not last:
            entering = lax.ppermute(leaving[0], "zh", [(block, block + 1)])

    waves, from_core = lax.optimization_barrier((waves, from_core))
    waves = lax.all_to_all(waves, ("x",) + QUAD, 0, 0, tiled=True)

    scale = 1.0 / math.sqrt(surface.shape[0] * lax.axis_size(FREQ))
    partial_image = pl.pallas_call(
        lambda *refs: image_kernel(scale, *refs),
        out_shape=jax.ShapeDtypeStruct((NX, REACH, LANES), jnp.bfloat16),
        in_specs=[SMEM] + [VMEM] * 4,
        out_specs=VMEM,
        scratch_shapes=[pltpu.VMEM((4 * GROUP, NX + H, LANES), jnp.float32)] * 2
        + [pltpu.VMEM((NX, H, LANES), jnp.float32)],
        compiler_params=PARAMS,
        cost_estimate=cost(10_000_000, 2_000_000),
        name="image",
    )(quarter, waves, packed, from_core, from_chip)

    parts = lax.all_to_all(partial_image, FREQ, 0, 0, tiled=True)

    return pl.pallas_call(
        sum_kernel,
        out_shape=jax.ShapeDtypeStruct((1, H, 1, NY), jnp.float32),
        in_specs=[VMEM],
        out_specs=VMEM,
        compiler_params=PARAMS,
        name="total",
    )(parts)


def solution(mesh):
    wide = Mesh(np.asarray(mesh.devices).reshape(3, 4, 4, 2, 4, 2), AXES)
    in_specs = (
        P(FREQ, None, None, None),
        P(DEPTH, None, None),
        P(FREQ, None, None, None, None),
        P(DEPTH, FREQ, None, None, None),
    )
    out_specs = P(DEPTH, None, FREQ, None)
    return jax.shard_map(body, mesh=wide, in_specs=in_specs, out_specs=out_specs, check_vma=False)
```

```python
import functools
import math

import jax
import jax.numpy as jnp
import numpy as np
from jax import lax
from jax.experimental import pallas as pl
from jax.experimental.pallas import tpu as pltpu
from jax.sharding import Mesh
from jax.sharding import PartitionSpec as P

H = 32
REACH = H // 2
NX = 64
NY = 256
LANES = 128
QUARTER = 64
R = 4
TAPS = 25
MID = TAPS // 2
GROUP = 4

AXES = ("zh", "x", "y", "zq", "zp", "core")
DEPTH = ("zh", "x")
FREQ = ("y", "zq", "zp", "core")
QUAD = ("zp", "core")


def onehot(shape, fit, value=1.0):
    row_at = lax.broadcasted_iota(jnp.int32, shape, 0)
    col_at = lax.broadcasted_iota(jnp.int32, shape, 1)
    return jnp.where(fit(row_at, col_at), value, 0.0).astype(jnp.bfloat16)


def exact(a, b):
    return jnp.dot(a, b, preferred_element_type=jnp.float32)


def tap_rows(taps):
    many = R * 2

    def row(pass_at, part):
        return lambda i, j: j == (i >> 1) * 4 + pass_at * 2 + part(i & 1)

    def lanes(shift, sign=1):
        return onehot((LANES, LANES), lambda k, n: k == ((sign * n + shift) & (LANES - 1)))

    def chosen(fit):
        return exact(fit, taps).astype(jnp.bfloat16)

    shape = (many, 2 * many)
    straight = chosen(onehot(shape, row(0, lambda p: p)))
    row_at = lax.broadcasted_iota(jnp.int32, (many, LANES), 0)
    crossed = exact(chosen(onehot(shape, row(0, lambda p: 1 - p))), lanes(-(QUARTER - MID)))
    crossed = jnp.where((row_at & 1) == 0, -crossed, crossed)
    rows_first = exact(straight, lanes(MID)) + crossed
    rows_second = exact(chosen(onehot(shape, row(1, lambda p: p))), lanes(MID, -1))
    return rows_first, rows_second


def fan(row, height, shift):
    wide = jnp.broadcast_to(row, (height, row.shape[-1]))
    return pltpu.roll(wide, shift, 1, stride=1, stride_axis=0)


def bands_kernel(index_ref, table_ref, band_first, band_even, band_odd):
    taps = table_ref[pl.ds(pl.multiple_of(index_ref[0] * 16, 16), 16), :]
    rows_first, rows_second = tap_rows(taps)
    row_at = lax.broadcasted_iota(jnp.int32, (NX, LANES), 0)
    lane_at = lax.broadcasted_iota(jnp.int32, (NX, LANES), 1)
    near = jnp.abs((lane_at & (NX - 1)) - row_at) <= MID
    for block in range(R * 2):
        band = fan(rows_first[block : block + 1, :], NX, 0)
        band_first[block * NX : (block + 1) * NX, :] = jnp.where(near, band, 0.0).astype(jnp.bfloat16)

    left = lax.broadcasted_iota(jnp.int32, (LANES, LANES), 1) < QUARTER
    for region in range(R):
        tap_real = rows_second[2 * region : 2 * region + 1, :]
        tap_imag = rows_second[2 * region + 1 : 2 * region + 2, :]
        cols = slice(region * LANES, (region + 1) * LANES)
        for part, (to_real, to_imag) in enumerate(((tap_real, tap_imag), (-tap_imag, tap_real))):
            rows = slice(part * LANES, (part + 1) * LANES)
            real_band = fan(to_real, LANES, 0)
            imag_band = fan(to_imag, LANES, QUARTER)
            band_even[rows, cols] = jnp.where(left, real_band, imag_band).astype(jnp.bfloat16)
            band_odd[rows, cols] = jnp.where(left, imag_band, real_band).astype(jnp.bfloat16)


def pick(masks, values):
    out = values[R - 1]
    for region in range(R - 2, -1, -1):
        out = jnp.where(masks[region], values[region], out)
    return out


def chain_kernel(first, turn_ref, band_first, band_even, band_odd, entering_ref, regions_ref, *refs):
    out_ref, state = refs[-2:]
    active = turn_ref[0] == 1

    @pl.when(active)
    def _():
        run_steps(band_first, band_even, band_odd, entering_ref, regions_ref, out_ref, state)

    @pl.when(jnp.logical_not(active))
    def _():
        out_ref[...] = jnp.zeros_like(out_ref) if first else refs[0][...]
        state[...] = jnp.zeros_like(state)


def run_steps(band_first, band_even, band_odd, entering_ref, regions_ref, out_ref, state):
    state[...] = entering_ref[...]
    lane = lax.broadcasted_iota(jnp.int32, (NX, LANES), 1)
    left = lane < QUARTER
    low = lane < 96
    high = lane >= 32

    def split(values):
        return [values == float(r) for r in range(R - 1)]

    for slot in range(GROUP):
        region = regions_ref[slot].astype(jnp.float32)
        halves = [region[:, :LANES], region[:, LANES:]]
        turned = [pltpu.roll(half, QUARTER, 1) for half in halves]
        full = split(region)
        even_mask = split(jnp.concatenate([jnp.where(left, a, b) for a, b in zip(halves, turned)], axis=0))
        odd_mask = split(jnp.concatenate([jnp.where(left, b, a) for a, b in zip(halves, turned)], axis=0))

        field = [
            jnp.dot(band_first[rows], state[...], preferred_element_type=jnp.float32)
            for rows in (slice(0, 4 * NX), slice(4 * NX, 8 * NX))
        ]
        field = jnp.concatenate(field, axis=0)
        even_in, odd_in = [], []
        for part in range(2):
            values = [field[(r * 2 + part) * NX : (r * 2 + part + 1) * NX] for r in range(R)]
            between = pick(full, values)
            a, b = between[:, :LANES], between[:, LANES:]
            even_in.append(jnp.concatenate([jnp.where(low, a, 0.0), jnp.where(low, b, a)], axis=0).astype(jnp.bfloat16))
            odd_in.append(jnp.concatenate([jnp.where(high, a, b), jnp.where(high, b, 0.0)], axis=0).astype(jnp.bfloat16))
        wide = jnp.dot(jnp.concatenate(even_in, axis=1), band_even[...], preferred_element_type=jnp.float32)
        even = pick(even_mask, [wide[:, r * LANES : (r + 1) * LANES] for r in range(R)])
        wide = jnp.dot(jnp.concatenate(odd_in, axis=1), band_odd[...], preferred_element_type=jnp.float32)
        odd = pick(odd_mask, [wide[:, r * LANES : (r + 1) * LANES] for r in range(R)])
        for half in range(2):
            rows = slice(half * NX, (half + 1) * NX)
            cols = slice(half * LANES, (half + 1) * LANES)
            e, o = even[rows], odd[rows]
            out_ref[slot * 4 + half * 2] = e.astype(jnp.bfloat16)
            out_ref[slot * 4 + half * 2 + 1] = o.astype(jnp.bfloat16)
            state[:NX, cols] = jnp.where(left, e, o).astype(jnp.bfloat16)
            state[NX:, cols] = pltpu.roll(jnp.where(left, o, e), QUARTER, 1).astype(jnp.bfloat16)


def pack_kernel(quarter_ref, source_ref, *refs):
    own_ref, chip_ref, core_ref, packed = refs
    row_at = lax.broadcasted_iota(jnp.int32, (NX, NX), 0)
    col_at = lax.broadcasted_iota(jnp.int32, (NX, NX), 1)
    flip = (row_at + col_at == NX - 1).astype(jnp.bfloat16)
    left = lax.broadcasted_iota(jnp.int32, (NX, LANES), 1) < QUARTER
    for f in range(GROUP):
        real = jnp.dot(flip, source_ref[f, 0], preferred_element_type=jnp.float32)
        imag = jnp.dot(flip, source_ref[f, 1], preferred_element_type=jnp.float32)
        for half in range(2):
            cols = slice(half * LANES, (half + 1) * LANES)
            a = real[:, cols]
            b = pltpu.roll(imag[:, cols], QUARTER, 1)
            packed[half * 2, f] = jnp.where(left, a, b).astype(jnp.bfloat16)
            packed[half * 2 + 1, f] = jnp.where(left, b, a).astype(jnp.bfloat16)
    mine = quarter_ref[0]
    own_ref[...] = packed[mine]
    chip_ref[0] = packed[mine ^ 2]
    chip_ref[1] = packed[mine ^ 3]
    core_ref[0] = packed[mine ^ 1]


def image_kernel(scale, quarter_ref, wave_ref, own_ref, core_ref, chip_ref, out_ref, wave, src, totals):
    sources = [own_ref, core_ref.at[0], chip_ref.at[0], core_ref.at[1]]
    edge = jnp.zeros((4 * GROUP, REACH, LANES), jnp.float32)
    for ref in (wave, src):
        ref[:, :REACH, :] = edge
        ref[:, REACH + NX :, :] = edge
    for k in range(4):
        group = (quarter_ref[0] ^ k) * GROUP
        for f in range(GROUP):
            wave[k * GROUP + f, REACH : REACH + NX, :] = wave_ref[f * 4 + k].astype(jnp.float32)
            src[group + f, REACH : REACH + NX, :] = sources[k][f].astype(jnp.float32)

    tall, deep = NX // 8, H // 8
    inside = range(1, tall + deep - 2)

    def rows_from(start, carry):
        sums = {}
        for i in range(4 * GROUP):
            waves = {j: wave[i, pl.ds(start + 8 * j, 8), :] for j in inside}
            sources = {j: src[i, pl.ds(7 - start + 8 * j, 8), :] for j in inside}
            for m in range(tall):
                for n in range(deep):
                    j, k = m + n, tall - 1 - m + n
                    if j in inside and k in inside:
                        term = waves[j] * sources[k]
                        sums[m, n] = sums[m, n] + term if i else term
        for m in range(tall):
            for n in range(deep):
                value = sums.get((m, n))
                totals[start + 8 * m, 8 * n : 8 * n + 8, :] = jnp.zeros((8, LANES), jnp.float32) if value is None else value
        return carry

    lax.fori_loop(0, 8, rows_from, 0)
    left = lax.broadcasted_iota(jnp.int32, (REACH, LANES), 1) < QUARTER

    def fold(x, carry):
        total = totals[x]
        total = (total + pltpu.roll(total, QUARTER, 1)) * scale
        out_ref[x] = jnp.where(left, total[:REACH], total[REACH:]).astype(jnp.bfloat16)
        return carry

    lax.fori_loop(0, NX, fold, 0, unroll=True)


def sum_kernel(part_ref, out_ref):
    many = part_ref.shape[0]
    left = lax.broadcasted_iota(jnp.int32, (REACH, LANES), 1) < QUARTER
    for half in range(2):
        totals = []
        for q in (2 * half, 2 * half + 1):
            total = jnp.zeros((REACH, LANES), jnp.float32)
            for i in range(q, many, 4):
                total = total + part_ref[i].astype(jnp.float32)
            totals.append(total)
        a, b = totals
        cols = slice(half * LANES, (half + 1) * LANES)
        out_ref[0, :REACH, 0, cols] = jnp.where(left, a, pltpu.roll(b, QUARTER, 1))
        out_ref[0, REACH:, 0, cols] = jnp.where(left, pltpu.roll(a, QUARTER, 1), b)


VMEM = pl.BlockSpec(memory_space=pltpu.VMEM)
SMEM = pl.BlockSpec(memory_space=pltpu.SMEM)
PARAMS = pltpu.CompilerParams(vmem_limit_bytes=24 << 20)


def cost(flops, moved):
    return pl.CostEstimate(flops=flops, bytes_accessed=moved, transcendentals=0)


def body(surface, regions, table, source):
    zh = lax.axis_index("zh")
    mine_x = lax.axis_index("x")
    core = lax.axis_index("core")
    blocks = lax.axis_size("zh")
    local = regions[0].astype(jnp.bfloat16)
    copies = jnp.broadcast_to(local[None], (GROUP, NX, NY))
    copies, local_source, table = lax.optimization_barrier((copies, source[0], table))
    all_regions = lax.all_to_all(copies, "x", 0, 0, tiled=True)
    quarter = (lax.axis_index("zp") * 2 + core).astype(jnp.int32).reshape(1)
    four = jax.ShapeDtypeStruct((GROUP, NX, LANES), jnp.bfloat16)
    pair = jax.ShapeDtypeStruct((2, GROUP, NX, LANES), jnp.bfloat16)
    one = jax.ShapeDtypeStruct((1, GROUP, NX, LANES), jnp.bfloat16)
    packed, to_chip, to_core = pl.pallas_call(
        pack_kernel,
        out_shape=(four, pair, one),
        in_specs=[SMEM, VMEM],
        out_specs=(VMEM,) * 3,
        scratch_shapes=[pltpu.VMEM((4, GROUP, NX, LANES), jnp.bfloat16)],
        compiler_params=PARAMS,
        cost_estimate=cost(20_000_000, 1_000_000),
        name="pack",
    )(quarter, local_source)
    from_chip = lax.ppermute(to_chip, "zp", [(0, 1), (1, 0)])
    from_core = lax.ppermute(
        jnp.concatenate([to_core, from_chip[1:]], axis=0), "core", [(0, 1), (1, 0)]
    )

    padded = jnp.pad(table.reshape(GROUP * R * 4, TAPS), ((0, 0), (0, LANES - TAPS)))
    bands = pl.pallas_call(
        bands_kernel,
        out_shape=(
            jax.ShapeDtypeStruct((R * 2 * NX, LANES), jnp.bfloat16),
            jax.ShapeDtypeStruct((2 * LANES, R * LANES), jnp.bfloat16),
            jax.ShapeDtypeStruct((2 * LANES, R * LANES), jnp.bfloat16),
        ),
        in_specs=[SMEM, VMEM],
        out_specs=(VMEM,) * 3,
        compiler_params=PARAMS,
        cost_estimate=cost(10_000_000, 1_000_000),
        name="bands",
    )(mine_x.astype(jnp.int32).reshape(1), padded)

    entering = lax.dynamic_index_in_dim(surface, mine_x, 0, keepdims=False).reshape(2 * NX, NY)
    before = ()
    for block in range(blocks):
        wave_shape = jax.ShapeDtypeStruct((GROUP * 4, NX, LANES), jnp.bfloat16)
        state_shape = (2 * NX, NY)
        last = block + 1 == blocks
        waves, *leaving = pl.pallas_call(
            functools.partial(chain_kernel, block == 0),
            out_shape=(wave_shape,) + (() if last else (jax.ShapeDtypeStruct(state_shape, jnp.bfloat16),)),
            in_specs=[SMEM] + [VMEM] * (5 + len(before)),
            out_specs=(VMEM,) * (1 if last else 2),
            scratch_shapes=[pltpu.VMEM(state_shape, jnp.bfloat16)] if last else [],
            compiler_params=PARAMS,
            cost_estimate=cost(300_000_000, 4_000_000),
            name="chain",
        )((zh == block).astype(jnp.int32).reshape(1), *bands, entering, all_regions, *before)
        before = (waves,)
        if not last:
            entering = lax.ppermute(leaving[0], "zh", [(block, block + 1)])

    waves, from_core = lax.optimization_barrier((waves, from_core))
    waves = lax.all_to_all(waves, ("x",) + QUAD, 0, 0, tiled=True)

    scale = 1.0 / math.sqrt(surface.shape[0] * lax.axis_size(FREQ))
    partial_image = pl.pallas_call(
        lambda *refs: image_kernel(scale, *refs),
        out_shape=jax.ShapeDtypeStruct((NX, REACH, LANES), jnp.bfloat16),
        in_specs=[SMEM] + [VMEM] * 4,
        out_specs=VMEM,
        scratch_shapes=[pltpu.VMEM((4 * GROUP, NX + H, LANES), jnp.float32)] * 2
        + [pltpu.VMEM((NX, H, LANES), jnp.float32)],
        compiler_params=PARAMS,
        cost_estimate=cost(10_000_000, 2_000_000),
        name="image",
    )(quarter, waves, packed, from_core, from_chip)

    parts = lax.all_to_all(partial_image, FREQ, 0, 0, tiled=True)

    return pl.pallas_call(
        sum_kernel,
        out_shape=jax.ShapeDtypeStruct((1, H, 1, NY), jnp.float32),
        in_specs=[VMEM],
        out_specs=VMEM,
        compiler_params=PARAMS,
        name="total",
    )(parts)


def solution(mesh):
    wide = Mesh(np.asarray(mesh.devices).reshape(3, 4, 8, 2, 2, 2), AXES)
    in_specs = (
        P(FREQ, None, None, None),
        P(DEPTH, None, None),
        P(FREQ, None, None, None, None),
        P(DEPTH, FREQ, None, None, None),
    )
    out_specs = P(DEPTH, None, FREQ, None)
    return jax.shard_map(body, mesh=wide, in_specs=in_specs, out_specs=out_specs, check_vma=False)
```

```python
import functools
import math

import jax
import jax.numpy as jnp
import numpy as np
from jax import lax
from jax.experimental import pallas as pl
from jax.experimental.pallas import tpu as pltpu
from jax.sharding import Mesh
from jax.sharding import PartitionSpec as P

H = 32
REACH = H // 2
NX = 64
NY = 256
LANES = 128
QUARTER = 64
R = 4
TAPS = 25
MID = TAPS // 2
GROUP = 4

AXES = ("zh", "x", "yq", "yp", "zl", "core")
DEPTH = ("zh", "x")
FREQ = ("yq", "yp", "zl", "core")
QUAD = ("yp", "core")


def onehot(shape, fit, value=1.0):
    row_at = lax.broadcasted_iota(jnp.int32, shape, 0)
    col_at = lax.broadcasted_iota(jnp.int32, shape, 1)
    return jnp.where(fit(row_at, col_at), value, 0.0).astype(jnp.bfloat16)


def exact(a, b):
    return jnp.dot(a, b, preferred_element_type=jnp.float32)


def tap_rows(taps):
    many = R * 2

    def row(pass_at, part):
        return lambda i, j: j == (i >> 1) * 4 + pass_at * 2 + part(i & 1)

    def lanes(shift, sign=1):
        return onehot((LANES, LANES), lambda k, n: k == ((sign * n + shift) & (LANES - 1)))

    def chosen(fit):
        return exact(fit, taps).astype(jnp.bfloat16)

    shape = (many, 2 * many)
    straight = chosen(onehot(shape, row(0, lambda p: p)))
    row_at = lax.broadcasted_iota(jnp.int32, (many, LANES), 0)
    crossed = exact(chosen(onehot(shape, row(0, lambda p: 1 - p))), lanes(-(QUARTER - MID)))
    crossed = jnp.where((row_at & 1) == 0, -crossed, crossed)
    rows_first = exact(straight, lanes(MID)) + crossed
    rows_second = exact(chosen(onehot(shape, row(1, lambda p: p))), lanes(MID, -1))
    return rows_first, rows_second


def fan(row, height, shift):
    wide = jnp.broadcast_to(row, (height, row.shape[-1]))
    return pltpu.roll(wide, shift, 1, stride=1, stride_axis=0)


def bands_kernel(index_ref, table_ref, band_first, band_even, band_odd):
    taps = table_ref[pl.ds(pl.multiple_of(index_ref[0] * 16, 16), 16), :]
    rows_first, rows_second = tap_rows(taps)
    row_at = lax.broadcasted_iota(jnp.int32, (NX, LANES), 0)
    lane_at = lax.broadcasted_iota(jnp.int32, (NX, LANES), 1)
    near = jnp.abs((lane_at & (NX - 1)) - row_at) <= MID
    for block in range(R * 2):
        band = fan(rows_first[block : block + 1, :], NX, 0)
        band_first[block * NX : (block + 1) * NX, :] = jnp.where(near, band, 0.0).astype(jnp.bfloat16)

    left = lax.broadcasted_iota(jnp.int32, (LANES, LANES), 1) < QUARTER
    for region in range(R):
        tap_real = rows_second[2 * region : 2 * region + 1, :]
        tap_imag = rows_second[2 * region + 1 : 2 * region + 2, :]
        cols = slice(region * LANES, (region + 1) * LANES)
        for part, (to_real, to_imag) in enumerate(((tap_real, tap_imag), (-tap_imag, tap_real))):
            rows = slice(part * LANES, (part + 1) * LANES)
            real_band = fan(to_real, LANES, 0)
            imag_band = fan(to_imag, LANES, QUARTER)
            band_even[rows, cols] = jnp.where(left, real_band, imag_band).astype(jnp.bfloat16)
            band_odd[rows, cols] = jnp.where(left, imag_band, real_band).astype(jnp.bfloat16)


def pick(masks, values):
    out = values[R - 1]
    for region in range(R - 2, -1, -1):
        out = jnp.where(masks[region], values[region], out)
    return out


def chain_kernel(first, turn_ref, band_first, band_even, band_odd, entering_ref, regions_ref, *refs):
    out_ref, state = refs[-2:]
    active = turn_ref[0] == 1

    @pl.when(active)
    def _():
        run_steps(band_first, band_even, band_odd, entering_ref, regions_ref, out_ref, state)

    @pl.when(jnp.logical_not(active))
    def _():
        out_ref[...] = jnp.zeros_like(out_ref) if first else refs[0][...]
        state[...] = jnp.zeros_like(state)


def run_steps(band_first, band_even, band_odd, entering_ref, regions_ref, out_ref, state):
    state[...] = entering_ref[...]
    lane = lax.broadcasted_iota(jnp.int32, (NX, LANES), 1)
    left = lane < QUARTER
    low = lane < 96
    high = lane >= 32

    def split(values):
        return [values == float(r) for r in range(R - 1)]

    for slot in range(GROUP):
        region = regions_ref[slot].astype(jnp.float32)
        halves = [region[:, :LANES], region[:, LANES:]]
        turned = [pltpu.roll(half, QUARTER, 1) for half in halves]
        full = split(region)
        even_mask = split(jnp.concatenate([jnp.where(left, a, b) for a, b in zip(halves, turned)], axis=0))
        odd_mask = split(jnp.concatenate([jnp.where(left, b, a) for a, b in zip(halves, turned)], axis=0))

        field = [
            jnp.dot(band_first[rows], state[...], preferred_element_type=jnp.float32)
            for rows in (slice(0, 4 * NX), slice(4 * NX, 8 * NX))
        ]
        field = jnp.concatenate(field, axis=0)
        even_in, odd_in = [], []
        for part in range(2):
            values = [field[(r * 2 + part) * NX : (r * 2 + part + 1) * NX] for r in range(R)]
            between = pick(full, values)
            a, b = between[:, :LANES], between[:, LANES:]
            even_in.append(jnp.concatenate([jnp.where(low, a, 0.0), jnp.where(low, b, a)], axis=0).astype(jnp.bfloat16))
            odd_in.append(jnp.concatenate([jnp.where(high, a, b), jnp.where(high, b, 0.0)], axis=0).astype(jnp.bfloat16))
        wide = jnp.dot(jnp.concatenate(even_in, axis=1), band_even[...], preferred_element_type=jnp.float32)
        even = pick(even_mask, [wide[:, r * LANES : (r + 1) * LANES] for r in range(R)])
        wide = jnp.dot(jnp.concatenate(odd_in, axis=1), band_odd[...], preferred_element_type=jnp.float32)
        odd = pick(odd_mask, [wide[:, r * LANES : (r + 1) * LANES] for r in range(R)])
        for half in range(2):
            rows = slice(half * NX, (half + 1) * NX)
            cols = slice(half * LANES, (half + 1) * LANES)
            e, o = even[rows], odd[rows]
            out_ref[slot * 4 + half * 2] = e.astype(jnp.bfloat16)
            out_ref[slot * 4 + half * 2 + 1] = o.astype(jnp.bfloat16)
            state[:NX, cols] = jnp.where(left, e, o).astype(jnp.bfloat16)
            state[NX:, cols] = pltpu.roll(jnp.where(left, o, e), QUARTER, 1).astype(jnp.bfloat16)


def pack_kernel(quarter_ref, source_ref, *refs):
    own_ref, core_ref, chip_ref, packed = refs
    row_at = lax.broadcasted_iota(jnp.int32, (NX, NX), 0)
    col_at = lax.broadcasted_iota(jnp.int32, (NX, NX), 1)
    flip = (row_at + col_at == NX - 1).astype(jnp.bfloat16)
    left = lax.broadcasted_iota(jnp.int32, (NX, LANES), 1) < QUARTER
    for f in range(GROUP):
        real = jnp.dot(flip, source_ref[f, 0], preferred_element_type=jnp.float32)
        imag = jnp.dot(flip, source_ref[f, 1], preferred_element_type=jnp.float32)
        for half in range(2):
            cols = slice(half * LANES, (half + 1) * LANES)
            a = real[:, cols]
            b = pltpu.roll(imag[:, cols], QUARTER, 1)
            packed[half * 2, f] = jnp.where(left, a, b).astype(jnp.bfloat16)
            packed[half * 2 + 1, f] = jnp.where(left, b, a).astype(jnp.bfloat16)
    mine = quarter_ref[0]
    own_ref[...] = packed[mine]
    core_ref[0] = packed[mine ^ 1]
    core_ref[1] = packed[mine ^ 3]
    chip_ref[0] = packed[mine ^ 2]


def image_kernel(scale, quarter_ref, wave_ref, own_ref, core_ref, chip_ref, out_ref, wave, src, totals):
    sources = [own_ref, core_ref.at[0], chip_ref.at[0], chip_ref.at[1]]
    edge = jnp.zeros((4 * GROUP, REACH, LANES), jnp.float32)
    for ref in (wave, src):
        ref[:, :REACH, :] = edge
        ref[:, REACH + NX :, :] = edge
    for k in range(4):
        group = (quarter_ref[0] ^ k) * GROUP
        for f in range(GROUP):
            wave[k * GROUP + f, REACH : REACH + NX, :] = wave_ref[f * 4 + k].astype(jnp.float32)
            src[group + f, REACH : REACH + NX, :] = sources[k][f].astype(jnp.float32)

    tall, deep = NX // 8, H // 8
    inside = range(1, tall + deep - 2)

    def rows_from(start, carry):
        sums = {}
        for i in range(4 * GROUP):
            waves = {j: wave[i, pl.ds(start + 8 * j, 8), :] for j in inside}
            sources = {j: src[i, pl.ds(7 - start + 8 * j, 8), :] for j in inside}
            for m in range(tall):
                for n in range(deep):
                    j, k = m + n, tall - 1 - m + n
                    if j in inside and k in inside:
                        term = waves[j] * sources[k]
                        sums[m, n] = sums[m, n] + term if i else term
        for m in range(tall):
            for n in range(deep):
                value = sums.get((m, n))
                totals[start + 8 * m, 8 * n : 8 * n + 8, :] = jnp.zeros((8, LANES), jnp.float32) if value is None else value
        return carry

    lax.fori_loop(0, 8, rows_from, 0)
    left = lax.broadcasted_iota(jnp.int32, (REACH, LANES), 1) < QUARTER

    def fold(x, carry):
        total = totals[x]
        total = (total + pltpu.roll(total, QUARTER, 1)) * scale
        out_ref[x] = jnp.where(left, total[:REACH], total[REACH:]).astype(jnp.bfloat16)
        return carry

    lax.fori_loop(0, NX, fold, 0, unroll=True)


def sum_kernel(part_ref, out_ref):
    many, line = part_ref.shape[0], 8
    left = lax.broadcasted_iota(jnp.int32, (REACH, LANES), 1) < QUARTER
    for half in range(2):
        totals = []
        for q in (2 * half, 2 * half + 1):
            pair, core = divmod(q, 2)
            total = jnp.zeros((REACH, LANES), jnp.float32)
            for start in range(pair * line, many, 2 * line):
                for i in range(start + core, start + line, 2):
                    total = total + part_ref[i].astype(jnp.float32)
            totals.append(total)
        a, b = totals
        cols = slice(half * LANES, (half + 1) * LANES)
        out_ref[0, :REACH, 0, cols] = jnp.where(left, a, pltpu.roll(b, QUARTER, 1))
        out_ref[0, REACH:, 0, cols] = jnp.where(left, pltpu.roll(a, QUARTER, 1), b)


VMEM = pl.BlockSpec(memory_space=pltpu.VMEM)
SMEM = pl.BlockSpec(memory_space=pltpu.SMEM)
PARAMS = pltpu.CompilerParams(vmem_limit_bytes=24 << 20)


def cost(flops, moved):
    return pl.CostEstimate(flops=flops, bytes_accessed=moved, transcendentals=0)


def body(surface, regions, table, source):
    zh = lax.axis_index("zh")
    mine_x = lax.axis_index("x")
    core = lax.axis_index("core")
    blocks = lax.axis_size("zh")
    slot = lax.broadcasted_iota(jnp.int32, (GROUP, NX, NY), 0)
    copies = jnp.where(slot < GROUP + mine_x, regions, 0).astype(jnp.bfloat16)
    copies, local_source, table = lax.optimization_barrier((copies, source[0], table))
    all_regions = lax.all_to_all(copies, "x", 0, 0, tiled=True)
    quarter = (lax.axis_index("yp") * 2 + core).astype(jnp.int32).reshape(1)
    four = jax.ShapeDtypeStruct((GROUP, NX, LANES), jnp.bfloat16)
    pair = jax.ShapeDtypeStruct((2, GROUP, NX, LANES), jnp.bfloat16)
    one = jax.ShapeDtypeStruct((1, GROUP, NX, LANES), jnp.bfloat16)
    packed, to_core, to_chip = pl.pallas_call(
        pack_kernel,
        out_shape=(four, pair, one),
        in_specs=[SMEM, VMEM],
        out_specs=(VMEM,) * 3,
        scratch_shapes=[pltpu.VMEM((4, GROUP, NX, LANES), jnp.bfloat16)],
        compiler_params=PARAMS,
        cost_estimate=cost(20_000_000, 1_000_000),
        name="pack",
    )(quarter, local_source)
    from_core = lax.ppermute(to_core, "core", [(0, 1), (1, 0)])
    from_chip = lax.ppermute(
        jnp.concatenate([to_chip, from_core[1:]], axis=0), "yp", [(0, 1), (1, 0)]
    )

    padded = jnp.pad(table.reshape(GROUP * R * 4, TAPS), ((0, 0), (0, LANES - TAPS)))
    bands = pl.pallas_call(
        bands_kernel,
        out_shape=(
            jax.ShapeDtypeStruct((R * 2 * NX, LANES), jnp.bfloat16),
            jax.ShapeDtypeStruct((2 * LANES, R * LANES), jnp.bfloat16),
            jax.ShapeDtypeStruct((2 * LANES, R * LANES), jnp.bfloat16),
        ),
        in_specs=[SMEM, VMEM],
        out_specs=(VMEM,) * 3,
        compiler_params=PARAMS,
        cost_estimate=cost(10_000_000, 1_000_000),
        name="bands",
    )(mine_x.astype(jnp.int32).reshape(1), padded)

    entering = lax.dynamic_index_in_dim(surface, mine_x, 0, keepdims=False).reshape(2 * NX, NY)
    before = ()
    for block in range(blocks):
        wave_shape = jax.ShapeDtypeStruct((GROUP * 4, NX, LANES), jnp.bfloat16)
        state_shape = (2 * NX, NY)
        last = block + 1 == blocks
        waves, *leaving = pl.pallas_call(
            functools.partial(chain_kernel, block == 0),
            out_shape=(wave_shape,) + (() if last else (jax.ShapeDtypeStruct(state_shape, jnp.bfloat16),)),
            in_specs=[SMEM] + [VMEM] * (5 + len(before)),
            out_specs=(VMEM,) * (1 if last else 2),
            scratch_shapes=[pltpu.VMEM(state_shape, jnp.bfloat16)] if last else [],
            compiler_params=PARAMS,
            cost_estimate=cost(300_000_000, 4_000_000),
            name="chain",
        )((zh == block).astype(jnp.int32).reshape(1), *bands, entering, all_regions, *before)
        before = (waves,)
        if not last:
            entering = lax.ppermute(leaving[0], "zh", [(block, block + 1)])

    waves, from_chip = lax.optimization_barrier((waves, from_chip))
    waves = lax.all_to_all(waves, ("x",) + QUAD, 0, 0, tiled=True)

    scale = 1.0 / math.sqrt(surface.shape[0] * lax.axis_size(FREQ))
    partial_image = pl.pallas_call(
        lambda *refs: image_kernel(scale, *refs),
        out_shape=jax.ShapeDtypeStruct((NX, REACH, LANES), jnp.bfloat16),
        in_specs=[SMEM] + [VMEM] * 4,
        out_specs=VMEM,
        scratch_shapes=[pltpu.VMEM((4 * GROUP, NX + H, LANES), jnp.float32)] * 2
        + [pltpu.VMEM((NX, H, LANES), jnp.float32)],
        compiler_params=PARAMS,
        cost_estimate=cost(10_000_000, 2_000_000),
        name="image",
    )(quarter, waves, packed, from_core, from_chip)

    parts = lax.all_to_all(partial_image, FREQ, 0, 0, tiled=True)

    return pl.pallas_call(
        sum_kernel,
        out_shape=jax.ShapeDtypeStruct((1, H, 1, NY), jnp.float32),
        in_specs=[VMEM],
        out_specs=VMEM,
        compiler_params=PARAMS,
        name="total",
    )(parts)


def solution(mesh):
    wide = Mesh(np.asarray(mesh.devices).reshape(3, 4, 4, 2, 4, 2), AXES)
    in_specs = (
        P(FREQ, None, None, None),
        P(DEPTH, None, None),
        P(FREQ, None, None, None, None),
        P(DEPTH, FREQ, None, None, None),
    )
    out_specs = P(DEPTH, None, FREQ, None)
    return jax.shard_map(body, mesh=wide, in_specs=in_specs, out_specs=out_specs, check_vma=False)
```
